512 devices in a mesh: space: 32 (over z_hi, y, core), angle: 16 (over z_lo, x).
Axes of the slice: x: 4, y: 8, z: 8 (z_hi: 2, z_lo: 4; z = z_hi * 4 + z_lo), core: 2. Of those that a mesh axis runs over, the one named last changes fastest.
Arguments:
- phase_delay: float32 [2, 1024, 2048], P(None, 'space'), may hold values from -6 to 6
- measured: float32 [16, 2, 1024, 2048], P('angle', None, 'space'), may hold values from -6 to 6
- tilts: float32 [16, 2], P('angle'), may hold values from -0.4 to 0.4
- fresnel_taps: float32 [2, 2, 33], replicated, may hold values from -0.75 to 0.75
Outputs:
- gradient: float32 [2, 1024, 2048], P(None, 'space', 'angle')
The draws below stay inside these ranges and needn't reach their ends.
All inputs are finite; a program needn't handle non-finite values.
Results may differ from the reference program's by a relative error of at most 0.0003.
Values sent between devices are 32-bit elements; how exact they have to be, the bound alone decides.
No kernel may reach another device: no remote copies, remote signals or barrier semaphores. Data moves between devices by JAX's collectives and lax.ppermute only.
A program may use at most 64 MiB of HBM per device.

```python
import jax
import jax.numpy as jnp
from jax import lax

NY = 2048
TAPS = 33
SLICES = 2
NX = 1024
ANGLES = 16


def steps_of(stream_key, extent, shards, least, largest):
    level = 1.0
    for axis_at, shards_of in shards:
        steps = jax.random.uniform(jax.random.fold_in(jax.random.fold_in(stream_key, 6), axis_at), (shards_of,), jnp.float32, least / len(shards), largest / len(shards))
        level = level * jnp.repeat(jnp.exp(steps), extent[axis_at] // shards_of).reshape((-1,) + (1,) * (len(extent) - 1 - axis_at))
    return level


def noise(stream_key, shape, width, limit, split=(), kind=jnp.bfloat16):
    values = width * jax.random.normal(stream_key, shape, jnp.float32)
    if split:
        values = values * steps_of(stream_key, shape, split, -0.22, 0.18)
    return jnp.clip(values, -limit, limit).astype(kind)


def setup_inputs(seed: int = 0) -> dict:
    keys = jax.random.split(jax.random.key(seed), 5)
    return {
        "phase_delay": noise(keys[0], (SLICES, NX, NY), 1.0, 6.0, ((1, 32),), jnp.float32),
        "measured": noise(keys[1], (ANGLES, 2, NX, NY), 1.0, 6.0, ((0, 16), (2, 32)), jnp.float32),
        "tilts": jnp.clip(jax.random.uniform(keys[2], (ANGLES, 2), jnp.float32, -0.4, 0.4) * steps_of(keys[2], (ANGLES, 2), ((0, 16),), -0.4, 0.0), -0.4, 0.4),
        "fresnel_taps": noise(keys[3], (2, 2, TAPS), (2 * TAPS) ** -0.5, 0.75, (), jnp.float32),
    }


def adjoint_kernel(kernel):
    return jnp.stack([kernel[0, ::-1], -kernel[1, ::-1]])


def along_rows(wave_field, kernel):
    reach = (kernel.shape[1] - 1) // 2
    length = wave_field.shape[1]
    padded = jnp.pad(wave_field, ((0, 0), (reach, reach), (0, 0)))
    real_part = jnp.zeros(wave_field.shape[1:], jnp.float32)
    imag_part = jnp.zeros(wave_field.shape[1:], jnp.float32)
    for offset in range(-reach, reach + 1):
        window = padded[:, reach - offset:reach - offset + length, :]
        tap_real = kernel[0, offset + reach]
        tap_imag = kernel[1, offset + reach]
        real_part = real_part + tap_real * window[0] - tap_imag * window[1]
        imag_part = imag_part + tap_real * window[1] + tap_imag * window[0]
    return jnp.stack([real_part, imag_part])


def along_columns(wave_field, kernel):
    reach = (kernel.shape[1] - 1) // 2
    length = wave_field.shape[2]
    padded = jnp.pad(wave_field, ((0, 0), (0, 0), (reach, reach)))
    real_part = jnp.zeros(wave_field.shape[1:], jnp.float32)
    imag_part = jnp.zeros(wave_field.shape[1:], jnp.float32)
    for offset in range(-reach, reach + 1):
        window = padded[:, :, reach - offset:reach - offset + length]
        tap_real = kernel[0, offset + reach]
        tap_imag = kernel[1, offset + reach]
        real_part = real_part + tap_real * window[0] - tap_imag * window[1]
        imag_part = imag_part + tap_real * window[1] + tap_imag * window[0]
    return jnp.stack([real_part, imag_part])


def transmit(wave_field, cosine, sine):
    return jnp.stack([cosine * wave_field[0] - sine * wave_field[1], cosine * wave_field[1] + sine * wave_field[0]])


def release(wave_field, cosine, sine):
    return jnp.stack([cosine * wave_field[0] + sine * wave_field[1], cosine * wave_field[1] - sine * wave_field[0]])


def reference(phase_delay, measured, tilts, fresnel_taps):
    row_taps = fresnel_taps[0]
    column_taps = fresnel_taps[1]
    row_back = adjoint_kernel(row_taps)
    column_back = adjoint_kernel(column_taps)
    cosines = jnp.cos(phase_delay)
    sines = jnp.sin(phase_delay)
    positions = jnp.arange(NX, dtype=jnp.float32)[:, None]
    columns = jnp.arange(NY, dtype=jnp.float32)[None, :]

    def one_angle(total, inputs):
        target, tilt = inputs
        ramp = tilt[0] * positions + tilt[1] * columns
        wave_field = jnp.stack([jnp.cos(ramp), jnp.sin(ramp)])
        stored = []
        for layer in range(SLICES):
            transmitted = transmit(wave_field, cosines[layer], sines[layer])
            stored.append(transmitted)
            wave_field = along_columns(along_rows(transmitted, row_taps), column_taps)
        backward = wave_field - target
        terms = [None] * SLICES
        for layer in reversed(range(SLICES)):
            sensitivity = along_rows(along_columns(backward, column_back), row_back)
            transmitted = stored[layer]
            terms[layer] = transmitted[0] * sensitivity[1] - transmitted[1] * sensitivity[0]
            backward = release(sensitivity, cosines[layer], sines[layer])
        return total + jnp.stack(terms), None

    total, unused = lax.scan(one_angle, jnp.zeros((SLICES, NX, NY), jnp.float32), (measured, tilts))
    return total
```

```python
import jax
import jax.numpy as jnp
from jax import lax
from jax.sharding import PartitionSpec as P

tile_width = 128
highest = lax.Precision.HIGHEST


def padded_2(block, sides, width):
    for axis, dim in sides:
        count = lax.axis_size(axis)
        forward = [(i, i + 1) for i in range(count - 1)]
        backward = [(target, source) for source, target in forward]
        low = lax.ppermute(
            lax.slice_in_dim(block, block.shape[dim] - width, None, axis=dim), axis, forward
        )
        high = lax.ppermute(lax.slice_in_dim(block, 0, width, axis=dim), axis, backward)
        block = jnp.concatenate([low, block, high], axis=dim)
    return block


def adjoint_kernel(kernel):
    return jnp.stack([kernel[0, ::-1], -kernel[1, ::-1]])


def tap_table(kernel, offsets):
    tap_count = kernel.shape[1]
    onehot = (offsets[None] == jnp.arange(tap_count, dtype=jnp.int32)[:, None, None]).astype(
        jnp.float32
    )
    return jnp.einsum("ck,kij->cij", kernel, onehot, precision=highest)


def band_blocks(kernel):
    reach = (kernel.shape[1] - 1) // 2
    source = lax.broadcasted_iota(jnp.int32, (tile_width, tile_width), 0)
    target = lax.broadcasted_iota(jnp.int32, (tile_width, tile_width), 1)
    stacked = []
    for block_shift in (-1, 0, 1):
        table = tap_table(kernel, target - source - tile_width * block_shift + reach)
        real_row = jnp.stack([table[0], table[1]], axis=1)
        imag_row = jnp.stack([-table[1], table[0]], axis=1)
        stacked.append(jnp.stack([real_row, imag_row]))
    return jnp.stack(stacked)


def row_matrix(kernel, out_rows):
    reach = (kernel.shape[1] - 1) // 2
    out_index = lax.broadcasted_iota(jnp.int32, (out_rows, out_rows + 2 * reach), 0)
    in_index = lax.broadcasted_iota(jnp.int32, (out_rows, out_rows + 2 * reach), 1)
    return tap_table(kernel, out_index + 2 * reach - in_index)


def complex_rows(padded, matrix):
    real_in = padded[..., 0, :, :]
    imag_in = padded[..., 1, :, :]
    real_out = jnp.einsum("xj,...jy->...xy", matrix[0], real_in, precision=highest) - jnp.einsum(
        "xj,...jy->...xy", matrix[1], imag_in, precision=highest
    )
    imag_out = jnp.einsum("xj,...jy->...xy", matrix[0], imag_in, precision=highest) + jnp.einsum(
        "xj,...jy->...xy", matrix[1], real_in, precision=highest
    )
    return jnp.stack([real_out, imag_out], axis=-3)


def complex_columns(wave_field, blocks):
    shape = wave_field.shape
    tile_count = shape[-1] // tile_width
    tiles = wave_field.reshape(shape[:-1] + (tile_count, tile_width))
    padding = [(0, 0)] * (tiles.ndim - 2) + [(1, 1), (0, 0)]
    tiles = jnp.pad(tiles, padding)
    total = None
    for position, block_shift in enumerate((-1, 0, 1)):
        source_tiles = tiles[..., 1 + block_shift : 1 + block_shift + tile_count, :]
        term = jnp.einsum(
            "...cxtk,ckdj->...dxtj", source_tiles, blocks[position], precision=highest
        )
        total = term if total is None else total + term
    return total.reshape(shape)


def transmit(wave_field, cosine, sine):
    real_in = wave_field[:, 0]
    imag_in = wave_field[:, 1]
    return jnp.stack([cosine * real_in - sine * imag_in, cosine * imag_in + sine * real_in], axis=1)


def release(wave_field, cosine, sine):
    real_in = wave_field[:, 0]
    imag_in = wave_field[:, 1]
    return jnp.stack([cosine * real_in + sine * imag_in, cosine * imag_in - sine * real_in], axis=1)


def incident(tilts, first_row, length, column_count):
    positions = (first_row + jnp.arange(length, dtype=jnp.int32)).astype(jnp.float32)
    columns_float = jnp.arange(column_count, dtype=jnp.float32)
    ramp = (
        tilts[:, 0, None, None] * positions[None, :, None]
        + tilts[:, 1, None, None] * columns_float[None, None, :]
    )
    return jnp.stack([jnp.cos(ramp), jnp.sin(ramp)], axis=1)


def body(phase_delay, measured, tilts, fresnel_taps):
    slice_count, strip_rows, column_count = phase_delay.shape
    reach = (fresnel_taps.shape[2] - 1) // 2
    first_row = lax.axis_index("space") * strip_rows
    column_blocks = band_blocks(fresnel_taps[1])
    column_back = band_blocks(adjoint_kernel(fresnel_taps[1]))
    cosines = jnp.cos(phase_delay)
    sines = jnp.sin(phase_delay)
    stored = []
    wave_field = incident(tilts, first_row, strip_rows, column_count)
    row_forward = row_matrix(fresnel_taps[0], strip_rows)
    for layer in range(slice_count):
        transmitted = transmit(wave_field, cosines[layer], sines[layer])
        stored.append(transmitted)
        padded = padded_2(transmitted, (("space", 2),), reach)
        wave_field = complex_columns(complex_rows(padded, row_forward), column_blocks)
    row_backward = row_matrix(adjoint_kernel(fresnel_taps[0]), strip_rows)
    backward = wave_field - measured
    terms = [None] * slice_count
    for layer in reversed(range(slice_count)):
        spread_field = complex_columns(backward, column_back)
        padded = padded_2(spread_field, (("space", 2),), reach)
        sensitivity = complex_rows(padded, row_backward)
        transmitted = stored[layer]
        terms[layer] = jnp.sum(
            transmitted[:, 0] * sensitivity[:, 1] - transmitted[:, 1] * sensitivity[:, 0], axis=0
        )
        if layer > 0:
            backward = release(sensitivity, cosines[layer], sines[layer])
    parts = lax.axis_size("angle")
    blocks = jnp.stack(terms).reshape(slice_count, strip_rows, parts, column_count // parts)
    blocks = lax.all_to_all(blocks.transpose(2, 0, 1, 3), "angle", 0, 0)
    return jnp.sum(blocks, axis=0)


def solution(mesh):
    return jax.shard_map(
        body,
        mesh=mesh,
        in_specs=(P(None, "space", None), P("angle", None, "space", None), P("angle", None), P()),
        out_specs=P(None, "space", "angle"),
        check_vma=False,
    )
```

```python
import functools

import jax
import jax.numpy as jnp
from jax import lax
from jax.experimental import pallas as pl
from jax.experimental.pallas import tpu as pltpu
from jax.sharding import PartitionSpec as P

TILE = 128
REACH = 16
TAPS = 2 * REACH + 1
ROWS = 32
WIDE = ROWS + 2 * REACH
WIDEST = ROWS + 4 * REACH
F32 = jnp.float32
BF16 = jnp.bfloat16
VMEM_LIMIT = 48 * 1024 * 1024


def split(x):
    high = x.astype(BF16)
    return high, (x - high.astype(F32)).astype(BF16)


def matmul(a, b):
    return jnp.dot(a, b, preferred_element_type=F32)


def tap_matrices(taps_ref, rows1_ref, rows2_ref, band_ref):
    lane = lax.broadcasted_iota(jnp.int32, (8, 256), 1)

    def laid(direction, part, start, step):
        out = jnp.zeros((8, 256), F32)
        for tap in range(TAPS):
            out = jnp.where(lane == start + step * tap, taps_ref[direction, part, tap], out)
        return out

    def toeplitz(vector, rows):
        full = jnp.broadcast_to(vector[:1], (rows, 256))
        return pltpu.roll(full, 0, 1, stride=1, stride_axis=0)

    def put(ref, index, value):
        high, low = split(value)
        ref[index, 0] = high
        ref[index, 1] = low

    for index, sign in ((0, 1.0), (1, -1.0)):
        for ref, out_rows, in_rows in ((rows1_ref, WIDE, WIDEST), (rows2_ref, ROWS, WIDE)):
            halves = []
            for offset in (0, in_rows):
                start, step = (offset + TAPS - 1, -1) if index == 0 else (offset, 1)
                halves.append((laid(0, 0, start, step), laid(0, 1, start, step) * sign))
            top = toeplitz(halves[0][0] - halves[1][1], out_rows)
            bottom = toeplitz(halves[0][1] + halves[1][0], out_rows)
            put(ref, index, jnp.concatenate([top, bottom], axis=0)[:, : 2 * in_rows])
        first = 256 - TILE // 2 - REACH
        start, step = (first, 1) if index == 0 else (first + TAPS - 1, -1)
        real = toeplitz(laid(1, 0, start, step), 256)[:, :TILE]
        imag = toeplitz(laid(1, 1, start, step) * sign, 256)[:, :TILE]
        put(
            band_ref,
            index,
            jnp.concatenate(
                [
                    jnp.concatenate([real, imag], axis=1),
                    jnp.concatenate([-imag, real], axis=1),
                ],
                axis=0,
            ),
        )


def row_pass(real, imag, matrix_ref, index):
    high, low = split(jnp.concatenate([real, imag], axis=0))
    matrix_high = matrix_ref[index, 0]
    both = jnp.concatenate([matrix_high, matrix_ref[index, 1]], axis=0)
    count = matrix_high.shape[0]
    product = matmul(both, high)
    total = product[:count] + (product[count:] + matmul(matrix_high, low))
    return total[: count // 2], total[count // 2 :]


def column_pass(real, imag, band_ref, index, tiles, first):
    rows = real.shape[0]
    have = real.shape[1] // TILE
    blank = jnp.zeros((rows, TILE), BF16)
    parts = [split(real), split(imag)]

    def stacked(level):
        def tile(part, j):
            if 0 <= j < have:
                return parts[part][level][:, j * TILE : (j + 1) * TILE]
            return blank

        return jnp.concatenate(
            [
                jnp.concatenate(
                    [tile(0, first + j), tile(0, first + j + 1), tile(1, first + j), tile(1, first + j + 1)],
                    axis=1,
                )
                for j in range(tiles)
            ],
            axis=0,
        )

    high, low = stacked(0), stacked(1)
    band_high = band_ref[index, 0]
    out = matmul(high, band_high) + (matmul(low, band_high) + matmul(high, band_ref[index, 1]))
    pieces = [out[j * rows : (j + 1) * rows] for j in range(tiles)]
    return (
        jnp.concatenate([p[:, :TILE] for p in pieces], axis=1),
        jnp.concatenate([p[:, TILE:] for p in pieces], axis=1),
    )


def neighbours(even, across, beside):
    return jnp.where(even, across, beside), jnp.where(even, beside, across)


def forward(
    where_ref, tilts_ref, own_ref, across_ref, beside_ref, measured_ref, rows1_ref, rows2_ref, band_ref,
    spread_ref, wave0_ref, wave1_ref, turn1_ref, *, total_rows, total_columns,
):
    first_row = where_ref[0]
    even = where_ref[1] == 0
    below, above = neighbours(even, across_ref[...], beside_ref[...])
    width = own_ref.shape[2]
    tiles = width // TILE

    def row_numbers(count, start):
        return first_row - start + lax.broadcasted_iota(jnp.int32, (count, 1), 0)

    def turn(phase, start):
        row = row_numbers(phase.shape[0], start)
        inside = (row >= 0) & (row < total_rows)
        return jnp.where(inside, jnp.cos(phase), 0.0), jnp.where(inside, jnp.sin(phase), 0.0)

    cos0, sin0 = turn(jnp.concatenate([below[:ROWS], own_ref[0], above[:ROWS]], axis=0), 2 * REACH)
    phase1 = jnp.concatenate([below[ROWS:], own_ref[1], above[ROWS:]], axis=0)
    cos1, sin1 = turn(phase1, REACH)
    half = jnp.zeros((WIDE, TILE // 2), F32)
    cos1 = jnp.concatenate([half, cos1, half], axis=1)
    sin1 = jnp.concatenate([half, sin1, half], axis=1)
    turn1_ref[0] = cos1
    turn1_ref[1] = sin1
    row = row_numbers(WIDEST, 2 * REACH).astype(F32)
    column = lax.broadcasted_iota(jnp.int32, (1, width), 1).astype(F32)
    for angle in range(measured_ref.shape[0]):
        along, over = tilts_ref[angle, 0] * row, tilts_ref[angle, 1] * column
        cos_r, sin_r, cos_c, sin_c = jnp.cos(along), jnp.sin(along), jnp.cos(over), jnp.sin(over)
        left_r, left_i = cos0 * cos_r - sin0 * sin_r, sin0 * cos_r + cos0 * sin_r
        real, imag = left_r * cos_c - left_i * sin_c, left_r * sin_c + left_i * cos_c
        wave0_ref[angle, 0] = real[2 * REACH : 2 * REACH + ROWS]
        wave0_ref[angle, 1] = imag[2 * REACH : 2 * REACH + ROWS]
        real, imag = row_pass(real, imag, rows1_ref, 0)
        real, imag = column_pass(real, imag, band_ref, 0, tiles + 1, -1)
        real, imag = cos1 * real - sin1 * imag, cos1 * imag + sin1 * real
        wave1_ref[angle, 0] = real[REACH : REACH + ROWS]
        wave1_ref[angle, 1] = imag[REACH : REACH + ROWS]
        real, imag = row_pass(real, imag, rows2_ref, 0)
        real, imag = column_pass(real, imag, band_ref, 0, tiles, 0)
        real, imag = real - measured_ref[angle, 0], imag - measured_ref[angle, 1]
        real, imag = column_pass(real, imag, band_ref, 1, tiles + 1, -1)
        spread_ref[angle, 0] = real
        spread_ref[angle, 1] = imag


def backward(
    where_ref, own_ref, across_ref, beside_ref, wave0_ref, wave1_ref, turn1_ref, rows1_ref, rows2_ref, band_ref,
    out_ref,
):
    even = where_ref[1] == 0
    tiles = wave0_ref.shape[3] // TILE
    for angle in range(own_ref.shape[0]):
        window = []
        for part in range(2):
            below, above = neighbours(even, across_ref[angle, part], beside_ref[angle, part])
            window.append(jnp.concatenate([below, own_ref[angle, part], above], axis=0))
        real, imag = row_pass(window[0], window[1], rows1_ref, 1)
        keep = slice(REACH, REACH + ROWS)
        term1 = wave1_ref[angle, 0] * imag[keep] - wave1_ref[angle, 1] * real[keep]
        cos1, sin1 = turn1_ref[0], turn1_ref[1]
        real, imag = cos1 * real + sin1 * imag, cos1 * imag - sin1 * real
        real, imag = column_pass(real, imag, band_ref, 1, tiles, 0)
        real, imag = row_pass(real, imag, rows2_ref, 1)
        term0 = wave0_ref[angle, 0] * imag - wave0_ref[angle, 1] * real
        total0 = term0 if angle == 0 else total0 + term0
        total1 = term1 if angle == 0 else total1 + term1
    total1 = total1[:, TILE // 2 : TILE // 2 + tiles * TILE]
    for j in range(tiles):
        out_ref[j, 0] = total0[:, j * TILE : (j + 1) * TILE]
        out_ref[j, 1] = total1[:, j * TILE : (j + 1) * TILE]


def call(kernel, shapes, scalars, arrays, flops):
    moved = sum(a.size * a.dtype.itemsize for a in arrays)
    moved += sum(int(s.size) * s.dtype.itemsize for s in shapes)
    return pl.pallas_call(
        kernel,
        out_shape=shapes,
        in_specs=[pl.BlockSpec(memory_space=pltpu.SMEM)] * len(scalars)
        + [pl.BlockSpec(memory_space=pltpu.VMEM)] * len(arrays),
        out_specs=[pl.BlockSpec(memory_space=pltpu.VMEM)] * len(shapes),
        compiler_params=pltpu.CompilerParams(vmem_limit_bytes=VMEM_LIMIT),
        cost_estimate=pl.CostEstimate(flops=flops, bytes_accessed=moved, transcendentals=0),
    )(*scalars, *arrays)


def swaps(pairs):
    return pairs + [(b, a) for a, b in pairs]


def body(total_rows, phase_delay, measured, tilts, fresnel_taps):
    angles, columns = measured.shape[0], phase_delay.shape[2]
    strips = lax.axis_size("space")
    strip = lax.axis_index("space")
    parity = strip % 2
    where = jnp.stack([strip * ROWS, parity]).astype(jnp.int32)
    over_border = swaps([(i, i + 1) for i in range(1, strips - 1, 2)])
    in_chip = swaps([(i, i + 1) for i in range(0, strips, 2)])
    low, high = phase_delay[1, :REACH], phase_delay[1, ROWS - REACH :]
    to_border = jnp.concatenate([phase_delay[0], jnp.where(parity == 0, low, high)], axis=0)
    to_core = jnp.concatenate([phase_delay[0], jnp.where(parity == 0, high, low)], axis=0)
    across = lax.ppermute(to_border, "space", over_border)
    beside = lax.ppermute(to_core, "space", in_chip)
    struct = jax.ShapeDtypeStruct
    rows1, rows2, band = call(
        tap_matrices,
        [
            struct((2, 2, 2 * WIDE, 2 * WIDEST), BF16),
            struct((2, 2, 2 * ROWS, 2 * WIDE), BF16),
            struct((2, 2, 512, 256), BF16),
        ],
        [fresnel_taps],
        [],
        10_000_000,
    )
    spread, wave0, wave1, turn1 = call(
        functools.partial(forward, total_rows=total_rows, total_columns=columns),
        [
            struct((angles, 2, ROWS, columns + TILE), F32),
            struct((angles, 2, ROWS, columns), F32),
            struct((angles, 2, ROWS, columns + TILE), F32),
            struct((2, WIDE, columns + TILE), F32),
        ],
        [where, tilts],
        [phase_delay, across, beside, measured, rows1, rows2, band],
        4_000_000_000,
    )
    across = lax.ppermute(spread, "space", over_border)
    beside = lax.ppermute(spread, "space", in_chip)
    (tiles,) = call(
        backward,
        [struct((columns // TILE, 2, ROWS, TILE), F32)],
        [where],
        [spread, across, beside, wave0, wave1, turn1, rows1, rows2, band],
        3_000_000_000,
    )
    return jnp.sum(lax.all_to_all(tiles, "angle", 0, 0), axis=0)


def solution(mesh):
    def step(phase_delay, measured, tilts, fresnel_taps):
        return jax.shard_map(
            functools.partial(body, phase_delay.shape[1]),
            mesh=mesh,
            in_specs=(P(None, "space", None), P("angle", None, "space", None), P("angle", None), P()),
            out_specs=P(None, "space", "angle"),
            check_vma=False,
        )(phase_delay, measured, tilts, fresnel_taps)

    return step
```

```python
import functools

import jax
import jax.numpy as jnp
from jax import lax
from jax.experimental import pallas as pl
from jax.experimental.pallas import tpu as pltpu
from jax.sharding import PartitionSpec as P

TILE = 128
REACH = 16
TAPS = 2 * REACH + 1
ROWS = 32
WIDE = ROWS + 2 * REACH
WIDEST = ROWS + 4 * REACH
F32 = jnp.float32
BF16 = jnp.bfloat16
VMEM_LIMIT = 48 * 1024 * 1024


def split(x):
    high = x.astype(BF16)
    return high, (x - high.astype(F32)).astype(BF16)


def cos_sin(x):
    turns = jnp.round(x * 0.6366197723675814)
    rest = ((x - turns * 1.5703125) - turns * 4.837512969970703125e-4) - turns * 7.54978995489188216e-8
    square = rest * rest
    sine = rest + rest * square * (
        -1.6666654611e-1 + square * (8.3321608736e-3 + square * -1.9515295891e-4)
    )
    cosine = (1.0 - 0.5 * square) + square * square * (
        4.166664568298827e-2 + square * (-1.388731625493765e-3 + square * 2.443315711809948e-5)
    )
    quarter = turns.astype(jnp.int32)
    odd = (quarter & 1) == 1
    cos_part, sin_part = jnp.where(odd, sine, cosine), jnp.where(odd, cosine, sine)
    return (
        jnp.where(((quarter + 1) & 2) == 2, -cos_part, cos_part),
        jnp.where((quarter & 2) == 2, -sin_part, sin_part),
    )


def matmul(a, b):
    return jnp.dot(a, b, preferred_element_type=F32)


def tap_matrices(taps_ref, rows1_ref, rows2_ref, band_ref):
    lane = lax.broadcasted_iota(jnp.int32, (8, 256), 1)

    def laid(direction, part, start, step):
        out = jnp.zeros((8, 256), F32)
        for tap in range(TAPS):
            out = jnp.where(lane == start + step * tap, taps_ref[direction, part, tap], out)
        return out

    def toeplitz(vector, rows):
        full = jnp.broadcast_to(vector[:1], (rows, 256))
        return pltpu.roll(full, 0, 1, stride=1, stride_axis=0)

    def put(ref, index, value):
        high, low = split(value)
        ref[index, 0] = high
        ref[index, 1] = low

    for index, sign in ((0, 1.0), (1, -1.0)):
        for ref, out_rows, in_rows in ((rows1_ref, WIDE, WIDEST), (rows2_ref, ROWS, WIDE)):
            halves = []
            for offset in (0, in_rows):
                start, step = (offset + TAPS - 1, -1) if index == 0 else (offset, 1)
                halves.append((laid(0, 0, start, step), laid(0, 1, start, step) * sign))
            top = toeplitz(halves[0][0] - halves[1][1], out_rows)
            bottom = toeplitz(halves[0][1] + halves[1][0], out_rows)
            put(ref, index, jnp.concatenate([top, bottom], axis=0)[:, : 2 * in_rows])
        first = 256 - TILE // 2 - REACH
        start, step = (first, 1) if index == 0 else (first + TAPS - 1, -1)
        real = toeplitz(laid(1, 0, start, step), 256)[:, :TILE]
        imag = toeplitz(laid(1, 1, start, step) * sign, 256)[:, :TILE]
        put(
            band_ref,
            index,
            jnp.concatenate(
                [
                    jnp.concatenate([real, imag], axis=1),
                    jnp.concatenate([-imag, real], axis=1),
                ],
                axis=0,
            ),
        )


def row_pass(real, imag, matrix_ref, index):
    high, low = split(jnp.concatenate([real, imag], axis=0))
    matrix_high = matrix_ref[index, 0]
    both = jnp.concatenate([matrix_high, matrix_ref[index, 1]], axis=0)
    count = matrix_high.shape[0]
    product = matmul(both, high)
    total = product[:count] + (product[count:] + matmul(matrix_high, low))
    return total[: count // 2], total[count // 2 :]


def column_pass(real, imag, band_ref, index, tiles, first):
    rows = real.shape[0]
    have = real.shape[1] // TILE
    blank = jnp.zeros((rows, TILE), BF16)
    parts = [split(real), split(imag)]

    def stacked(level):
        def tile(part, j):
            if 0 <= j < have:
                return parts[part][level][:, j * TILE : (j + 1) * TILE]
            return blank

        return jnp.concatenate(
            [
                jnp.concatenate(
                    [tile(0, first + j), tile(0, first + j + 1), tile(1, first + j), tile(1, first + j + 1)],
                    axis=1,
                )
                for j in range(tiles)
            ],
            axis=0,
        )

    high, low = stacked(0), stacked(1)
    band_high = band_ref[index, 0]
    out = matmul(high, band_high) + (matmul(low, band_high) + matmul(high, band_ref[index, 1]))
    pieces = [out[j * rows : (j + 1) * rows] for j in range(tiles)]
    return (
        jnp.concatenate([p[:, :TILE] for p in pieces], axis=1),
        jnp.concatenate([p[:, TILE:] for p in pieces], axis=1),
    )


def neighbours(even, across, beside):
    return jnp.where(even, across, beside), jnp.where(even, beside, across)


def pack(where_ref, phase_ref, border_ref, core_ref):
    even = where_ref[1] == 0
    low, high = phase_ref[1, :REACH], phase_ref[1, ROWS - REACH :]
    for ref, nearest in ((border_ref, jnp.where(even, low, high)), (core_ref, jnp.where(even, high, low))):
        ref[:ROWS] = phase_ref[0]
        ref[ROWS:] = nearest


def half_tile(x):
    blank = jnp.zeros((x.shape[0], TILE // 2), x.dtype)
    return jnp.concatenate([blank, x, blank], axis=1)


def prepare(
    where_ref, tilts_ref, taps_ref, phase_ref,
    turn0_ref, turn1_ref, along_ref, over_ref, rows1_ref, rows2_ref, band_ref,
):
    tap_matrices(taps_ref, rows1_ref, rows2_ref, band_ref)
    turn0_ref[0], turn0_ref[1] = cos_sin(phase_ref[0])
    cosine, sine = cos_sin(phase_ref[1])
    turn1_ref[0], turn1_ref[1] = half_tile(cosine), half_tile(sine)
    row = (where_ref[0] - 2 * REACH + lax.broadcasted_iota(jnp.int32, (WIDEST, TILE), 0)).astype(F32)
    column = lax.broadcasted_iota(jnp.int32, (8, phase_ref.shape[2]), 1).astype(F32)
    for angle in range(along_ref.shape[0]):
        along_ref[angle, 0], along_ref[angle, 1] = cos_sin(tilts_ref[angle, 0] * row)
        over_ref[angle, 0], over_ref[angle, 1] = cos_sin(tilts_ref[angle, 1] * column)


def forward(
    where_ref, across_ref, beside_ref, own0_ref, own1_ref, along_ref, over_ref, measured_ref,
    rows1_ref, rows2_ref, band_ref, spread_ref, wave0_ref, wave1_ref, turn1_ref, *, total_rows,
):
    first_row = where_ref[0]
    even = where_ref[1] == 0
    below, above = neighbours(even, across_ref[...], beside_ref[...])
    tiles = own0_ref.shape[2] // TILE
    below_there, above_there = first_row > 0, first_row + ROWS < total_rows

    def turn(phase, there):
        cosine, sine = cos_sin(phase)
        return jnp.where(there, cosine, 0.0), jnp.where(there, sine, 0.0)

    cos_b, sin_b = turn(below, below_there)
    cos_a, sin_a = turn(above, above_there)
    cos0 = jnp.concatenate([cos_b[:ROWS], own0_ref[0], cos_a[:ROWS]], axis=0)
    sin0 = jnp.concatenate([sin_b[:ROWS], own0_ref[1], sin_a[:ROWS]], axis=0)
    cos1 = jnp.concatenate([half_tile(cos_b[ROWS:]), own1_ref[0], half_tile(cos_a[ROWS:])], axis=0)
    sin1 = jnp.concatenate([half_tile(sin_b[ROWS:]), own1_ref[1], half_tile(sin_a[ROWS:])], axis=0)
    turn1_ref[0] = cos1
    turn1_ref[1] = sin1
    for angle in range(measured_ref.shape[0]):
        cos_r, sin_r = along_ref[angle, 0, :, :1], along_ref[angle, 1, :, :1]
        cos_c, sin_c = over_ref[angle, 0, :1], over_ref[angle, 1, :1]
        left_r, left_i = cos0 * cos_r - sin0 * sin_r, sin0 * cos_r + cos0 * sin_r
        real, imag = left_r * cos_c - left_i * sin_c, left_r * sin_c + left_i * cos_c
        wave0_ref[angle, 0] = real[2 * REACH : 2 * REACH + ROWS]
        wave0_ref[angle, 1] = imag[2 * REACH : 2 * REACH + ROWS]
        real, imag = row_pass(real, imag, rows1_ref, 0)
        real, imag = column_pass(real, imag, band_ref, 0, tiles + 1, -1)
        real, imag = cos1 * real - sin1 * imag, cos1 * imag + sin1 * real
        wave1_ref[angle, 0] = real[REACH : REACH + ROWS]
        wave1_ref[angle, 1] = imag[REACH : REACH + ROWS]
        real, imag = row_pass(real, imag, rows2_ref, 0)
        real, imag = column_pass(real, imag, band_ref, 0, tiles, 0)
        real, imag = real - measured_ref[angle, 0], imag - measured_ref[angle, 1]
        real, imag = column_pass(real, imag, band_ref, 1, tiles + 1, -1)
        spread_ref[angle, 0] = real
        spread_ref[angle, 1] = imag


def backward(
    where_ref, own_ref, across_ref, beside_ref, wave0_ref, wave1_ref, turn1_ref, rows1_ref, rows2_ref, band_ref,
    out_ref,
):
    even = where_ref[1] == 0
    tiles = wave0_ref.shape[3] // TILE
    for angle in range(own_ref.shape[0]):
        window = []
        for part in range(2):
            below, above = neighbours(even, across_ref[angle, part], beside_ref[angle, part])
            window.append(jnp.concatenate([below, own_ref[angle, part], above], axis=0))
        real, imag = row_pass(window[0], window[1], rows1_ref, 1)
        keep = slice(REACH, REACH + ROWS)
        term1 = wave1_ref[angle, 0] * imag[keep] - wave1_ref[angle, 1] * real[keep]
        cos1, sin1 = turn1_ref[0], turn1_ref[1]
        real, imag = cos1 * real + sin1 * imag, cos1 * imag - sin1 * real
        real, imag = column_pass(real, imag, band_ref, 1, tiles, 0)
        real, imag = row_pass(real, imag, rows2_ref, 1)
        term0 = wave0_ref[angle, 0] * imag - wave0_ref[angle, 1] * real
        total0 = term0 if angle == 0 else total0 + term0
        total1 = term1 if angle == 0 else total1 + term1
    total1 = total1[:, TILE // 2 : TILE // 2 + tiles * TILE]
    for j in range(tiles):
        out_ref[j, 0] = total0[:, j * TILE : (j + 1) * TILE]
        out_ref[j, 1] = total1[:, j * TILE : (j + 1) * TILE]


def call(kernel, shapes, scalars, arrays, flops):
    moved = sum(a.size * a.dtype.itemsize for a in arrays)
    moved += sum(int(s.size) * s.dtype.itemsize for s in shapes)
    return pl.pallas_call(
        kernel,
        out_shape=shapes,
        in_specs=[pl.BlockSpec(memory_space=pltpu.SMEM)] * len(scalars)
        + [pl.BlockSpec(memory_space=pltpu.VMEM)] * len(arrays),
        out_specs=[pl.BlockSpec(memory_space=pltpu.VMEM)] * len(shapes),
        compiler_params=pltpu.CompilerParams(vmem_limit_bytes=VMEM_LIMIT),
        cost_estimate=pl.CostEstimate(flops=flops, bytes_accessed=moved, transcendentals=0),
    )(*scalars, *arrays)


def swaps(pairs):
    return pairs + [(b, a) for a, b in pairs]


def body(total_rows, phase_delay, measured, tilts, fresnel_taps):
    angles, columns = measured.shape[0], phase_delay.shape[2]
    strips = lax.axis_size("space")
    strip = lax.axis_index("space")
    parity = strip % 2
    where = jnp.stack([strip * ROWS, parity]).astype(jnp.int32)
    over_border = swaps([(i, i + 1) for i in range(1, strips - 1, 2)])
    in_chip = swaps([(i, i + 1) for i in range(0, strips, 2)])
    struct = jax.ShapeDtypeStruct
    to_border, to_core = call(
        pack, [struct((ROWS + REACH, columns), F32)] * 2, [where], [phase_delay], 0
    )
    beside = lax.ppermute(to_core, "space", in_chip)
    across = lax.ppermute(to_border, "space", over_border)
    own0, own1, along, over, rows1, rows2, band = call(
        prepare,
        [
            struct((2, ROWS, columns), F32),
            struct((2, ROWS, columns + TILE), F32),
            struct((angles, 2, WIDEST, TILE), F32),
            struct((angles, 2, 8, columns), F32),
            struct((2, 2, 2 * WIDE, 2 * WIDEST), BF16),
            struct((2, 2, 2 * ROWS, 2 * WIDE), BF16),
            struct((2, 2, 512, 256), BF16),
        ],
        [where, tilts, fresnel_taps],
        [phase_delay],
        10_000_000,
    )
    spread, wave0, wave1, turn1 = call(
        functools.partial(forward, total_rows=total_rows),
        [
            struct((angles, 2, ROWS, columns + TILE), F32),
            struct((angles, 2, ROWS, columns), F32),
            struct((angles, 2, ROWS, columns + TILE), F32),
            struct((2, WIDE, columns + TILE), F32),
        ],
        [where],
        [across, beside, own0, own1, along, over, measured, rows1, rows2, band],
        4_000_000_000,
    )
    beside = lax.ppermute(spread, "space", in_chip)
    across = lax.ppermute(spread, "space", over_border)
    (tiles,) = call(
        backward,
        [struct((columns // TILE, 2, ROWS, TILE), F32)],
        [where],
        [spread, across, beside, wave0, wave1, turn1, rows1, rows2, band],
        3_000_000_000,
    )
    return jnp.sum(lax.all_to_all(tiles, "angle", 0, 0), axis=0)


def solution(mesh):
    def step(phase_delay, measured, tilts, fresnel_taps):
        return jax.shard_map(
            functools.partial(body, phase_delay.shape[1]),
            mesh=mesh,
            in_specs=(P(None, "space", None), P("angle", None, "space", None), P("angle", None), P()),
            out_specs=P(None, "space", "angle"),
            check_vma=False,
        )(phase_delay, measured, tilts, fresnel_taps)

    return step
```

```python
import functools

import jax
import jax.numpy as jnp
from jax import lax
from jax.experimental import pallas as pl
from jax.experimental.pallas import tpu as pltpu
from jax.sharding import PartitionSpec as P

TILE = 128
REACH = 16
TAPS = 2 * REACH + 1
ROWS = 32
WIDE = ROWS + 2 * REACH
WIDEST = ROWS + 4 * REACH
F32 = jnp.float32
BF16 = jnp.bfloat16
GROUP = 4
BLOCK = 512
FRAME0 = BLOCK + 2 * TILE
FRAME1 = BLOCK + TILE
VMEM_LIMIT = 32 * 1024 * 1024


def split(x):
    high = x.astype(BF16)
    return high, (x - high.astype(F32)).astype(BF16)


def cos_sin(x):
    turns = jnp.round(x * 0.6366197723675814)
    rest = ((x - turns * 1.5703125) - turns * 4.837512969970703125e-4) - turns * 7.54978995489188216e-8
    square = rest * rest
    sine = rest + rest * square * (
        -1.6666654611e-1 + square * (8.3321608736e-3 + square * -1.9515295891e-4)
    )
    cosine = (1.0 - 0.5 * square) + square * square * (
        4.166664568298827e-2 + square * (-1.388731625493765e-3 + square * 2.443315711809948e-5)
    )
    quarter = turns.astype(jnp.int32)
    odd = (quarter & 1) == 1
    cos_part, sin_part = jnp.where(odd, sine, cosine), jnp.where(odd, cosine, sine)
    return (
        jnp.where(((quarter + 1) & 2) == 2, -cos_part, cos_part),
        jnp.where((quarter & 2) == 2, -sin_part, sin_part),
    )


def matmul(a, b):
    return jnp.dot(a, b, preferred_element_type=F32)


def tap_matrices(taps_ref, into1_ref, into2_ref, out1_ref, out2_ref, band_ref):
    lane = lax.broadcasted_iota(jnp.int32, (8, 256), 1)

    def laid(direction, part, start, step):
        out = jnp.zeros((8, 256), F32)
        for tap in range(TAPS):
            out = jnp.where(lane == (start + step * tap) % 256, taps_ref[direction, part, tap], out)
        return out

    def toeplitz(vector, rows):
        full = jnp.broadcast_to(vector[:1], (rows, 256))
        return pltpu.roll(full, 0, 1, stride=1, stride_axis=0)

    def put(ref, index, value):
        high, low = split(value)
        ref[index, 0] = high
        ref[index, 1] = low

    for ref, out_rows, in_rows, last, step, sign in (
        (into1_ref, WIDE, WIDEST, TAPS - 1, -1, 1.0),
        (into2_ref, ROWS, WIDE, TAPS - 1, -1, 1.0),
        (out1_ref, WIDE, ROWS, 1 - TAPS, 1, -1.0),
        (out2_ref, WIDEST, WIDE, 1 - TAPS, 1, -1.0),
    ):
        column = lax.broadcasted_iota(jnp.int32, (out_rows, 256), 1)
        real, imag = laid(0, 0, last, step), laid(0, 1, last, step) * sign
        real_2, imag_2 = laid(0, 0, in_rows + last, step), laid(0, 1, in_rows + last, step) * sign
        first = column < in_rows
        top = jnp.where(first, toeplitz(real, out_rows), -toeplitz(imag_2, out_rows))
        bottom = jnp.where(first, toeplitz(imag, out_rows), toeplitz(real_2, out_rows))
        put(ref, 0, jnp.concatenate([top, bottom], axis=0)[:, : 2 * in_rows])
    for index, sign in ((0, 1.0), (1, -1.0)):
        first = 256 - TILE // 2 - REACH
        start, step = (first, 1) if index == 0 else (first + TAPS - 1, -1)
        real = toeplitz(laid(1, 0, start, step), 256)[:, :TILE]
        imag = toeplitz(laid(1, 1, start, step) * sign, 256)[:, :TILE]
        put(
            band_ref,
            index,
            jnp.concatenate(
                [
                    jnp.concatenate([real, imag], axis=1),
                    jnp.concatenate([-imag, real], axis=1),
                ],
                axis=0,
            ),
        )


def row_pass(real, imag, matrix_ref):
    high, low = split(jnp.concatenate([real, imag], axis=0))
    matrix_high = matrix_ref[0, 0]
    both = jnp.concatenate([matrix_high, matrix_ref[0, 1]], axis=0)
    count = matrix_high.shape[0]
    product = matmul(both, high)
    total = product[:count] + (product[count:] + matmul(matrix_high, low))
    return total[: count // 2], total[count // 2 :]


def column_pass(real, imag, band_ref, index, tiles, first):
    rows = real.shape[0]
    have = real.shape[1] // TILE
    blank = jnp.zeros((rows, TILE), BF16)
    parts = [split(real), split(imag)]

    def stacked(level):
        def tile(part, j):
            if 0 <= j < have:
                return parts[part][level][:, j * TILE : (j + 1) * TILE]
            return blank

        return jnp.concatenate(
            [
                jnp.concatenate(
                    [tile(0, first + j), tile(0, first + j + 1), tile(1, first + j), tile(1, first + j + 1)],
                    axis=1,
                )
                for j in range(tiles)
            ],
            axis=0,
        )

    high, low = stacked(0), stacked(1)
    band_high = band_ref[index, 0]
    out = matmul(high, band_high) + (matmul(low, band_high) + matmul(high, band_ref[index, 1]))
    pieces = [out[j * rows : (j + 1) * rows] for j in range(tiles)]
    return (
        jnp.concatenate([p[:, :TILE] for p in pieces], axis=1),
        jnp.concatenate([p[:, TILE:] for p in pieces], axis=1),
    )


def neighbours(even, across, beside):
    return jnp.where(even, across, beside), jnp.where(even, beside, across)


def half_tile(x):
    blank = jnp.zeros((x.shape[0], TILE // 2), x.dtype)
    return jnp.concatenate([blank, x, blank], axis=1)


def padded_columns(source_ref, room_ref, semaphore):
    columns = source_ref.shape[-1]
    copy = pltpu.make_async_copy(source_ref, room_ref.at[:, :, TILE : TILE + columns], semaphore)
    copy.start()
    blank = jnp.zeros(room_ref.shape[:2] + (TILE,), F32)
    room_ref[:, :, :TILE] = blank
    room_ref[:, :, TILE + columns :] = blank
    copy.wait()


def block_of(room_ref, part, block):
    start = pl.multiple_of(block * BLOCK, TILE)
    return room_ref[part, :, pl.ds(start, FRAME0)][:, TILE // 2 : TILE // 2 + FRAME1]


def pack_phase(where_ref, phase_ref, border_ref, core_ref, own_ref, room_ref, semaphore):
    even = where_ref[1] == 0
    padded_columns(phase_ref, room_ref, semaphore)
    own_ref[0] = block_of(room_ref, 0, where_ref[2])
    own_ref[1] = block_of(room_ref, 1, where_ref[2])
    low, high = own_ref[1, :REACH], own_ref[1, ROWS - REACH :]
    for ref, nearest in ((border_ref, jnp.where(even, low, high)), (core_ref, jnp.where(even, high, low))):
        ref[:ROWS] = own_ref[0]
        ref[ROWS:] = nearest


def pack_measured(where_ref, tilts_ref, measured_ref, *refs):
    block_refs, room_ref, semaphore = refs[:GROUP], refs[GROUP], refs[GROUP + 1]
    padded_columns(measured_ref.at[0], room_ref, semaphore)
    lane = lax.broadcasted_iota(jnp.int32, (8, TILE), 1)
    row = lax.broadcasted_iota(jnp.int32, (8, TILE), 0)
    for shift, ref in enumerate(block_refs):
        block = lax.rem(where_ref[2] + shift, GROUP)
        ref[0] = block_of(room_ref, 0, block)
        ref[1] = block_of(room_ref, 1, block)
        corner = ref[0, :8, :TILE]
        corner = jnp.where((row == 0) & (lane == 0), tilts_ref[0, 0], corner)
        ref[0, :8, :TILE] = jnp.where((row == 0) & (lane == 1), tilts_ref[0, 1], corner)


def prepare(where_ref, taps_ref, own_ref, turn_ref, into1_ref, into2_ref, out1_ref, out2_ref, band_ref):
    tap_matrices(taps_ref, into1_ref, into2_ref, out1_ref, out2_ref, band_ref)
    for layer in range(2):
        turn_ref[layer, 0], turn_ref[layer, 1] = inside_grid(where_ref, *cos_sin(own_ref[layer]))


def inside_grid(where_ref, *fields):
    count = fields[0].shape[1]
    margin = (count - BLOCK) // 2
    lane = lax.broadcasted_iota(jnp.int32, (1, count), 1)
    there = ((lane >= margin) | (where_ref[2] != 0)) & ((lane < margin + BLOCK) | (where_ref[2] != GROUP - 1))
    return [jnp.where(there, field, 0.0) for field in fields]


def turns(where_ref, across_ref, beside_ref, own_ref, turn0_ref, turn1_ref, total_rows):
    even = where_ref[1] == 0
    first_row = where_ref[0]
    below, above = neighbours(even, across_ref[...], beside_ref[...])
    below = [jnp.where(first_row > 0, x, 0.0) for x in inside_grid(where_ref, *cos_sin(below))]
    above = [jnp.where(first_row + ROWS < total_rows, x, 0.0) for x in inside_grid(where_ref, *cos_sin(above))]
    for part in range(2):
        turn0_ref[part] = half_tile(jnp.concatenate([below[part][:ROWS], own_ref[0, part], above[part][:ROWS]], axis=0))
        turn1_ref[part] = jnp.concatenate([below[part][ROWS:], own_ref[1, part], above[part][ROWS:]], axis=0)


def sweep(where_ref, measured_ref, turn0_ref, turn1_ref, into1_ref, into2_ref, out1_ref, out2_ref, band_ref):
    row = (where_ref[0] - 2 * REACH + lax.broadcasted_iota(jnp.int32, (WIDEST, TILE), 0)).astype(F32)
    column = where_ref[2] * BLOCK - TILE + lax.broadcasted_iota(jnp.int32, (8, FRAME0), 1)
    cos_r, sin_r = cos_sin(measured_ref[0, :1, :1] * row)
    cos_c, sin_c = cos_sin(measured_ref[0, :1, 1:2] * column.astype(F32))
    cos_r, sin_r, cos_c, sin_c = cos_r[:, :1], sin_r[:, :1], cos_c[:1], sin_c[:1]
    cos0, sin0, cos1, sin1 = turn0_ref[0], turn0_ref[1], turn1_ref[0], turn1_ref[1]
    left_r, left_i = cos0 * cos_r - sin0 * sin_r, sin0 * cos_r + cos0 * sin_r
    wave0 = left_r * cos_c - left_i * sin_c, left_r * sin_c + left_i * cos_c
    real, imag = row_pass(*wave0, into1_ref)
    real, imag = column_pass(real, imag, band_ref, 0, FRAME1 // TILE, 0)
    wave1 = cos1 * real - sin1 * imag, cos1 * imag + sin1 * real
    real, imag = row_pass(*wave1, into2_ref)
    real, imag = column_pass(real, imag, band_ref, 0, FRAME0 // TILE, -1)
    real, imag = inside_grid(
        where_ref, real - half_tile(measured_ref[0]), imag - half_tile(measured_ref[1])
    )
    real, imag = column_pass(real, imag, band_ref, 1, FRAME1 // TILE, 0)
    real, imag = row_pass(real, imag, out1_ref)
    term1 = wave1[0] * imag - wave1[1] * real
    real, imag = cos1 * real + sin1 * imag, cos1 * imag - sin1 * real
    real, imag = column_pass(real, imag, band_ref, 1, BLOCK // TILE, 0)
    real, imag = row_pass(real, imag, out2_ref)
    middle = slice(TILE, TILE + BLOCK)
    return wave0[0][:, middle] * imag - wave0[1][:, middle] * real, term1


def first_angle(
    where_ref, across_ref, beside_ref, own_ref, measured_ref, into1_ref, into2_ref, out1_ref, out2_ref, band_ref,
    turn0_ref, turn1_ref, total0_ref, total1_ref, *, total_rows,
):
    turns(where_ref, across_ref, beside_ref, own_ref, turn0_ref, turn1_ref, total_rows)
    total0_ref[...], total1_ref[...] = sweep(
        where_ref, measured_ref, turn0_ref, turn1_ref, into1_ref, into2_ref, out1_ref, out2_ref, band_ref
    )


def other_angles(where_ref, *refs):
    measured_refs, (total0_ref, total1_ref), rest = refs[: GROUP - 1], refs[GROUP - 1 : GROUP + 1], refs[GROUP + 1 : -1]
    out_ref = refs[-1]
    total0, total1 = total0_ref[...], total1_ref[...]
    for measured_ref in measured_refs:
        term0, term1 = sweep(where_ref, measured_ref, *rest)
        total0, total1 = total0 + term0, total1 + term1
    total1 = total1[:, TILE // 2 : TILE // 2 + BLOCK]
    for j in range(BLOCK // TILE):
        out_ref[j, :WIDEST] = total0[:, j * TILE : (j + 1) * TILE]
        out_ref[j, WIDEST:] = total1[:, j * TILE : (j + 1) * TILE]


def add_angles(where_ref, tiles_ref, own_ref, border_ref, core_ref):
    even = where_ref[1] == 0
    total = tiles_ref[0]
    for j in range(1, tiles_ref.shape[0]):
        total = total + tiles_ref[j]
    slice0, slice1 = total[:WIDEST], total[WIDEST:]
    own_ref[0] = slice0[ROWS : 2 * ROWS]
    own_ref[1] = slice1[REACH : REACH + ROWS]
    low = jnp.concatenate([slice0[:ROWS], slice1[:REACH]], axis=0)
    high = jnp.concatenate([slice0[2 * ROWS :], slice1[REACH + ROWS :]], axis=0)
    border_ref[...] = jnp.where(even, low, high)
    core_ref[...] = jnp.where(even, high, low)


def add_strips(where_ref, own_ref, across_ref, beside_ref, out_ref):
    below, above = neighbours(where_ref[1] == 0, across_ref[...], beside_ref[...])
    out_ref[0] = own_ref[0] + (below[:ROWS] + above[:ROWS])
    out_ref[1, :REACH] = own_ref[1, :REACH] + below[ROWS:]
    out_ref[1, REACH:] = own_ref[1, REACH:] + above[ROWS:]


def call(kernel, shapes, scalars, arrays, flops, scratch=(), space=pltpu.VMEM):
    moved = sum(a.size * a.dtype.itemsize for a in arrays)
    moved += sum(int(s.size) * s.dtype.itemsize for s in shapes)
    return pl.pallas_call(
        kernel,
        out_shape=shapes,
        in_specs=[pl.BlockSpec(memory_space=pltpu.SMEM)] * len(scalars)
        + [pl.BlockSpec(memory_space=space)] * len(arrays),
        out_specs=[pl.BlockSpec(memory_space=pltpu.VMEM)] * len(shapes),
        scratch_shapes=list(scratch),
        compiler_params=pltpu.CompilerParams(vmem_limit_bytes=VMEM_LIMIT),
        cost_estimate=pl.CostEstimate(flops=flops, bytes_accessed=moved, transcendentals=0),
    )(*scalars, *arrays)


def swaps(pairs):
    return pairs + [(b, a) for a, b in pairs]


def body(total_rows, phase_delay, measured, tilts, fresnel_taps):
    columns = phase_delay.shape[2]
    strips = lax.axis_size("space")
    along = lax.axis_size("angle") // GROUP
    strip = lax.axis_index("space")
    block = lax.axis_index("angle") // along
    where = jnp.stack([strip * ROWS, strip & 1, block]).astype(jnp.int32)
    over_border = swaps([(i, i + 1) for i in range(1, strips - 1, 2)])
    in_chip = swaps([(i, i + 1) for i in range(0, strips, 2)])

    def shifted(shift):
        return [(g * along + i, (g + shift) % GROUP * along + i) for g in range(GROUP) for i in range(along)]

    struct = jax.ShapeDtypeStruct
    room = [pltpu.VMEM((2, ROWS, columns + 2 * TILE), F32), pltpu.SemaphoreType.DMA]
    to_border, to_core, own_phase = call(
        pack_phase,
        [struct((ROWS + REACH, FRAME1), F32)] * 2 + [struct((2, ROWS, FRAME1), F32)],
        [where],
        [phase_delay],
        0,
        room,
        pl.ANY,
    )
    beside = lax.ppermute(to_core, "space", in_chip)
    across = lax.ppermute(to_border, "space", over_border)
    blocks = call(
        pack_measured,
        [struct((2, ROWS, FRAME1), F32)] * GROUP,
        [where, tilts],
        [measured],
        0,
        room,
        pl.ANY,
    )
    arrived = [lax.ppermute(blocks[shift], "angle", shifted(shift)) for shift in range(1, GROUP)]
    own, *matrices = call(
        prepare,
        [
            struct((2, 2, ROWS, FRAME1), F32),
            struct((1, 2, 2 * WIDE, 2 * WIDEST), BF16),
            struct((1, 2, 2 * ROWS, 2 * WIDE), BF16),
            struct((1, 2, 2 * WIDE, 2 * ROWS), BF16),
            struct((1, 2, 2 * WIDEST, 2 * WIDE), BF16),
            struct((2, 2, 512, 256), BF16),
        ],
        [where, fresnel_taps],
        [own_phase],
        10_000_000,
    )
    turn0, turn1, total0, total1 = call(
        functools.partial(first_angle, total_rows=total_rows),
        [
            struct((2, WIDEST, FRAME0), F32),
            struct((2, WIDE, FRAME1), F32),
            struct((WIDEST, BLOCK), F32),
            struct((WIDE, FRAME1), F32),
        ],
        [where],
        [across, beside, own, blocks[0], *matrices],
        2_000_000_000,
    )
    (tiles,) = call(
        other_angles,
        [struct((BLOCK // TILE, WIDEST + WIDE, TILE), F32)],
        [where],
        [*arrived, total0, total1, turn0, turn1, *matrices],
        6_000_000_000,
    )
    beside_x = [[g * along + i for i in range(along)] for g in range(GROUP)]
    tiles = lax.all_to_all(tiles, "angle", 0, 0, axis_index_groups=beside_x)
    total, to_border, to_core = call(
        add_angles,
        [struct((2, ROWS, TILE), F32)] + [struct((ROWS + REACH, TILE), F32)] * 2,
        [where],
        [tiles],
        0,
    )
    beside = lax.ppermute(to_core, "space", in_chip)
    across = lax.ppermute(to_border, "space", over_border)
    (gradient,) = call(add_strips, [struct((2, ROWS, TILE), F32)], [where], [total, across, beside], 0)
    return gradient


def solution(mesh):
    def step(phase_delay, measured, tilts, fresnel_taps):
        return jax.shard_map(
            functools.partial(body, phase_delay.shape[1]),
            mesh=mesh,
            in_specs=(P(None, "space", None), P("angle", None, "space", None), P("angle", None), P()),
            out_specs=P(None, "space", "angle"),
            check_vma=False,
        )(phase_delay, measured, tilts, fresnel_taps)

    return step
```

```python
import functools

import jax
import jax.numpy as jnp
from jax import lax
from jax.experimental import pallas as pl
from jax.experimental.pallas import tpu as pltpu
from jax.sharding import PartitionSpec as P

TILE = 128
REACH = 16
TAPS = 2 * REACH + 1
ROWS = 32
WIDE = ROWS + 2 * REACH
WIDEST = ROWS + 4 * REACH
F32 = jnp.float32
BF16 = jnp.bfloat16
GROUP = 4
BLOCK = 512
FRAME0 = BLOCK + 2 * TILE
FRAME1 = BLOCK + TILE
VMEM_LIMIT = 32 * 1024 * 1024


def split(x):
    high = x.astype(BF16)
    return high, (x - high.astype(F32)).astype(BF16)


def cos_sin(x):
    turns = jnp.round(x * 0.6366197723675814)
    rest = ((x - turns * 1.5703125) - turns * 4.837512969970703125e-4) - turns * 7.54978995489188216e-8
    square = rest * rest
    sine = rest + rest * square * (
        -1.6666654611e-1 + square * (8.3321608736e-3 + square * -1.9515295891e-4)
    )
    cosine = (1.0 - 0.5 * square) + square * square * (
        4.166664568298827e-2 + square * (-1.388731625493765e-3 + square * 2.443315711809948e-5)
    )
    quarter = turns.astype(jnp.int32)
    odd = (quarter & 1) == 1
    cos_part, sin_part = jnp.where(odd, sine, cosine), jnp.where(odd, cosine, sine)
    return (
        jnp.where(((quarter + 1) & 2) == 2, -cos_part, cos_part),
        jnp.where((quarter & 2) == 2, -sin_part, sin_part),
    )


def matmul(a, b):
    return jnp.dot(a, b, preferred_element_type=F32)


def tap_matrices(taps_ref, into1_ref, into2_ref, out1_ref, out2_ref, band_ref):
    lane = lax.broadcasted_iota(jnp.int32, (8, 256), 1)

    def laid(direction, part, start, step):
        out = jnp.zeros((8, 256), F32)
        for tap in range(TAPS):
            out = jnp.where(lane == (start + step * tap) % 256, taps_ref[direction, part, tap], out)
        return out

    def toeplitz(vector, rows):
        full = jnp.broadcast_to(vector[:1], (rows, 256))
        return pltpu.roll(full, 0, 1, stride=1, stride_axis=0)

    def put(ref, index, value):
        high, low = split(value)
        ref[index, 0] = high
        ref[index, 1] = low

    for ref, out_rows, in_rows, last, step, sign in (
        (into1_ref, WIDE, WIDEST, TAPS - 1, -1, 1.0),
        (into2_ref, ROWS, WIDE, TAPS - 1, -1, 1.0),
        (out1_ref, WIDE, ROWS, 1 - TAPS, 1, -1.0),
        (out2_ref, WIDEST, WIDE, 1 - TAPS, 1, -1.0),
    ):
        column = lax.broadcasted_iota(jnp.int32, (out_rows, 256), 1)
        real, imag = laid(0, 0, last, step), laid(0, 1, last, step) * sign
        real_2, imag_2 = laid(0, 0, in_rows + last, step), laid(0, 1, in_rows + last, step) * sign
        first = column < in_rows
        top = jnp.where(first, toeplitz(real, out_rows), -toeplitz(imag_2, out_rows))
        bottom = jnp.where(first, toeplitz(imag, out_rows), toeplitz(real_2, out_rows))
        high, low = split(jnp.concatenate([top, bottom], axis=0)[:, : 2 * in_rows])
        if ref.shape[1] == 2 * in_rows:
            ref[...] = jnp.concatenate([high, low], axis=0)
        else:
            high = high.astype(F32)
            low = low.astype(F32)
            both = jnp.concatenate([high, low], axis=0), jnp.concatenate([high, jnp.zeros_like(low)], axis=0)
            ref[...] = jnp.concatenate(both, axis=1).astype(BF16)
    for index, sign in ((0, 1.0), (1, -1.0)):
        first = 256 - TILE // 2 - REACH
        start, step = (first, 1) if index == 0 else (first + TAPS - 1, -1)
        real = toeplitz(laid(1, 0, start, step), 256)[:, :TILE]
        imag = toeplitz(laid(1, 1, start, step) * sign, 256)[:, :TILE]
        put(
            band_ref,
            index,
            jnp.concatenate(
                [
                    jnp.concatenate([real, imag], axis=1),
                    jnp.concatenate([-imag, real], axis=1),
                ],
                axis=0,
            ),
        )


def row_pass(fields, matrix_ref):
    columns = fields[0][0].shape[1]
    high, low = split(jnp.concatenate([jnp.concatenate(field, axis=0) for field in fields], axis=1))
    matrix = matrix_ref[...]
    count = matrix.shape[0] // 2
    if matrix.shape[1] == high.shape[0]:
        product = matmul(matrix, high)
        total = product[:count] + (product[count:] + matmul(matrix[:count], low))
    else:
        product = matmul(matrix, jnp.concatenate([high, low], axis=0))
        total = product[:count] + product[count:]
    pieces = [total[:, i * columns : (i + 1) * columns] for i in range(len(fields))]
    return [(piece[: count // 2], piece[count // 2 :]) for piece in pieces]


def column_pass(fields, band_ref, index, tiles, first):
    rows = fields[0][0].shape[0]
    have = fields[0][0].shape[1] // TILE
    blank = jnp.zeros((rows, TILE), BF16)

    def stacked(parts):
        def tile(part, j):
            return part[:, j * TILE : (j + 1) * TILE] if 0 <= j < have else blank

        return jnp.concatenate(
            [
                jnp.concatenate([tile(part, first + j + i) for part in field for i in range(2)], axis=1)
                for field in parts
                for j in range(tiles)
            ],
            axis=0,
        )

    levels = [[split(part) for part in field] for field in fields]
    high = stacked([[part[0] for part in field] for field in levels])
    low = stacked([[part[1] for part in field] for field in levels])
    band_high = band_ref[index, 0]
    out = matmul(high, band_high) + (matmul(low, band_high) + matmul(high, band_ref[index, 1]))
    results = []
    for i in range(len(fields)):
        pieces = [out[(i * tiles + j) * rows : (i * tiles + j + 1) * rows] for j in range(tiles)]
        results.append(
            (
                jnp.concatenate([p[:, :TILE] for p in pieces], axis=1),
                jnp.concatenate([p[:, TILE:] for p in pieces], axis=1),
            )
        )
    return results


def neighbours(even, across, beside):
    return jnp.where(even, across, beside), jnp.where(even, beside, across)


def half_tile(x):
    blank = jnp.zeros((x.shape[0], TILE // 2), x.dtype)
    return jnp.concatenate([blank, x, blank], axis=1)


def padded_columns(source_ref, room_ref, semaphore):
    columns = source_ref.shape[-1]
    copy = pltpu.make_async_copy(source_ref, room_ref.at[:, :, TILE : TILE + columns], semaphore)
    copy.start()
    blank = jnp.zeros(room_ref.shape[:2] + (TILE,), F32)
    room_ref[:, :, :TILE] = blank
    room_ref[:, :, TILE + columns :] = blank
    copy.wait()


def block_of(room_ref, part, block):
    start = pl.multiple_of(block * BLOCK, TILE)
    return room_ref[part, :, pl.ds(start, FRAME0)][:, TILE // 2 : TILE // 2 + FRAME1]


def pack_phase(where_ref, phase_ref, border_ref, core_ref, own_ref, room_ref, semaphore):
    even = where_ref[1] == 0
    padded_columns(phase_ref, room_ref, semaphore)
    own_ref[0] = block_of(room_ref, 0, where_ref[2])
    own_ref[1] = block_of(room_ref, 1, where_ref[2])
    low, high = own_ref[1, :REACH], own_ref[1, ROWS - REACH :]
    for ref, nearest in ((border_ref, jnp.where(even, low, high)), (core_ref, jnp.where(even, high, low))):
        ref[:ROWS] = own_ref[0]
        ref[ROWS:] = nearest


def pack_measured(where_ref, tilts_ref, measured_ref, *refs):
    block_refs, room_ref, semaphore = refs[:GROUP], refs[GROUP], refs[GROUP + 1]
    padded_columns(measured_ref.at[0], room_ref, semaphore)
    lane = lax.broadcasted_iota(jnp.int32, (8, TILE), 1)
    row = lax.broadcasted_iota(jnp.int32, (8, TILE), 0)
    for shift, ref in enumerate(block_refs):
        block = where_ref[2] ^ shift
        ref[0] = block_of(room_ref, 0, block)
        ref[1] = block_of(room_ref, 1, block)
        corner = ref[0, :8, :TILE]
        corner = jnp.where((row == 0) & (lane == 0), tilts_ref[0, 0], corner)
        ref[0, :8, :TILE] = jnp.where((row == 0) & (lane == 1), tilts_ref[0, 1], corner)


def prepare(where_ref, taps_ref, own_ref, turn_ref, into1_ref, into2_ref, out1_ref, out2_ref, band_ref):
    tap_matrices(taps_ref, into1_ref, into2_ref, out1_ref, out2_ref, band_ref)
    for layer in range(2):
        turn_ref[layer, 0], turn_ref[layer, 1] = inside_grid(where_ref, *cos_sin(own_ref[layer]))


def inside_grid(where_ref, *fields):
    count = fields[0].shape[1]
    margin = (count - BLOCK) // 2
    lane = lax.broadcasted_iota(jnp.int32, (1, count), 1)
    there = ((lane >= margin) | (where_ref[2] != 0)) & ((lane < margin + BLOCK) | (where_ref[2] != GROUP - 1))
    return [jnp.where(there, field, 0.0) for field in fields]


def turns(where_ref, across_ref, beside_ref, own_ref, turn0_ref, turn1_ref, total_rows):
    even = where_ref[1] == 0
    first_row = where_ref[0]
    below, above = neighbours(even, across_ref[...], beside_ref[...])
    below = [jnp.where(first_row > 0, x, 0.0) for x in inside_grid(where_ref, *cos_sin(below))]
    above = [jnp.where(first_row + ROWS < total_rows, x, 0.0) for x in inside_grid(where_ref, *cos_sin(above))]
    for part in range(2):
        turn0_ref[part] = half_tile(jnp.concatenate([below[part][:ROWS], own_ref[0, part], above[part][:ROWS]], axis=0))
        turn1_ref[part] = jnp.concatenate([below[part][ROWS:], own_ref[1, part], above[part][ROWS:]], axis=0)


def sweep(where_ref, measured_refs, turn0_ref, turn1_ref, into1_ref, into2_ref, out1_ref, out2_ref, band_ref):
    row = (where_ref[0] - 2 * REACH + lax.broadcasted_iota(jnp.int32, (WIDEST, TILE), 0)).astype(F32)
    column = where_ref[2] * BLOCK - TILE + lax.broadcasted_iota(jnp.int32, (8, FRAME0), 1)
    cos0, sin0, cos1, sin1 = turn0_ref[0], turn0_ref[1], turn1_ref[0], turn1_ref[1]
    waves0 = []
    for measured_ref in measured_refs:
        cos_r, sin_r = cos_sin(measured_ref[0, :1, :1] * row)
        cos_c, sin_c = cos_sin(measured_ref[0, :1, 1:2] * column.astype(F32))
        cos_r, sin_r, cos_c, sin_c = cos_r[:, :1], sin_r[:, :1], cos_c[:1], sin_c[:1]
        left_r, left_i = cos0 * cos_r - sin0 * sin_r, sin0 * cos_r + cos0 * sin_r
        waves0.append((left_r * cos_c - left_i * sin_c, left_r * sin_c + left_i * cos_c))
    fields = column_pass(row_pass(waves0, into1_ref), band_ref, 0, FRAME1 // TILE, 0)
    waves1 = [(cos1 * real - sin1 * imag, cos1 * imag + sin1 * real) for real, imag in fields]
    fields = column_pass(row_pass(waves1, into2_ref), band_ref, 0, FRAME0 // TILE, -1)
    fields = [
        inside_grid(where_ref, real - half_tile(measured_ref[0]), imag - half_tile(measured_ref[1]))
        for (real, imag), measured_ref in zip(fields, measured_refs)
    ]
    fields = row_pass(column_pass(fields, band_ref, 1, FRAME1 // TILE, 0), out1_ref)
    total1 = sum(wave[0] * imag - wave[1] * real for wave, (real, imag) in zip(waves1, fields))
    fields = [(cos1 * real + sin1 * imag, cos1 * imag - sin1 * real) for real, imag in fields]
    fields = row_pass(column_pass(fields, band_ref, 1, BLOCK // TILE, 0), out2_ref)
    middle = slice(TILE, TILE + BLOCK)
    total0 = sum(
        wave[0][:, middle] * imag - wave[1][:, middle] * real for wave, (real, imag) in zip(waves0, fields)
    )
    return total0, total1


def first_angle(
    where_ref, across_ref, beside_ref, own_ref, measured_ref, into1_ref, into2_ref, out1_ref, out2_ref, band_ref,
    turn0_ref, turn1_ref, total0_ref, total1_ref, *, total_rows,
):
    turns(where_ref, across_ref, beside_ref, own_ref, turn0_ref, turn1_ref, total_rows)
    total0_ref[...], total1_ref[...] = sweep(
        where_ref, [measured_ref], turn0_ref, turn1_ref, into1_ref, into2_ref, out1_ref, out2_ref, band_ref
    )


def other_angles(where_ref, *refs):
    measured_refs, (total0_ref, total1_ref), rest = refs[: GROUP - 1], refs[GROUP - 1 : GROUP + 1], refs[GROUP + 1 : -1]
    out_ref = refs[-1]
    term0, term1 = sweep(where_ref, measured_refs, *rest)
    total0, total1 = total0_ref[...] + term0, total1_ref[...] + term1
    total1 = total1[:, TILE // 2 : TILE // 2 + BLOCK]
    for j in range(BLOCK // TILE):
        out_ref[j, :WIDEST] = total0[:, j * TILE : (j + 1) * TILE]
        out_ref[j, WIDEST:] = total1[:, j * TILE : (j + 1) * TILE]


def add_angles(where_ref, tiles_ref, own_ref, border_ref, core_ref):
    even = where_ref[1] == 0
    total = tiles_ref[0]
    for j in range(1, tiles_ref.shape[0]):
        total = total + tiles_ref[j]
    slice0, slice1 = total[:WIDEST], total[WIDEST:]
    own_ref[0] = slice0[ROWS : 2 * ROWS]
    own_ref[1] = slice1[REACH : REACH + ROWS]
    low = jnp.concatenate([slice0[:ROWS], slice1[:REACH]], axis=0)
    high = jnp.concatenate([slice0[2 * ROWS :], slice1[REACH + ROWS :]], axis=0)
    border_ref[...] = jnp.where(even, low, high)
    core_ref[...] = jnp.where(even, high, low)


def add_strips(where_ref, own_ref, across_ref, beside_ref, out_ref):
    below, above = neighbours(where_ref[1] == 0, across_ref[...], beside_ref[...])
    out_ref[0] = own_ref[0] + (below[:ROWS] + above[:ROWS])
    out_ref[1, :REACH] = own_ref[1, :REACH] + below[ROWS:]
    out_ref[1, REACH:] = own_ref[1, REACH:] + above[ROWS:]


def call(kernel, shapes, scalars, arrays, flops, scratch=(), space=pltpu.VMEM):
    moved = sum(a.size * a.dtype.itemsize for a in arrays)
    moved += sum(int(s.size) * s.dtype.itemsize for s in shapes)
    return pl.pallas_call(
        kernel,
        out_shape=shapes,
        in_specs=[pl.BlockSpec(memory_space=pltpu.SMEM)] * len(scalars)
        + [pl.BlockSpec(memory_space=space)] * len(arrays),
        out_specs=[pl.BlockSpec(memory_space=pltpu.VMEM)] * len(shapes),
        scratch_shapes=list(scratch),
        compiler_params=pltpu.CompilerParams(vmem_limit_bytes=VMEM_LIMIT),
        cost_estimate=pl.CostEstimate(flops=flops, bytes_accessed=moved, transcendentals=0),
    )(*scalars, *arrays)


def swaps(pairs):
    return pairs + [(b, a) for a, b in pairs]


def body(total_rows, phase_delay, measured, tilts, fresnel_taps):
    columns = phase_delay.shape[2]
    strips = lax.axis_size("space")
    along = lax.axis_size("angle") // GROUP
    strip = lax.axis_index("space")
    block = lax.axis_index("angle") // along
    where = jnp.stack([strip * ROWS, strip & 1, block]).astype(jnp.int32)
    over_border = swaps([(i, i + 1) for i in range(1, strips - 1, 2)])
    in_chip = swaps([(i, i + 1) for i in range(0, strips, 2)])

    def swapped(shift):
        return [(g * along + i, (g ^ shift) * along + i) for g in range(GROUP) for i in range(along)]

    struct = jax.ShapeDtypeStruct
    room = [pltpu.VMEM((2, ROWS, columns + 2 * TILE), F32), pltpu.SemaphoreType.DMA]
    to_border, to_core, own_phase = call(
        pack_phase,
        [struct((ROWS + REACH, FRAME1), F32)] * 2 + [struct((2, ROWS, FRAME1), F32)],
        [where],
        [phase_delay],
        0,
        room,
        pltpu.HBM,
    )
    beside = lax.ppermute(to_core, "space", in_chip)
    across = lax.ppermute(to_border, "space", over_border)
    blocks = call(
        pack_measured,
        [struct((2, ROWS, FRAME1), F32)] * GROUP,
        [where, tilts],
        [measured],
        0,
        room,
        pltpu.HBM,
    )
    arrived = [lax.ppermute(blocks[shift], "angle", swapped(shift)) for shift in range(1, GROUP)]
    own, *matrices = call(
        prepare,
        [
            struct((2, 2, ROWS, FRAME1), F32),
            struct((4 * WIDE, 2 * WIDEST), BF16),
            struct((4 * ROWS, 4 * WIDE), BF16),
            struct((4 * WIDE, 4 * ROWS), BF16),
            struct((4 * WIDEST, 4 * WIDE), BF16),
            struct((2, 2, 512, 256), BF16),
        ],
        [where, fresnel_taps],
        [own_phase],
        10_000_000,
    )
    turn0, turn1, total0, total1 = call(
        functools.partial(first_angle, total_rows=total_rows),
        [
            struct((2, WIDEST, FRAME0), F32),
            struct((2, WIDE, FRAME1), F32),
            struct((WIDEST, BLOCK), F32),
            struct((WIDE, FRAME1), F32),
        ],
        [where],
        [across, beside, own, blocks[0], *matrices],
        2_000_000_000,
    )
    (tiles,) = call(
        other_angles,
        [struct((BLOCK // TILE, WIDEST + WIDE, TILE), F32)],
        [where],
        [*arrived, total0, total1, turn0, turn1, *matrices],
        6_000_000_000,
    )
    beside_x = [[g * along + i for i in range(along)] for g in range(GROUP)]
    tiles = lax.all_to_all(tiles, "angle", 0, 0, axis_index_groups=beside_x)
    total, to_border, to_core = call(
        add_angles,
        [struct((2, ROWS, TILE), F32)] + [struct((ROWS + REACH, TILE), F32)] * 2,
        [where],
        [tiles],
        0,
    )
    beside = lax.ppermute(to_core, "space", in_chip)
    across = lax.ppermute(to_border, "space", over_border)
    (gradient,) = call(add_strips, [struct((2, ROWS, TILE), F32)], [where], [total, across, beside], 0)
    return gradient


def solution(mesh):
    def step(phase_delay, measured, tilts, fresnel_taps):
        return jax.shard_map(
            functools.partial(body, phase_delay.shape[1]),
            mesh=mesh,
            in_specs=(P(None, "space", None), P("angle", None, "space", None), P("angle", None), P()),
            out_specs=P(None, "space", "angle"),
            check_vma=False,
        )(phase_delay, measured, tilts, fresnel_taps)

    return step
```

```python
import functools

import jax
import jax.numpy as jnp
from jax import lax
from jax.experimental import pallas as pl
from jax.experimental.pallas import tpu as pltpu
from jax.sharding import PartitionSpec as P

TILE = 128
REACH = 16
TAPS = 2 * REACH + 1
ROWS = 32
WIDE = ROWS + 2 * REACH
WIDEST = ROWS + 4 * REACH
F32 = jnp.float32
BF16 = jnp.bfloat16
GROUP = 4
BLOCK = 512
FRAME0 = BLOCK + 2 * TILE
FRAME1 = BLOCK + TILE
VMEM_LIMIT = 32 * 1024 * 1024
PACK_LIMIT = 60 * 1024 * 1024


def split(x):
    high = x.astype(BF16)
    return high, (x - high.astype(F32)).astype(BF16)


def cos_sin(x):
    turns = jnp.round(x * 0.6366197723675814)
    rest = ((x - turns * 1.5703125) - turns * 4.837512969970703125e-4) - turns * 7.54978995489188216e-8
    square = rest * rest
    sine = rest + rest * square * (
        -1.6666654611e-1 + square * (8.3321608736e-3 + square * -1.9515295891e-4)
    )
    cosine = (1.0 - 0.5 * square) + square * square * (
        4.166664568298827e-2 + square * (-1.388731625493765e-3 + square * 2.443315711809948e-5)
    )
    quarter = turns.astype(jnp.int32)
    odd = (quarter & 1) == 1
    cos_part, sin_part = jnp.where(odd, sine, cosine), jnp.where(odd, cosine, sine)
    return (
        jnp.where(((quarter + 1) & 2) == 2, -cos_part, cos_part),
        jnp.where((quarter & 2) == 2, -sin_part, sin_part),
    )


def matmul(a, b):
    return jnp.dot(a, b, preferred_element_type=F32)


def tap_matrices(taps_ref, into1_ref, into2_ref, out1_ref, out2_ref, band_ref):
    lane = lax.broadcasted_iota(jnp.int32, (8, 256), 1)

    def laid(direction, part, start, step):
        out = jnp.zeros((8, 256), F32)
        for tap in range(TAPS):
            out = jnp.where(lane == (start + step * tap) % 256, taps_ref[direction, part, tap], out)
        return out

    def toeplitz(vector, rows):
        full = jnp.broadcast_to(vector[:1], (rows, 256))
        return pltpu.roll(full, 0, 1, stride=1, stride_axis=0)

    def put(ref, index, value):
        high, low = split(value)
        ref[index, 0] = high
        ref[index, 1] = low

    for ref, out_rows, in_rows, last, step, sign in (
        (into1_ref, WIDE, WIDEST, TAPS - 1, -1, 1.0),
        (into2_ref, ROWS, WIDE, TAPS - 1, -1, 1.0),
        (out1_ref, WIDE, ROWS, 1 - TAPS, 1, -1.0),
        (out2_ref, WIDEST, WIDE, 1 - TAPS, 1, -1.0),
    ):
        column = lax.broadcasted_iota(jnp.int32, (out_rows, 256), 1)
        real, imag = laid(0, 0, last, step), laid(0, 1, last, step) * sign
        real_2, imag_2 = laid(0, 0, in_rows + last, step), laid(0, 1, in_rows + last, step) * sign
        first = column < in_rows
        top = jnp.where(first, toeplitz(real, out_rows), -toeplitz(imag_2, out_rows))
        bottom = jnp.where(first, toeplitz(imag, out_rows), toeplitz(real_2, out_rows))
        high, low = split(jnp.concatenate([top, bottom], axis=0)[:, : 2 * in_rows])
        if ref.shape[1] == 2 * in_rows:
            ref[...] = jnp.concatenate([high, low], axis=0)
        else:
            high = high.astype(F32)
            low = low.astype(F32)
            both = jnp.concatenate([high, low], axis=0), jnp.concatenate([high, jnp.zeros_like(low)], axis=0)
            ref[...] = jnp.concatenate(both, axis=1).astype(BF16)
    for index, sign in ((0, 1.0), (1, -1.0)):
        first = 256 - TILE // 2 - REACH
        start, step = (first, 1) if index == 0 else (first + TAPS - 1, -1)
        real = toeplitz(laid(1, 0, start, step), 256)[:, :TILE]
        imag = toeplitz(laid(1, 1, start, step) * sign, 256)[:, :TILE]
        put(
            band_ref,
            index,
            jnp.concatenate(
                [
                    jnp.concatenate([real, imag], axis=1),
                    jnp.concatenate([-imag, real], axis=1),
                ],
                axis=0,
            ),
        )


def row_pass(fields, matrix_ref):
    columns = fields[0][0].shape[1]
    high, low = split(jnp.concatenate([jnp.concatenate(field, axis=0) for field in fields], axis=1))
    matrix = matrix_ref[...]
    count = matrix.shape[0] // 2
    if matrix.shape[1] == high.shape[0]:
        product = matmul(matrix, high)
        total = product[:count] + (product[count:] + matmul(matrix[:count], low))
    else:
        product = matmul(matrix, jnp.concatenate([high, low], axis=0))
        total = product[:count] + product[count:]
    pieces = [total[:, i * columns : (i + 1) * columns] for i in range(len(fields))]
    return [(piece[: count // 2], piece[count // 2 :]) for piece in pieces]


def column_pass(fields, band_ref, index, tiles, first):
    rows = fields[0][0].shape[0]
    have = fields[0][0].shape[1] // TILE
    blank = jnp.zeros((rows, TILE), BF16)

    def stacked(parts):
        def tile(part, j):
            return part[:, j * TILE : (j + 1) * TILE] if 0 <= j < have else blank

        return jnp.concatenate(
            [
                jnp.concatenate([tile(part, first + j + i) for part in field for i in range(2)], axis=1)
                for field in parts
                for j in range(tiles)
            ],
            axis=0,
        )

    levels = [[split(part) for part in field] for field in fields]
    high = stacked([[part[0] for part in field] for field in levels])
    low = stacked([[part[1] for part in field] for field in levels])
    band_high = band_ref[index, 0]
    out = matmul(high, band_high) + (matmul(low, band_high) + matmul(high, band_ref[index, 1]))
    results = []
    for i in range(len(fields)):
        pieces = [out[(i * tiles + j) * rows : (i * tiles + j + 1) * rows] for j in range(tiles)]
        results.append(
            (
                jnp.concatenate([p[:, :TILE] for p in pieces], axis=1),
                jnp.concatenate([p[:, TILE:] for p in pieces], axis=1),
            )
        )
    return results


def neighbours(even, across, beside):
    return jnp.where(even, across, beside), jnp.where(even, beside, across)


def half_tile(x):
    blank = jnp.zeros((x.shape[0], TILE // 2), x.dtype)
    return jnp.concatenate([blank, x, blank], axis=1)


def padded_columns(source_ref, room_ref, semaphore):
    columns = source_ref.shape[-1]
    copy = pltpu.make_async_copy(source_ref, room_ref.at[:, :, TILE : TILE + columns], semaphore)
    copy.start()
    blank = jnp.zeros(room_ref.shape[:2] + (TILE,), F32)
    room_ref[:, :, :TILE] = blank
    room_ref[:, :, TILE + columns :] = blank
    return copy


def block_of(room_ref, part, block):
    start = pl.multiple_of(block * BLOCK, TILE)
    return room_ref[part, :, pl.ds(start, FRAME0)][:, TILE // 2 : TILE // 2 + FRAME1]


def measured_block(where_ref, tilts_ref, room_ref, shift, ref):
    block = where_ref[2] ^ shift
    ref[0] = block_of(room_ref, 0, block)
    ref[1] = block_of(room_ref, 1, block)
    lane = lax.broadcasted_iota(jnp.int32, (8, TILE), 1)
    row = lax.broadcasted_iota(jnp.int32, (8, TILE), 0)
    corner = ref[0, :8, :TILE]
    corner = jnp.where((row == 0) & (lane == 0), tilts_ref[0, 0], corner)
    ref[0, :8, :TILE] = jnp.where((row == 0) & (lane == 1), tilts_ref[0, 1], corner)


def pack(
    where_ref, tilts_ref, phase_ref, measured_ref, border_ref, core_ref, own_ref, far_ref,
    phase_room, measured_room, phase_semaphore, measured_semaphore,
):
    even = where_ref[1] == 0
    phase_copy = padded_columns(phase_ref, phase_room, phase_semaphore)
    measured_copy = padded_columns(measured_ref.at[0], measured_room, measured_semaphore)
    phase_copy.wait()
    own_ref[0] = block_of(phase_room, 0, where_ref[2])
    own_ref[1] = block_of(phase_room, 1, where_ref[2])
    low, high = own_ref[1, :REACH], own_ref[1, ROWS - REACH :]
    for ref, nearest in ((border_ref, jnp.where(even, low, high)), (core_ref, jnp.where(even, high, low))):
        ref[:ROWS] = own_ref[0]
        ref[ROWS:] = nearest
    measured_copy.wait()
    measured_block(where_ref, tilts_ref, measured_room, 2, far_ref)


def prepare(
    where_ref, tilts_ref, taps_ref, own_ref, measured_ref,
    own_block_ref, block1_ref, block3_ref, turn_ref, into1_ref, into2_ref, out1_ref, out2_ref, band_ref,
    room_ref, semaphore,
):
    copy = padded_columns(measured_ref.at[0], room_ref, semaphore)
    tap_matrices(taps_ref, into1_ref, into2_ref, out1_ref, out2_ref, band_ref)
    for layer in range(2):
        turn_ref[layer, 0], turn_ref[layer, 1] = inside_grid(where_ref, *cos_sin(own_ref[layer]))
    copy.wait()
    for shift, ref in ((0, own_block_ref), (1, block1_ref), (3, block3_ref)):
        measured_block(where_ref, tilts_ref, room_ref, shift, ref)


def inside_grid(where_ref, *fields):
    count = fields[0].shape[1]
    margin = (count - BLOCK) // 2
    lane = lax.broadcasted_iota(jnp.int32, (1, count), 1)
    there = ((lane >= margin) | (where_ref[2] != 0)) & ((lane < margin + BLOCK) | (where_ref[2] != GROUP - 1))
    return [jnp.where(there, field, 0.0) for field in fields]


def turns(where_ref, across_ref, beside_ref, own_ref, turn0_ref, turn1_ref, total_rows):
    even = where_ref[1] == 0
    first_row = where_ref[0]
    below, above = neighbours(even, across_ref[...], beside_ref[...])
    below = [jnp.where(first_row > 0, x, 0.0) for x in inside_grid(where_ref, *cos_sin(below))]
    above = [jnp.where(first_row + ROWS < total_rows, x, 0.0) for x in inside_grid(where_ref, *cos_sin(above))]
    for part in range(2):
        turn0_ref[part] = half_tile(jnp.concatenate([below[part][:ROWS], own_ref[0, part], above[part][:ROWS]], axis=0))
        turn1_ref[part] = jnp.concatenate([below[part][ROWS:], own_ref[1, part], above[part][ROWS:]], axis=0)


def sweep(where_ref, measured_refs, turn0_ref, turn1_ref, into1_ref, into2_ref, out1_ref, out2_ref, band_ref):
    row = (where_ref[0] - 2 * REACH + lax.broadcasted_iota(jnp.int32, (WIDEST, TILE), 0)).astype(F32)
    column = where_ref[2] * BLOCK - TILE + lax.broadcasted_iota(jnp.int32, (8, FRAME0), 1)
    cos0, sin0, cos1, sin1 = turn0_ref[0], turn0_ref[1], turn1_ref[0], turn1_ref[1]
    waves0 = []
    for measured_ref in measured_refs:
        cos_r, sin_r = cos_sin(measured_ref[0, :1, :1] * row)
        cos_c, sin_c = cos_sin(measured_ref[0, :1, 1:2] * column.astype(F32))
        cos_r, sin_r, cos_c, sin_c = cos_r[:, :1], sin_r[:, :1], cos_c[:1], sin_c[:1]
        left_r, left_i = cos0 * cos_r - sin0 * sin_r, sin0 * cos_r + cos0 * sin_r
        waves0.append((left_r * cos_c - left_i * sin_c, left_r * sin_c + left_i * cos_c))
    fields = column_pass(row_pass(waves0, into1_ref), band_ref, 0, FRAME1 // TILE, 0)
    waves1 = [(cos1 * real - sin1 * imag, cos1 * imag + sin1 * real) for real, imag in fields]
    fields = column_pass(row_pass(waves1, into2_ref), band_ref, 0, FRAME0 // TILE, -1)
    fields = [
        inside_grid(where_ref, real - half_tile(measured_ref[0]), imag - half_tile(measured_ref[1]))
        for (real, imag), measured_ref in zip(fields, measured_refs)
    ]
    fields = row_pass(column_pass(fields, band_ref, 1, FRAME1 // TILE, 0), out1_ref)
    total1 = sum(wave[0] * imag - wave[1] * real for wave, (real, imag) in zip(waves1, fields))
    fields = [(cos1 * real + sin1 * imag, cos1 * imag - sin1 * real) for real, imag in fields]
    fields = row_pass(column_pass(fields, band_ref, 1, BLOCK // TILE, 0), out2_ref)
    middle = slice(TILE, TILE + BLOCK)
    total0 = sum(
        wave[0][:, middle] * imag - wave[1][:, middle] * real for wave, (real, imag) in zip(waves0, fields)
    )
    return total0, total1


def first_angles(
    where_ref, across_ref, beside_ref, own_ref, near_ref, far_ref, into1_ref, into2_ref, out1_ref, out2_ref, band_ref,
    turn0_ref, turn1_ref, total0_ref, total1_ref, *, total_rows,
):
    turns(where_ref, across_ref, beside_ref, own_ref, turn0_ref, turn1_ref, total_rows)
    total0_ref[...], total1_ref[...] = sweep(
        where_ref, [near_ref, far_ref], turn0_ref, turn1_ref, into1_ref, into2_ref, out1_ref, out2_ref, band_ref
    )


def other_angles(where_ref, near_ref, far_ref, total0_ref, total1_ref, *refs):
    out_ref = refs[-1]
    term0, term1 = sweep(where_ref, [near_ref, far_ref], *refs[:-1])
    total0, total1 = total0_ref[...] + term0, total1_ref[...] + term1
    total1 = total1[:, TILE // 2 : TILE // 2 + BLOCK]
    for j in range(BLOCK // TILE):
        out_ref[j, :WIDEST] = total0[:, j * TILE : (j + 1) * TILE]
        out_ref[j, WIDEST:] = total1[:, j * TILE : (j + 1) * TILE]


def add_angles(where_ref, tiles_ref, own_ref, border_ref, core_ref):
    even = where_ref[1] == 0
    total = tiles_ref[0]
    for j in range(1, tiles_ref.shape[0]):
        total = total + tiles_ref[j]
    slice0, slice1 = total[:WIDEST], total[WIDEST:]
    own_ref[0] = slice0[ROWS : 2 * ROWS]
    own_ref[1] = slice1[REACH : REACH + ROWS]
    low = jnp.concatenate([slice0[:ROWS], slice1[:REACH]], axis=0)
    high = jnp.concatenate([slice0[2 * ROWS :], slice1[REACH + ROWS :]], axis=0)
    border_ref[...] = jnp.where(even, low, high)
    core_ref[...] = jnp.where(even, high, low)


def add_strips(where_ref, own_ref, across_ref, beside_ref, out_ref):
    below, above = neighbours(where_ref[1] == 0, across_ref[...], beside_ref[...])
    out_ref[0] = own_ref[0] + (below[:ROWS] + above[:ROWS])
    out_ref[1, :REACH] = own_ref[1, :REACH] + below[ROWS:]
    out_ref[1, REACH:] = own_ref[1, REACH:] + above[ROWS:]


def call(kernel, shapes, scalars, arrays, flops, scratch=(), in_hbm=0, limit=VMEM_LIMIT):
    moved = sum(a.size * a.dtype.itemsize for a in arrays)
    moved += sum(int(s.size) * s.dtype.itemsize for s in shapes)
    spaces = [pltpu.SMEM] * len(scalars) + [pltpu.VMEM] * (len(arrays) - in_hbm) + [pltpu.HBM] * in_hbm
    return pl.pallas_call(
        kernel,
        out_shape=shapes,
        in_specs=[pl.BlockSpec(memory_space=space) for space in spaces],
        out_specs=[pl.BlockSpec(memory_space=pltpu.VMEM)] * len(shapes),
        scratch_shapes=list(scratch),
        compiler_params=pltpu.CompilerParams(vmem_limit_bytes=limit),
        cost_estimate=pl.CostEstimate(flops=flops, bytes_accessed=moved, transcendentals=0),
    )(*scalars, *arrays)


def swaps(pairs):
    return pairs + [(b, a) for a, b in pairs]


def body(total_rows, phase_delay, measured, tilts, fresnel_taps):
    columns = phase_delay.shape[2]
    strips = lax.axis_size("space")
    along = lax.axis_size("angle") // GROUP
    strip = lax.axis_index("space")
    block = lax.axis_index("angle") // along
    where = jnp.stack([strip * ROWS, strip & 1, block]).astype(jnp.int32)
    over_border = swaps([(i, i + 1) for i in range(1, strips - 1, 2)])
    in_chip = swaps([(i, i + 1) for i in range(0, strips, 2)])

    def swapped(shift):
        return [(g * along + i, (g ^ shift) * along + i) for g in range(GROUP) for i in range(along)]

    struct = jax.ShapeDtypeStruct
    room = pltpu.VMEM((2, ROWS, columns + 2 * TILE), F32)
    measured_struct = struct((2, ROWS, FRAME1), F32)
    to_border, to_core, own_phase, far = call(
        pack,
        [struct((ROWS + REACH, FRAME1), F32)] * 2 + [struct((2, ROWS, FRAME1), F32), measured_struct],
        [where, tilts],
        [phase_delay, measured],
        0,
        [room, room, pltpu.SemaphoreType.DMA, pltpu.SemaphoreType.DMA],
        in_hbm=2,
        limit=PACK_LIMIT,
    )
    far = lax.ppermute(far, "angle", swapped(2))
    beside = lax.ppermute(to_core, "space", in_chip)
    across = lax.ppermute(to_border, "space", over_border)
    near, block1, block3, own, *matrices = call(
        prepare,
        [
            measured_struct,
            measured_struct,
            measured_struct,
            struct((2, 2, ROWS, FRAME1), F32),
            struct((4 * WIDE, 2 * WIDEST), BF16),
            struct((4 * ROWS, 4 * WIDE), BF16),
            struct((4 * WIDE, 4 * ROWS), BF16),
            struct((4 * WIDEST, 4 * WIDE), BF16),
            struct((2, 2, 512, 256), BF16),
        ],
        [where, tilts, fresnel_taps],
        [own_phase, measured],
        10_000_000,
        [room, pltpu.SemaphoreType.DMA],
        in_hbm=1,
    )
    block1 = lax.ppermute(block1, "angle", swapped(1))
    block3 = lax.ppermute(block3, "angle", swapped(3))
    turn0, turn1, total0, total1 = call(
        functools.partial(first_angles, total_rows=total_rows),
        [
            struct((2, WIDEST, FRAME0), F32),
            struct((2, WIDE, FRAME1), F32),
            struct((WIDEST, BLOCK), F32),
            struct((WIDE, FRAME1), F32),
        ],
        [where],
        [across, beside, own, near, far, *matrices],
        4_000_000_000,
    )
    (tiles,) = call(
        other_angles,
        [struct((BLOCK // TILE, WIDEST + WIDE, TILE), F32)],
        [where],
        [block3, block1, total0, total1, turn0, turn1, *matrices],
        4_000_000_000,
    )
    beside_x = [[g * along + i for i in range(along)] for g in range(GROUP)]
    tiles = lax.all_to_all(tiles, "angle", 0, 0, axis_index_groups=beside_x)
    total, to_border, to_core = call(
        add_angles,
        [struct((2, ROWS, TILE), F32)] + [struct((ROWS + REACH, TILE), F32)] * 2,
        [where],
        [tiles],
        0,
    )
    beside = lax.ppermute(to_core, "space", in_chip)
    across = lax.ppermute(to_border, "space", over_border)
    (gradient,) = call(add_strips, [struct((2, ROWS, TILE), F32)], [where], [total, across, beside], 0)
    return gradient


def solution(mesh):
    def step(phase_delay, measured, tilts, fresnel_taps):
        return jax.shard_map(
            functools.partial(body, phase_delay.shape[1]),
            mesh=mesh,
            in_specs=(P(None, "space", None), P("angle", None, "space", None), P("angle", None), P()),
            out_specs=P(None, "space", "angle"),
            check_vma=False,
        )(phase_delay, measured, tilts, fresnel_taps)

    return step
```

```python
import functools

import jax
import jax.numpy as jnp
from jax import lax
from jax.experimental import pallas as pl
from jax.experimental.pallas import tpu as pltpu
from jax.sharding import PartitionSpec as P

TILE = 128
REACH = 16
TAPS = 2 * REACH + 1
ROWS = 32
WIDE = ROWS + 2 * REACH
WIDEST = ROWS + 4 * REACH
F32 = jnp.float32
BF16 = jnp.bfloat16
GROUP = 4
BLOCK = 512
FRAME0 = BLOCK + 2 * TILE
FRAME1 = BLOCK + TILE
VMEM_LIMIT = 32 * 1024 * 1024


def split(x):
    high = x.astype(BF16)
    return high, (x - high.astype(F32)).astype(BF16)


def cos_sin(x):
    turns = jnp.round(x * 0.6366197723675814)
    rest = ((x - turns * 1.5703125) - turns * 4.837512969970703125e-4) - turns * 7.54978995489188216e-8
    square = rest * rest
    sine = rest + rest * square * (
        -1.6666654611e-1 + square * (8.3321608736e-3 + square * -1.9515295891e-4)
    )
    cosine = (1.0 - 0.5 * square) + square * square * (
        4.166664568298827e-2 + square * (-1.388731625493765e-3 + square * 2.443315711809948e-5)
    )
    quarter = turns.astype(jnp.int32)
    odd = (quarter & 1) == 1
    cos_part, sin_part = jnp.where(odd, sine, cosine), jnp.where(odd, cosine, sine)
    return (
        jnp.where(((quarter + 1) & 2) == 2, -cos_part, cos_part),
        jnp.where((quarter & 2) == 2, -sin_part, sin_part),
    )


def matmul(a, b):
    return jnp.dot(a, b, preferred_element_type=F32)


def tap_matrices(taps_ref, into1_ref, into2_ref, out1_ref, out2_ref, band_ref):
    lane = lax.broadcasted_iota(jnp.int32, (8, 256), 1)

    def laid(direction, part, start, step):
        out = jnp.zeros((8, 256), F32)
        for tap in range(TAPS):
            out = jnp.where(lane == (start + step * tap) % 256, taps_ref[direction, part, tap], out)
        return out

    def toeplitz(vector, rows):
        full = jnp.broadcast_to(vector[:1], (rows, 256))
        return pltpu.roll(full, 0, 1, stride=1, stride_axis=0)

    def put(ref, index, value):
        high, low = split(value)
        ref[index, 0] = high
        ref[index, 1] = low

    for ref, out_rows, in_rows, last, step, sign in (
        (into1_ref, WIDE, WIDEST, TAPS - 1, -1, 1.0),
        (into2_ref, ROWS, WIDE, TAPS - 1, -1, 1.0),
        (out1_ref, WIDE, ROWS, 1 - TAPS, 1, -1.0),
        (out2_ref, WIDEST, WIDE, 1 - TAPS, 1, -1.0),
    ):
        column = lax.broadcasted_iota(jnp.int32, (out_rows, 256), 1)
        real, imag = laid(0, 0, last, step), laid(0, 1, last, step) * sign
        real_2, imag_2 = laid(0, 0, in_rows + last, step), laid(0, 1, in_rows + last, step) * sign
        first = column < in_rows
        top = jnp.where(first, toeplitz(real, out_rows), -toeplitz(imag_2, out_rows))
        bottom = jnp.where(first, toeplitz(imag, out_rows), toeplitz(real_2, out_rows))
        high, low = split(jnp.concatenate([top, bottom], axis=0)[:, : 2 * in_rows])
        if ref.shape[1] == 2 * in_rows:
            ref[...] = jnp.concatenate([high, low], axis=0)
        else:
            high = high.astype(F32)
            low = low.astype(F32)
            both = jnp.concatenate([high, low], axis=0), jnp.concatenate([high, jnp.zeros_like(low)], axis=0)
            ref[...] = jnp.concatenate(both, axis=1).astype(BF16)
    for index, sign in ((0, 1.0), (1, -1.0)):
        first = 256 - TILE // 2 - REACH
        start, step = (first, 1) if index == 0 else (first + TAPS - 1, -1)
        real = toeplitz(laid(1, 0, start, step), 256)[:, :TILE]
        imag = toeplitz(laid(1, 1, start, step) * sign, 256)[:, :TILE]
        put(
            band_ref,
            index,
            jnp.concatenate(
                [
                    jnp.concatenate([real, imag], axis=1),
                    jnp.concatenate([-imag, real], axis=1),
                ],
                axis=0,
            ),
        )


def row_pass(fields, matrix_ref):
    columns = fields[0][0].shape[1]
    high, low = split(jnp.concatenate([jnp.concatenate(field, axis=0) for field in fields], axis=1))
    matrix = matrix_ref[...]
    count = matrix.shape[0] // 2
    if matrix.shape[1] == high.shape[0]:
        product = matmul(matrix, high)
        total = product[:count] + (product[count:] + matmul(matrix[:count], low))
    else:
        product = matmul(matrix, jnp.concatenate([high, low], axis=0))
        total = product[:count] + product[count:]
    pieces = [total[:, i * columns : (i + 1) * columns] for i in range(len(fields))]
    return [(piece[: count // 2], piece[count // 2 :]) for piece in pieces]


def column_pass(fields, band_ref, index, tiles, first):
    rows = fields[0][0].shape[0]
    have = fields[0][0].shape[1] // TILE
    blank = jnp.zeros((rows, TILE), BF16)

    def stacked(parts):
        def tile(part, j):
            return part[:, j * TILE : (j + 1) * TILE] if 0 <= j < have else blank

        return jnp.concatenate(
            [
                jnp.concatenate([tile(part, first + j + i) for part in field for i in range(2)], axis=1)
                for field in parts
                for j in range(tiles)
            ],
            axis=0,
        )

    levels = [[split(part) for part in field] for field in fields]
    high = stacked([[part[0] for part in field] for field in levels])
    low = stacked([[part[1] for part in field] for field in levels])
    band_high = band_ref[index, 0]
    out = matmul(high, band_high) + (matmul(low, band_high) + matmul(high, band_ref[index, 1]))
    results = []
    for i in range(len(fields)):
        pieces = [out[(i * tiles + j) * rows : (i * tiles + j + 1) * rows] for j in range(tiles)]
        results.append(
            (
                jnp.concatenate([p[:, :TILE] for p in pieces], axis=1),
                jnp.concatenate([p[:, TILE:] for p in pieces], axis=1),
            )
        )
    return results


def neighbours(even, across, beside):
    return jnp.where(even, across, beside), jnp.where(even, beside, across)


def half_tile(x):
    blank = jnp.zeros((x.shape[0], TILE // 2), x.dtype)
    return jnp.concatenate([blank, x, blank], axis=1)


def padded_columns(source_ref, room_ref, semaphore):
    columns = source_ref.shape[-1]
    copy = pltpu.make_async_copy(source_ref, room_ref.at[:, :, TILE : TILE + columns], semaphore)
    copy.start()
    blank = jnp.zeros(room_ref.shape[:2] + (TILE,), F32)
    room_ref[:, :, :TILE] = blank
    room_ref[:, :, TILE + columns :] = blank
    return copy


def block_of(room_ref, part, block):
    start = pl.multiple_of(block * BLOCK, TILE)
    return room_ref[part, :, pl.ds(start, FRAME0)][:, TILE // 2 : TILE // 2 + FRAME1]


def pack_phase(where_ref, phase_ref, border_ref, core_ref, own_ref, room_ref, semaphore):
    even = where_ref[1] == 0
    padded_columns(phase_ref, room_ref, semaphore).wait()
    low, high = slice(0, REACH), slice(ROWS - REACH, ROWS)
    border_ref[:ROWS] = block_of(room_ref, 0, where_ref[3])
    slice1 = block_of(room_ref, 1, where_ref[3])
    border_ref[ROWS:] = jnp.where(even, slice1[low], slice1[high])
    own_ref[0] = block_of(room_ref, 0, where_ref[2])
    own_ref[1] = block_of(room_ref, 1, where_ref[2])
    core_ref[:ROWS] = own_ref[0]
    core_ref[ROWS:] = jnp.where(even, own_ref[1, high], own_ref[1, low])


def pack_measured(where_ref, tilts_ref, measured_ref, after_ref, *refs):
    block_refs, room_ref, semaphore = refs[:GROUP], refs[GROUP], refs[GROUP + 1]
    padded_columns(measured_ref.at[0], room_ref, semaphore).wait()
    lane = lax.broadcasted_iota(jnp.int32, (8, TILE), 1)
    row = lax.broadcasted_iota(jnp.int32, (8, TILE), 0)
    for shift, ref in enumerate(block_refs):
        block = where_ref[2] ^ shift
        ref[0] = block_of(room_ref, 0, block)
        ref[1] = block_of(room_ref, 1, block)
        corner = ref[0, :8, :TILE]
        corner = jnp.where((row == 0) & (lane == 0), tilts_ref[0, 0], corner)
        ref[0, :8, :TILE] = jnp.where((row == 0) & (lane == 1), tilts_ref[0, 1], corner)


def prepare(where_ref, taps_ref, own_ref, turn_ref, into1_ref, into2_ref, out1_ref, out2_ref, band_ref):
    tap_matrices(taps_ref, into1_ref, into2_ref, out1_ref, out2_ref, band_ref)
    for layer in range(2):
        turn_ref[layer, 0], turn_ref[layer, 1] = inside_grid(where_ref, *cos_sin(own_ref[layer]))


def inside_grid(where_ref, *fields):
    count = fields[0].shape[1]
    margin = (count - BLOCK) // 2
    lane = lax.broadcasted_iota(jnp.int32, (1, count), 1)
    there = ((lane >= margin) | (where_ref[2] != 0)) & ((lane < margin + BLOCK) | (where_ref[2] != GROUP - 1))
    return [jnp.where(there, field, 0.0) for field in fields]


def turns(where_ref, across_ref, beside_ref, own_ref, turn0_ref, turn1_ref, total_rows):
    even = where_ref[1] == 0
    first_row = where_ref[0]
    below, above = neighbours(even, across_ref[...], beside_ref[...])
    below = [jnp.where(first_row > 0, x, 0.0) for x in inside_grid(where_ref, *cos_sin(below))]
    above = [jnp.where(first_row + ROWS < total_rows, x, 0.0) for x in inside_grid(where_ref, *cos_sin(above))]
    for part in range(2):
        turn0_ref[part] = half_tile(jnp.concatenate([below[part][:ROWS], own_ref[0, part], above[part][:ROWS]], axis=0))
        turn1_ref[part] = jnp.concatenate([below[part][ROWS:], own_ref[1, part], above[part][ROWS:]], axis=0)


def sweep(where_ref, measured_refs, turn0_ref, turn1_ref, into1_ref, into2_ref, out1_ref, out2_ref, band_ref):
    row = (where_ref[0] - 2 * REACH + lax.broadcasted_iota(jnp.int32, (WIDEST, TILE), 0)).astype(F32)
    column = where_ref[2] * BLOCK - TILE + lax.broadcasted_iota(jnp.int32, (8, FRAME0), 1)
    cos0, sin0, cos1, sin1 = turn0_ref[0], turn0_ref[1], turn1_ref[0], turn1_ref[1]
    waves0 = []
    for measured_ref in measured_refs:
        cos_r, sin_r = cos_sin(measured_ref[0, :1, :1] * row)
        cos_c, sin_c = cos_sin(measured_ref[0, :1, 1:2] * column.astype(F32))
        cos_r, sin_r, cos_c, sin_c = cos_r[:, :1], sin_r[:, :1], cos_c[:1], sin_c[:1]
        left_r, left_i = cos0 * cos_r - sin0 * sin_r, sin0 * cos_r + cos0 * sin_r
        waves0.append((left_r * cos_c - left_i * sin_c, left_r * sin_c + left_i * cos_c))
    fields = column_pass(row_pass(waves0, into1_ref), band_ref, 0, FRAME1 // TILE, 0)
    waves1 = [(cos1 * real - sin1 * imag, cos1 * imag + sin1 * real) for real, imag in fields]
    fields = column_pass(row_pass(waves1, into2_ref), band_ref, 0, FRAME0 // TILE, -1)
    fields = [
        inside_grid(where_ref, real - half_tile(measured_ref[0]), imag - half_tile(measured_ref[1]))
        for (real, imag), measured_ref in zip(fields, measured_refs)
    ]
    fields = row_pass(column_pass(fields, band_ref, 1, FRAME1 // TILE, 0), out1_ref)
    total1 = sum(wave[0] * imag - wave[1] * real for wave, (real, imag) in zip(waves1, fields))
    fields = [(cos1 * real + sin1 * imag, cos1 * imag - sin1 * real) for real, imag in fields]
    fields = row_pass(column_pass(fields, band_ref, 1, BLOCK // TILE, 0), out2_ref)
    middle = slice(TILE, TILE + BLOCK)
    total0 = sum(
        wave[0][:, middle] * imag - wave[1][:, middle] * real for wave, (real, imag) in zip(waves0, fields)
    )
    return total0, total1


def first_angle(
    where_ref, across_ref, beside_ref, own_ref, measured_ref, into1_ref, into2_ref, out1_ref, out2_ref, band_ref,
    turn0_ref, turn1_ref, total0_ref, total1_ref, *, total_rows,
):
    turns(where_ref, across_ref, beside_ref, own_ref, turn0_ref, turn1_ref, total_rows)
    total0_ref[...], total1_ref[...] = sweep(
        where_ref, [measured_ref], turn0_ref, turn1_ref, into1_ref, into2_ref, out1_ref, out2_ref, band_ref
    )


def next_angle(where_ref, measured_ref, total0_ref, total1_ref, *refs):
    term0, term1 = sweep(where_ref, [measured_ref], *refs[:-2])
    refs[-2][...] = total0_ref[...] + term0
    refs[-1][...] = total1_ref[...] + term1


def last_angles(where_ref, near_ref, far_ref, total0_ref, total1_ref, *refs):
    out_ref = refs[-1]
    term0, term1 = sweep(where_ref, [near_ref, far_ref], *refs[:-1])
    total0, total1 = total0_ref[...] + term0, total1_ref[...] + term1
    total1 = total1[:, TILE // 2 : TILE // 2 + BLOCK]
    for j in range(BLOCK // TILE):
        out_ref[j, :WIDEST] = total0[:, j * TILE : (j + 1) * TILE]
        out_ref[j, WIDEST:] = total1[:, j * TILE : (j + 1) * TILE]


def add_angles(where_ref, tiles_ref, own_ref, border_ref, core_ref):
    even = where_ref[1] == 0
    total = tiles_ref[0]
    for j in range(1, tiles_ref.shape[0]):
        total = total + tiles_ref[j]
    slice0, slice1 = total[:WIDEST], total[WIDEST:]
    own_ref[0] = slice0[ROWS : 2 * ROWS]
    own_ref[1] = slice1[REACH : REACH + ROWS]
    low = jnp.concatenate([slice0[:ROWS], slice1[:REACH]], axis=0)
    high = jnp.concatenate([slice0[2 * ROWS :], slice1[REACH + ROWS :]], axis=0)
    border_ref[...] = jnp.where(even, low, high)
    core_ref[...] = jnp.where(even, high, low)


def add_strips(where_ref, own_ref, across_ref, beside_ref, out_ref):
    below, above = neighbours(where_ref[1] == 0, across_ref[...], beside_ref[...])
    out_ref[0] = own_ref[0] + (below[:ROWS] + above[:ROWS])
    out_ref[1, :REACH] = own_ref[1, :REACH] + below[ROWS:]
    out_ref[1, REACH:] = own_ref[1, REACH:] + above[ROWS:]


def call(kernel, shapes, scalars, arrays, flops, scratch=()):
    moved = sum(a.size * a.dtype.itemsize for a in arrays)
    moved += sum(int(s.size) * s.dtype.itemsize for s in shapes)
    return pl.pallas_call(
        kernel,
        out_shape=shapes,
        in_specs=[pl.BlockSpec(memory_space=pltpu.SMEM)] * len(scalars)
        + [pl.BlockSpec(memory_space=pltpu.VMEM)] * len(arrays),
        out_specs=[pl.BlockSpec(memory_space=pltpu.VMEM)] * len(shapes),
        scratch_shapes=list(scratch),
        compiler_params=pltpu.CompilerParams(vmem_limit_bytes=VMEM_LIMIT),
        cost_estimate=pl.CostEstimate(flops=flops, bytes_accessed=moved, transcendentals=0),
    )(*scalars, *arrays)


def swaps(pairs):
    return pairs + [(b, a) for a, b in pairs]


def body(total_rows, phase_delay, measured, tilts, fresnel_taps):
    columns = phase_delay.shape[2]
    strips = lax.axis_size("space")
    along = lax.axis_size("angle") // GROUP
    strip = lax.axis_index("space")
    block = lax.axis_index("angle") // along
    middle = strips // 2
    far = (strip == middle - 1) | (strip == middle)
    where = jnp.stack([strip * ROWS, strip & 1, block, jnp.where(far, GROUP - 1 - block, block)]).astype(jnp.int32)
    over_border = swaps([(i, i + 1) for i in range(1, strips - 1, 2)])
    in_chip = swaps([(i, i + 1) for i in range(0, strips, 2)])
    over_border_nearest = swaps(
        [
            ((i * GROUP + g) * along + j, ((i + 1) * GROUP + (GROUP - 1 - g if i + 1 == middle else g)) * along + j)
            for i in range(1, strips - 1, 2)
            for g in range(GROUP)
            for j in range(along)
        ]
    )

    def swapped(shift):
        return [(g * along + i, (g ^ shift) * along + i) for g in range(GROUP) for i in range(along)]

    struct = jax.ShapeDtypeStruct
    room = [pltpu.VMEM((2, ROWS, columns + 2 * TILE), F32), pltpu.SemaphoreType.DMA]
    to_border, to_core, own_phase = call(
        pack_phase,
        [struct((ROWS + REACH, FRAME1), F32)] * 2 + [struct((2, ROWS, FRAME1), F32)],
        [where],
        [phase_delay],
        0,
        room,
    )
    beside = lax.ppermute(to_core, "space", in_chip)
    across = lax.ppermute(to_border, ("space", "angle"), over_border_nearest)
    blocks = call(
        pack_measured, [struct((2, ROWS, FRAME1), F32)] * GROUP, [where, tilts], [measured, own_phase], 0, room
    )
    near, block1, block2, block3 = [blocks[0]] + [
        lax.ppermute(blocks[shift], "angle", swapped(shift)) for shift in range(1, GROUP)
    ]
    own, *matrices = call(
        prepare,
        [
            struct((2, 2, ROWS, FRAME1), F32),
            struct((4 * WIDE, 2 * WIDEST), BF16),
            struct((4 * ROWS, 4 * WIDE), BF16),
            struct((4 * WIDE, 4 * ROWS), BF16),
            struct((4 * WIDEST, 4 * WIDE), BF16),
            struct((2, 2, 512, 256), BF16),
        ],
        [where, fresnel_taps],
        [own_phase],
        10_000_000,
    )
    totals = [struct((WIDEST, BLOCK), F32), struct((WIDE, FRAME1), F32)]
    turn0, turn1, total0, total1 = call(
        functools.partial(first_angle, total_rows=total_rows),
        [struct((2, WIDEST, FRAME0), F32), struct((2, WIDE, FRAME1), F32)] + totals,
        [where],
        [across, beside, own, near, *matrices],
        2_000_000_000,
    )
    total0, total1 = call(
        next_angle, totals, [where], [block1, total0, total1, turn0, turn1, *matrices], 2_000_000_000
    )
    (tiles,) = call(
        last_angles,
        [struct((BLOCK // TILE, WIDEST + WIDE, TILE), F32)],
        [where],
        [block2, block3, total0, total1, turn0, turn1, *matrices],
        4_000_000_000,
    )
    beside_x = [[g * along + i for i in range(along)] for g in range(GROUP)]
    tiles = lax.all_to_all(tiles, "angle", 0, 0, axis_index_groups=beside_x)
    total, to_border, to_core = call(
        add_angles,
        [struct((2, ROWS, TILE), F32)] + [struct((ROWS + REACH, TILE), F32)] * 2,
        [where],
        [tiles],
        0,
    )
    beside = lax.ppermute(to_core, "space", in_chip)
    across = lax.ppermute(to_border, "space", over_border)
    (gradient,) = call(add_strips, [struct((2, ROWS, TILE), F32)], [where], [total, across, beside], 0)
    return gradient


def solution(mesh):
    def step(phase_delay, measured, tilts, fresnel_taps):
        return jax.shard_map(
            functools.partial(body, phase_delay.shape[1]),
            mesh=mesh,
            in_specs=(P(None, "space", None), P("angle", None, "space", None), P("angle", None), P()),
            out_specs=P(None, "space", "angle"),
            check_vma=False,
        )(phase_delay, measured, tilts, fresnel_taps)

    return step
```

```python
import functools

import jax
import jax.numpy as jnp
from jax import lax
from jax.experimental import pallas as pl
from jax.experimental.pallas import tpu as pltpu
from jax.sharding import PartitionSpec as P

TILE = 128
REACH = 16
TAPS = 2 * REACH + 1
ROWS = 32
WIDE = ROWS + 2 * REACH
WIDEST = ROWS + 4 * REACH
F32 = jnp.float32
BF16 = jnp.bfloat16
SIDE = 2 * REACH
GROUP = 4
BLOCK = 512
FRAME0 = BLOCK + 2 * TILE
FRAME1 = BLOCK + TILE
SIDES_AT = 2 * ROWS * BLOCK // TILE
TILTS_AT = SIDES_AT + ROWS
MESSAGE = TILTS_AT + 8
VMEM_LIMIT = 32 * 1024 * 1024


def split(x):
    high = x.astype(BF16)
    return high, (x - high.astype(F32)).astype(BF16)


def cos_sin(x):
    turns = jnp.round(x * 0.6366197723675814)
    rest = ((x - turns * 1.5703125) - turns * 4.837512969970703125e-4) - turns * 7.54978995489188216e-8
    square = rest * rest
    sine = rest + rest * square * (
        -1.6666654611e-1 + square * (8.3321608736e-3 + square * -1.9515295891e-4)
    )
    cosine = (1.0 - 0.5 * square) + square * square * (
        4.166664568298827e-2 + square * (-1.388731625493765e-3 + square * 2.443315711809948e-5)
    )
    quarter = turns.astype(jnp.int32)
    odd = (quarter & 1) == 1
    cos_part, sin_part = jnp.where(odd, sine, cosine), jnp.where(odd, cosine, sine)
    return (
        jnp.where(((quarter + 1) & 2) == 2, -cos_part, cos_part),
        jnp.where((quarter & 2) == 2, -sin_part, sin_part),
    )


def matmul(a, b):
    return jnp.dot(a, b, preferred_element_type=F32)


def tap_matrices(taps_ref, into1_ref, into2_ref, out1_ref, out2_ref, band_ref):
    lane = lax.broadcasted_iota(jnp.int32, (8, 256), 1)

    def laid(direction, part, start, step):
        out = jnp.zeros((8, 256), F32)
        for tap in range(TAPS):
            out = jnp.where(lane == (start + step * tap) % 256, taps_ref[direction, part, tap], out)
        return out

    def toeplitz(vector, rows):
        full = jnp.broadcast_to(vector[:1], (rows, 256))
        return pltpu.roll(full, 0, 1, stride=1, stride_axis=0)

    def put(ref, index, value):
        high, low = split(value)
        ref[index, 0] = high
        ref[index, 1] = low

    for ref, out_rows, in_rows, last, step, sign in (
        (into1_ref, WIDE, WIDEST, TAPS - 1, -1, 1.0),
        (into2_ref, ROWS, WIDE, TAPS - 1, -1, 1.0),
        (out1_ref, WIDE, ROWS, 1 - TAPS, 1, -1.0),
        (out2_ref, WIDEST, WIDE, 1 - TAPS, 1, -1.0),
    ):
        column = lax.broadcasted_iota(jnp.int32, (out_rows, 256), 1)
        real, imag = laid(0, 0, last, step), laid(0, 1, last, step) * sign
        real_2, imag_2 = laid(0, 0, in_rows + last, step), laid(0, 1, in_rows + last, step) * sign
        first = column < in_rows
        top = jnp.where(first, toeplitz(real, out_rows), -toeplitz(imag_2, out_rows))
        bottom = jnp.where(first, toeplitz(imag, out_rows), toeplitz(real_2, out_rows))
        high, low = split(jnp.concatenate([top, bottom], axis=0)[:, : 2 * in_rows])
        if ref.shape[1] == 2 * in_rows:
            ref[...] = jnp.concatenate([high, low], axis=0)
        else:
            high = high.astype(F32)
            low = low.astype(F32)
            both = jnp.concatenate([high, low], axis=0), jnp.concatenate([high, jnp.zeros_like(low)], axis=0)
            ref[...] = jnp.concatenate(both, axis=1).astype(BF16)
    for index, sign in ((0, 1.0), (1, -1.0)):
        first = 256 - TILE // 2 - REACH
        start, step = (first, 1) if index == 0 else (first + TAPS - 1, -1)
        real = toeplitz(laid(1, 0, start, step), 256)[:, :TILE]
        imag = toeplitz(laid(1, 1, start, step) * sign, 256)[:, :TILE]
        put(
            band_ref,
            index,
            jnp.concatenate(
                [
                    jnp.concatenate([real, imag], axis=1),
                    jnp.concatenate([-imag, real], axis=1),
                ],
                axis=0,
            ),
        )


def row_pass(fields, matrix_ref):
    columns = fields[0][0].shape[1]
    high, low = split(jnp.concatenate([jnp.concatenate(field, axis=0) for field in fields], axis=1))
    matrix = matrix_ref[...]
    count = matrix.shape[0] // 2
    if matrix.shape[1] == high.shape[0]:
        product = matmul(matrix, high)
        total = product[:count] + (product[count:] + matmul(matrix[:count], low))
    else:
        product = matmul(matrix, jnp.concatenate([high, low], axis=0))
        total = product[:count] + product[count:]
    pieces = [total[:, i * columns : (i + 1) * columns] for i in range(len(fields))]
    return [(piece[: count // 2], piece[count // 2 :]) for piece in pieces]


def column_pass(fields, band_ref, index, tiles, first):
    rows = fields[0][0].shape[0]
    have = fields[0][0].shape[1] // TILE
    blank = jnp.zeros((rows, TILE), BF16)

    def stacked(parts):
        def tile(part, j):
            return part[:, j * TILE : (j + 1) * TILE] if 0 <= j < have else blank

        return jnp.concatenate(
            [
                jnp.concatenate([tile(part, first + j + i) for part in field for i in range(2)], axis=1)
                for field in parts
                for j in range(tiles)
            ],
            axis=0,
        )

    levels = [[split(part) for part in field] for field in fields]
    high = stacked([[part[0] for part in field] for field in levels])
    low = stacked([[part[1] for part in field] for field in levels])
    band_high = band_ref[index, 0]
    out = matmul(high, band_high) + (matmul(low, band_high) + matmul(high, band_ref[index, 1]))
    results = []
    for i in range(len(fields)):
        pieces = [out[(i * tiles + j) * rows : (i * tiles + j + 1) * rows] for j in range(tiles)]
        results.append(
            (
                jnp.concatenate([p[:, :TILE] for p in pieces], axis=1),
                jnp.concatenate([p[:, TILE:] for p in pieces], axis=1),
            )
        )
    return results


def neighbours(even, across, beside):
    return jnp.where(even, across, beside), jnp.where(even, beside, across)


def half_tile(x):
    blank = jnp.zeros((x.shape[0], TILE // 2), x.dtype)
    return jnp.concatenate([blank, x, blank], axis=1)


def padded_columns(source_ref, room_ref, semaphore):
    columns = source_ref.shape[-1]
    copy = pltpu.make_async_copy(source_ref, room_ref.at[:, :, TILE : TILE + columns], semaphore)
    copy.start()
    blank = jnp.zeros(room_ref.shape[:2] + (TILE,), F32)
    room_ref[:, :, :TILE] = blank
    room_ref[:, :, TILE + columns :] = blank
    return copy


def block_of(room_ref, part, block):
    start = pl.multiple_of(block * BLOCK, TILE)
    return room_ref[part, :, pl.ds(start, FRAME0)][:, TILE // 2 : TILE // 2 + FRAME1]


def pack_phase(where_ref, phase_ref, border_ref, core_ref, own_ref, room_ref, semaphore):
    even = where_ref[1] == 0
    padded_columns(phase_ref, room_ref, semaphore).wait()
    low, high = slice(0, REACH), slice(ROWS - REACH, ROWS)
    border_ref[:ROWS] = block_of(room_ref, 0, where_ref[3])
    slice1 = block_of(room_ref, 1, where_ref[3])
    border_ref[ROWS:] = jnp.where(even, slice1[low], slice1[high])
    own_ref[0] = block_of(room_ref, 0, where_ref[2])
    own_ref[1] = block_of(room_ref, 1, where_ref[2])
    core_ref[:ROWS] = own_ref[0]
    core_ref[ROWS:] = jnp.where(even, own_ref[1, high], own_ref[1, low])


def pack_measured(where_ref, tilts_ref, measured_ref, after_ref, *refs):
    block_refs, room_ref, semaphore = refs[:GROUP], refs[GROUP], refs[GROUP + 1]
    padded_columns(measured_ref.at[0], room_ref, semaphore).wait()
    lane = lax.broadcasted_iota(jnp.int32, (ROWS, TILE), 1)
    tilts = jnp.where(lane[:8] == 0, tilts_ref[0, 0], tilts_ref[0, 1])
    for shift, ref in enumerate(block_refs):
        start = (where_ref[2] ^ shift) * BLOCK

        def tile(part, index):
            return room_ref[part, :, pl.ds(pl.multiple_of(start + index * TILE, TILE), TILE)]

        for part in range(2):
            for j in range(BLOCK // TILE):
                ref[pl.ds((part * (BLOCK // TILE) + j) * ROWS, ROWS)] = tile(part, 1 + j)
        sides = [
            pltpu.roll(tile(part, index), SIDE + 2 * SIDE * part, 1)
            for part in range(2)
            for index in (0, 1 + BLOCK // TILE)
        ]
        left, right = jnp.where(lane < SIDE, sides[0], sides[1]), jnp.where(lane < 3 * SIDE, sides[2], sides[3])
        ref[pl.ds(SIDES_AT, ROWS)] = jnp.where(lane < 2 * SIDE, left, right)
        ref[pl.ds(TILTS_AT, 8)] = tilts


def measured_part(ref, part):
    lane = lax.broadcasted_iota(jnp.int32, (ROWS, TILE), 1)
    sides = pltpu.roll(ref[pl.ds(SIDES_AT, ROWS)], 3 * SIDE - 2 * SIDE * part, 1)
    tiles = [ref[pl.ds((part * (BLOCK // TILE) + j) * ROWS, ROWS)] for j in range(BLOCK // TILE)]
    left, right = jnp.where(lane >= TILE - SIDE, sides, 0.0), jnp.where(lane < SIDE, sides, 0.0)
    return jnp.concatenate([left, *tiles, right], axis=1)


def prepare(where_ref, taps_ref, own_ref, turn_ref, into1_ref, into2_ref, out1_ref, out2_ref, band_ref):
    tap_matrices(taps_ref, into1_ref, into2_ref, out1_ref, out2_ref, band_ref)
    for layer in range(2):
        turn_ref[layer, 0], turn_ref[layer, 1] = inside_grid(where_ref, *cos_sin(own_ref[layer]))


def inside_grid(where_ref, *fields):
    count = fields[0].shape[1]
    margin = (count - BLOCK) // 2
    lane = lax.broadcasted_iota(jnp.int32, (1, count), 1)
    there = ((lane >= margin) | (where_ref[2] != 0)) & ((lane < margin + BLOCK) | (where_ref[2] != GROUP - 1))
    return [jnp.where(there, field, 0.0) for field in fields]


def turns(where_ref, across_ref, beside_ref, own_ref, turn0_ref, turn1_ref, total_rows):
    even = where_ref[1] == 0
    first_row = where_ref[0]
    below, above = neighbours(even, across_ref[...], beside_ref[...])
    below = [jnp.where(first_row > 0, x, 0.0) for x in inside_grid(where_ref, *cos_sin(below))]
    above = [jnp.where(first_row + ROWS < total_rows, x, 0.0) for x in inside_grid(where_ref, *cos_sin(above))]
    for part in range(2):
        turn0_ref[part] = half_tile(jnp.concatenate([below[part][:ROWS], own_ref[0, part], above[part][:ROWS]], axis=0))
        turn1_ref[part] = jnp.concatenate([below[part][ROWS:], own_ref[1, part], above[part][ROWS:]], axis=0)


def sweep(where_ref, measured_refs, turn0_ref, turn1_ref, into1_ref, into2_ref, out1_ref, out2_ref, band_ref):
    row = (where_ref[0] - 2 * REACH + lax.broadcasted_iota(jnp.int32, (WIDEST, TILE), 0)).astype(F32)
    column = where_ref[2] * BLOCK - TILE + lax.broadcasted_iota(jnp.int32, (8, FRAME0), 1)
    cos0, sin0, cos1, sin1 = turn0_ref[0], turn0_ref[1], turn1_ref[0], turn1_ref[1]
    waves0 = []
    for measured_ref in measured_refs:
        cos_r, sin_r = cos_sin(measured_ref[TILTS_AT : TILTS_AT + 1, :1] * row)
        cos_c, sin_c = cos_sin(measured_ref[TILTS_AT : TILTS_AT + 1, 1:2] * column.astype(F32))
        cos_r, sin_r, cos_c, sin_c = cos_r[:, :1], sin_r[:, :1], cos_c[:1], sin_c[:1]
        left_r, left_i = cos0 * cos_r - sin0 * sin_r, sin0 * cos_r + cos0 * sin_r
        waves0.append((left_r * cos_c - left_i * sin_c, left_r * sin_c + left_i * cos_c))
    fields = column_pass(row_pass(waves0, into1_ref), band_ref, 0, FRAME1 // TILE, 0)
    waves1 = [(cos1 * real - sin1 * imag, cos1 * imag + sin1 * real) for real, imag in fields]
    fields = column_pass(row_pass(waves1, into2_ref), band_ref, 0, FRAME0 // TILE, -1)
    fields = [
        inside_grid(where_ref, real - measured_part(measured_ref, 0), imag - measured_part(measured_ref, 1))
        for (real, imag), measured_ref in zip(fields, measured_refs)
    ]
    fields = row_pass(column_pass(fields, band_ref, 1, FRAME1 // TILE, 0), out1_ref)
    total1 = sum(wave[0] * imag - wave[1] * real for wave, (real, imag) in zip(waves1, fields))
    fields = [(cos1 * real + sin1 * imag, cos1 * imag - sin1 * real) for real, imag in fields]
    fields = row_pass(column_pass(fields, band_ref, 1, BLOCK // TILE, 0), out2_ref)
    middle = slice(TILE, TILE + BLOCK)
    total0 = sum(
        wave[0][:, middle] * imag - wave[1][:, middle] * real for wave, (real, imag) in zip(waves0, fields)
    )
    return total0, total1


def first_angle(
    where_ref, across_ref, beside_ref, own_ref, measured_ref, into1_ref, into2_ref, out1_ref, out2_ref, band_ref,
    turn0_ref, turn1_ref, total0_ref, total1_ref, *, total_rows,
):
    turns(where_ref, across_ref, beside_ref, own_ref, turn0_ref, turn1_ref, total_rows)
    total0_ref[...], total1_ref[...] = sweep(
        where_ref, [measured_ref], turn0_ref, turn1_ref, into1_ref, into2_ref, out1_ref, out2_ref, band_ref
    )


def next_angle(where_ref, measured_ref, total0_ref, total1_ref, *refs):
    term0, term1 = sweep(where_ref, [measured_ref], *refs[:-2])
    refs[-2][...] = total0_ref[...] + term0
    refs[-1][...] = total1_ref[...] + term1


def last_angles(where_ref, near_ref, far_ref, total0_ref, total1_ref, *refs):
    out_ref = refs[-1]
    term0, term1 = sweep(where_ref, [near_ref, far_ref], *refs[:-1])
    total0, total1 = total0_ref[...] + term0, total1_ref[...] + term1
    total1 = total1[:, TILE // 2 : TILE // 2 + BLOCK]
    for j in range(BLOCK // TILE):
        out_ref[j, :WIDEST] = total0[:, j * TILE : (j + 1) * TILE]
        out_ref[j, WIDEST:] = total1[:, j * TILE : (j + 1) * TILE]


def add_angles(where_ref, tiles_ref, own_ref, border_ref, core_ref):
    even = where_ref[1] == 0
    total = tiles_ref[0]
    for j in range(1, tiles_ref.shape[0]):
        total = total + tiles_ref[j]
    slice0, slice1 = total[:WIDEST], total[WIDEST:]
    own_ref[0] = slice0[ROWS : 2 * ROWS]
    own_ref[1] = slice1[REACH : REACH + ROWS]
    low = jnp.concatenate([slice0[:ROWS], slice1[:REACH]], axis=0)
    high = jnp.concatenate([slice0[2 * ROWS :], slice1[REACH + ROWS :]], axis=0)
    border_ref[...] = jnp.where(even, low, high)
    core_ref[...] = jnp.where(even, high, low)


def add_strips(where_ref, own_ref, across_ref, beside_ref, out_ref):
    below, above = neighbours(where_ref[1] == 0, across_ref[...], beside_ref[...])
    out_ref[0] = own_ref[0] + (below[:ROWS] + above[:ROWS])
    out_ref[1, :REACH] = own_ref[1, :REACH] + below[ROWS:]
    out_ref[1, REACH:] = own_ref[1, REACH:] + above[ROWS:]


def call(kernel, shapes, scalars, arrays, flops, scratch=()):
    moved = sum(a.size * a.dtype.itemsize for a in arrays)
    moved += sum(int(s.size) * s.dtype.itemsize for s in shapes)
    return pl.pallas_call(
        kernel,
        out_shape=shapes,
        in_specs=[pl.BlockSpec(memory_space=pltpu.SMEM)] * len(scalars)
        + [pl.BlockSpec(memory_space=pltpu.VMEM)] * len(arrays),
        out_specs=[pl.BlockSpec(memory_space=pltpu.VMEM)] * len(shapes),
        scratch_shapes=list(scratch),
        compiler_params=pltpu.CompilerParams(vmem_limit_bytes=VMEM_LIMIT),
        cost_estimate=pl.CostEstimate(flops=flops, bytes_accessed=moved, transcendentals=0),
    )(*scalars, *arrays)


def swaps(pairs):
    return pairs + [(b, a) for a, b in pairs]


def body(total_rows, phase_delay, measured, tilts, fresnel_taps):
    columns = phase_delay.shape[2]
    strips = lax.axis_size("space")
    along = lax.axis_size("angle") // GROUP
    strip = lax.axis_index("space")
    block = lax.axis_index("angle") // along
    middle = strips // 2
    far = (strip == middle - 1) | (strip == middle)
    where = jnp.stack([strip * ROWS, strip & 1, block, jnp.where(far, GROUP - 1 - block, block)]).astype(jnp.int32)
    over_border = swaps([(i, i + 1) for i in range(1, strips - 1, 2)])
    in_chip = swaps([(i, i + 1) for i in range(0, strips, 2)])
    over_border_nearest = swaps(
        [
            ((i * GROUP + g) * along + j, ((i + 1) * GROUP + (GROUP - 1 - g if i + 1 == middle else g)) * along + j)
            for i in range(1, strips - 1, 2)
            for g in range(GROUP)
            for j in range(along)
        ]
    )

    def swapped(shift):
        return [(g * along + i, (g ^ shift) * along + i) for g in range(GROUP) for i in range(along)]

    struct = jax.ShapeDtypeStruct
    room = [pltpu.VMEM((2, ROWS, columns + 2 * TILE), F32), pltpu.SemaphoreType.DMA]
    to_border, to_core, own_phase = call(
        pack_phase,
        [struct((ROWS + REACH, FRAME1), F32)] * 2 + [struct((2, ROWS, FRAME1), F32)],
        [where],
        [phase_delay],
        0,
        room,
    )
    beside = lax.ppermute(to_core, "space", in_chip)
    across = lax.ppermute(to_border, ("space", "angle"), over_border_nearest)
    blocks = call(
        pack_measured, [struct((MESSAGE, TILE), F32)] * GROUP, [where, tilts], [measured, own_phase], 0, room
    )
    near, block1, block2, block3 = [blocks[0]] + [
        lax.ppermute(blocks[shift], "angle", swapped(shift)) for shift in range(1, GROUP)
    ]
    own, *matrices = call(
        prepare,
        [
            struct((2, 2, ROWS, FRAME1), F32),
            struct((4 * WIDE, 2 * WIDEST), BF16),
            struct((4 * ROWS, 4 * WIDE), BF16),
            struct((4 * WIDE, 4 * ROWS), BF16),
            struct((4 * WIDEST, 4 * WIDE), BF16),
            struct((2, 2, 512, 256), BF16),
        ],
        [where, fresnel_taps],
        [own_phase],
        10_000_000,
    )
    totals = [struct((WIDEST, BLOCK), F32), struct((WIDE, FRAME1), F32)]
    turn0, turn1, total0, total1 = call(
        functools.partial(first_angle, total_rows=total_rows),
        [struct((2, WIDEST, FRAME0), F32), struct((2, WIDE, FRAME1), F32)] + totals,
        [where],
        [across, beside, own, near, *matrices],
        800_000_000,
    )
    total0, total1 = call(
        next_angle, totals, [where], [block1, total0, total1, turn0, turn1, *matrices], 2_000_000_000
    )
    (tiles,) = call(
        last_angles,
        [struct((BLOCK // TILE, WIDEST + WIDE, TILE), F32)],
        [where],
        [block2, block3, total0, total1, turn0, turn1, *matrices],
        4_000_000_000,
    )
    beside_x = [[g * along + i for i in range(along)] for g in range(GROUP)]
    tiles = lax.all_to_all(tiles, "angle", 0, 0, axis_index_groups=beside_x)
    total, to_border, to_core = call(
        add_angles,
        [struct((2, ROWS, TILE), F32)] + [struct((ROWS + REACH, TILE), F32)] * 2,
        [where],
        [tiles],
        0,
    )
    beside = lax.ppermute(to_core, "space", in_chip)
    across = lax.ppermute(to_border, "space", over_border)
    (gradient,) = call(add_strips, [struct((2, ROWS, TILE), F32)], [where], [total, across, beside], 0)
    return gradient


def solution(mesh):
    def step(phase_delay, measured, tilts, fresnel_taps):
        return jax.shard_map(
            functools.partial(body, phase_delay.shape[1]),
            mesh=mesh,
            in_specs=(P(None, "space", None), P("angle", None, "space", None), P("angle", None), P()),
            out_specs=P(None, "space", "angle"),
            check_vma=False,
        )(phase_delay, measured, tilts, fresnel_taps)

    return step
```

```python
import functools

import jax
import jax.numpy as jnp
from jax import lax
from jax.experimental import pallas as pl
from jax.experimental.pallas import tpu as pltpu
from jax.sharding import PartitionSpec as P

TILE = 128
REACH = 16
TAPS = 2 * REACH + 1
ROWS = 32
WIDE = ROWS + 2 * REACH
WIDEST = ROWS + 4 * REACH
F32 = jnp.float32
BF16 = jnp.bfloat16
SIDE = 2 * REACH
GROUP = 4
BLOCK = 512
FRAME0 = BLOCK + 2 * TILE
FRAME1 = BLOCK + TILE
SIDES_AT = 2 * ROWS * BLOCK // TILE
TILTS_AT = SIDES_AT + ROWS
MESSAGE = TILTS_AT + 8
VMEM_LIMIT = 32 * 1024 * 1024


def split(x):
    high = x.astype(BF16)
    return high, (x - high.astype(F32)).astype(BF16)


def cos_sin(x):
    turns = jnp.round(x * 0.6366197723675814)
    rest = ((x - turns * 1.5703125) - turns * 4.837512969970703125e-4) - turns * 7.54978995489188216e-8
    square = rest * rest
    sine = rest + rest * square * (
        -1.6666654611e-1 + square * (8.3321608736e-3 + square * -1.9515295891e-4)
    )
    cosine = (1.0 - 0.5 * square) + square * square * (
        4.166664568298827e-2 + square * (-1.388731625493765e-3 + square * 2.443315711809948e-5)
    )
    quarter = turns.astype(jnp.int32)
    odd = (quarter & 1) == 1
    cos_part, sin_part = jnp.where(odd, sine, cosine), jnp.where(odd, cosine, sine)
    return (
        jnp.where(((quarter + 1) & 2) == 2, -cos_part, cos_part),
        jnp.where((quarter & 2) == 2, -sin_part, sin_part),
    )


def matmul(a, b):
    return jnp.dot(a, b, preferred_element_type=F32)


def tap_matrices(taps_ref, into1_ref, into2_ref, out1_ref, out2_ref, band_ref):
    lane = lax.broadcasted_iota(jnp.int32, (8, 256), 1)

    def plain(direction, part, step):
        out = jnp.zeros((8, 256), F32)
        for tap in range(TAPS):
            out = jnp.where(lane == step * tap % 256, taps_ref[direction, part, tap], out)
        return out

    base = {
        (direction, part, step): plain(direction, part, step)
        for direction in range(2)
        for part in range(2)
        for step in (1, -1)
    }

    def laid(direction, part, start, step):
        return pltpu.roll(base[direction, part, step], start % 256, 1)

    def toeplitz(vector, rows):
        full = jnp.broadcast_to(vector[:1], (rows, 256))
        return pltpu.roll(full, 0, 1, stride=1, stride_axis=0)

    def put(ref, index, value):
        high, low = split(value)
        ref[index, 0] = high
        ref[index, 1] = low

    for ref, out_rows, in_rows, last, step, sign in (
        (into1_ref, WIDE, WIDEST, TAPS - 1, -1, 1.0),
        (into2_ref, ROWS, WIDE, TAPS - 1, -1, 1.0),
        (out1_ref, WIDE, ROWS, 1 - TAPS, 1, -1.0),
        (out2_ref, WIDEST, WIDE, 1 - TAPS, 1, -1.0),
    ):
        column = lax.broadcasted_iota(jnp.int32, (out_rows, 256), 1)
        real, imag = laid(0, 0, last, step), laid(0, 1, last, step) * sign
        real_2, imag_2 = laid(0, 0, in_rows + last, step), laid(0, 1, in_rows + last, step) * sign
        first = column < in_rows
        top = jnp.where(first, toeplitz(real, out_rows), -toeplitz(imag_2, out_rows))
        bottom = jnp.where(first, toeplitz(imag, out_rows), toeplitz(real_2, out_rows))
        high, low = split(jnp.concatenate([top, bottom], axis=0)[:, : 2 * in_rows])
        if ref.shape[1] == 2 * in_rows:
            ref[...] = jnp.concatenate([high, low], axis=0)
        else:
            high = high.astype(F32)
            low = low.astype(F32)
            both = jnp.concatenate([high, low], axis=0), jnp.concatenate([high, jnp.zeros_like(low)], axis=0)
            ref[...] = jnp.concatenate(both, axis=1).astype(BF16)
    for index, sign in ((0, 1.0), (1, -1.0)):
        first = 256 - TILE // 2 - REACH
        start, step = (first, 1) if index == 0 else (first + TAPS - 1, -1)
        real = toeplitz(laid(1, 0, start, step), 256)[:, :TILE]
        imag = toeplitz(laid(1, 1, start, step) * sign, 256)[:, :TILE]
        put(
            band_ref,
            index,
            jnp.concatenate(
                [
                    jnp.concatenate([real, imag], axis=1),
                    jnp.concatenate([-imag, real], axis=1),
                ],
                axis=0,
            ),
        )


def row_pass(fields, matrix_ref):
    columns = fields[0][0].shape[1]
    high, low = split(jnp.concatenate([jnp.concatenate(field, axis=0) for field in fields], axis=1))
    matrix = matrix_ref[...]
    count = matrix.shape[0] // 2
    if matrix.shape[1] == high.shape[0]:
        product = matmul(matrix, high)
        total = product[:count] + (product[count:] + matmul(matrix[:count], low))
    else:
        product = matmul(matrix, jnp.concatenate([high, low], axis=0))
        total = product[:count] + product[count:]
    pieces = [total[:, i * columns : (i + 1) * columns] for i in range(len(fields))]
    return [(piece[: count // 2], piece[count // 2 :]) for piece in pieces]


def column_pass(fields, band_ref, index, tiles, first):
    rows = fields[0][0].shape[0]
    have = fields[0][0].shape[1] // TILE
    blank = jnp.zeros((rows, TILE), BF16)

    def stacked(parts):
        def tile(part, j):
            return part[:, j * TILE : (j + 1) * TILE] if 0 <= j < have else blank

        return jnp.concatenate(
            [
                jnp.concatenate([tile(part, first + j + i) for part in field for i in range(2)], axis=1)
                for field in parts
                for j in range(tiles)
            ],
            axis=0,
        )

    levels = [[split(part) for part in field] for field in fields]
    high = stacked([[part[0] for part in field] for field in levels])
    low = stacked([[part[1] for part in field] for field in levels])
    band_high = band_ref[index, 0]
    out = matmul(high, band_high) + (matmul(low, band_high) + matmul(high, band_ref[index, 1]))
    results = []
    for i in range(len(fields)):
        pieces = [out[(i * tiles + j) * rows : (i * tiles + j + 1) * rows] for j in range(tiles)]
        results.append(
            (
                jnp.concatenate([p[:, :TILE] for p in pieces], axis=1),
                jnp.concatenate([p[:, TILE:] for p in pieces], axis=1),
            )
        )
    return results


def neighbours(even, across, beside):
    return jnp.where(even, across, beside), jnp.where(even, beside, across)


def half_tile(x):
    blank = jnp.zeros((x.shape[0], TILE // 2), x.dtype)
    return jnp.concatenate([blank, x, blank], axis=1)


def padded_columns(source_ref, room_ref, semaphore):
    columns = source_ref.shape[-1]
    copy = pltpu.make_async_copy(source_ref, room_ref.at[:, :, TILE : TILE + columns], semaphore)
    copy.start()
    blank = jnp.zeros(room_ref.shape[:2] + (TILE,), F32)
    room_ref[:, :, :TILE] = blank
    room_ref[:, :, TILE + columns :] = blank
    return copy


def block_of(room_ref, part, block):
    start = pl.multiple_of(block * BLOCK, TILE)
    return room_ref[part, :, pl.ds(start, FRAME0)][:, TILE // 2 : TILE // 2 + FRAME1]


def pack_phase(where_ref, phase_ref, border_ref, core_ref, own_ref, room_ref, semaphore):
    even = where_ref[1] == 0
    padded_columns(phase_ref, room_ref, semaphore).wait()
    low, high = slice(0, REACH), slice(ROWS - REACH, ROWS)
    border_ref[:ROWS] = block_of(room_ref, 0, where_ref[3])
    slice1 = block_of(room_ref, 1, where_ref[3])
    border_ref[ROWS:] = jnp.where(even, slice1[low], slice1[high])
    own_ref[0] = block_of(room_ref, 0, where_ref[2])
    own_ref[1] = block_of(room_ref, 1, where_ref[2])
    core_ref[:ROWS] = own_ref[0]
    core_ref[ROWS:] = jnp.where(even, own_ref[1, high], own_ref[1, low])


def pack_measured(where_ref, tilts_ref, measured_ref, after_ref, *refs):
    block_refs, room_ref, semaphore = refs[:GROUP], refs[GROUP], refs[GROUP + 1]
    padded_columns(measured_ref.at[0], room_ref, semaphore).wait()
    lane = lax.broadcasted_iota(jnp.int32, (ROWS, TILE), 1)
    tilts = jnp.where(lane[:8] == 0, tilts_ref[0, 0], tilts_ref[0, 1])
    for shift, ref in enumerate(block_refs):
        start = (where_ref[2] ^ shift) * BLOCK

        def tile(part, index):
            return room_ref[part, :, pl.ds(pl.multiple_of(start + index * TILE, TILE), TILE)]

        for part in range(2):
            for j in range(BLOCK // TILE):
                ref[pl.ds((part * (BLOCK // TILE) + j) * ROWS, ROWS)] = tile(part, 1 + j)
        sides = [
            pltpu.roll(tile(part, index), SIDE + 2 * SIDE * part, 1)
            for part in range(2)
            for index in (0, 1 + BLOCK // TILE)
        ]
        left, right = jnp.where(lane < SIDE, sides[0], sides[1]), jnp.where(lane < 3 * SIDE, sides[2], sides[3])
        ref[pl.ds(SIDES_AT, ROWS)] = jnp.where(lane < 2 * SIDE, left, right)
        ref[pl.ds(TILTS_AT, 8)] = tilts


def measured_part(ref, part):
    lane = lax.broadcasted_iota(jnp.int32, (ROWS, TILE), 1)
    sides = pltpu.roll(ref[pl.ds(SIDES_AT, ROWS)], 3 * SIDE - 2 * SIDE * part, 1)
    tiles = [ref[pl.ds((part * (BLOCK // TILE) + j) * ROWS, ROWS)] for j in range(BLOCK // TILE)]
    left, right = jnp.where(lane >= TILE - SIDE, sides, 0.0), jnp.where(lane < SIDE, sides, 0.0)
    return jnp.concatenate([left, *tiles, right], axis=1)


def prepare(where_ref, taps_ref, own_ref, turn_ref, into1_ref, into2_ref, out1_ref, out2_ref, band_ref):
    tap_matrices(taps_ref, into1_ref, into2_ref, out1_ref, out2_ref, band_ref)
    for layer in range(2):
        turn_ref[layer, 0], turn_ref[layer, 1] = inside_grid(where_ref, *cos_sin(own_ref[layer]))


def inside_grid(where_ref, *fields):
    count = fields[0].shape[1]
    margin = (count - BLOCK) // 2
    lane = lax.broadcasted_iota(jnp.int32, (1, count), 1)
    there = ((lane >= margin) | (where_ref[2] != 0)) & ((lane < margin + BLOCK) | (where_ref[2] != GROUP - 1))
    return [jnp.where(there, field, 0.0) for field in fields]


def turns(where_ref, across_ref, beside_ref, own_ref, turn0_ref, turn1_ref, total_rows):
    even = where_ref[1] == 0
    first_row = where_ref[0]
    below, above = neighbours(even, across_ref[...], beside_ref[...])
    below = [jnp.where(first_row > 0, x, 0.0) for x in inside_grid(where_ref, *cos_sin(below))]
    above = [jnp.where(first_row + ROWS < total_rows, x, 0.0) for x in inside_grid(where_ref, *cos_sin(above))]
    for part in range(2):
        turn0_ref[part] = half_tile(jnp.concatenate([below[part][:ROWS], own_ref[0, part], above[part][:ROWS]], axis=0))
        turn1_ref[part] = jnp.concatenate([below[part][ROWS:], own_ref[1, part], above[part][ROWS:]], axis=0)


def sweep(where_ref, measured_refs, turn0_ref, turn1_ref, into1_ref, into2_ref, out1_ref, out2_ref, band_ref):
    row = (where_ref[0] - 2 * REACH + lax.broadcasted_iota(jnp.int32, (WIDEST, TILE), 0)).astype(F32)
    column = where_ref[2] * BLOCK - TILE + lax.broadcasted_iota(jnp.int32, (8, FRAME0), 1)
    cos0, sin0, cos1, sin1 = turn0_ref[0], turn0_ref[1], turn1_ref[0], turn1_ref[1]
    waves0 = []
    for measured_ref in measured_refs:
        cos_r, sin_r = cos_sin(measured_ref[TILTS_AT : TILTS_AT + 1, :1] * row)
        cos_c, sin_c = cos_sin(measured_ref[TILTS_AT : TILTS_AT + 1, 1:2] * column.astype(F32))
        cos_r, sin_r, cos_c, sin_c = cos_r[:, :1], sin_r[:, :1], cos_c[:1], sin_c[:1]
        left_r, left_i = cos0 * cos_r - sin0 * sin_r, sin0 * cos_r + cos0 * sin_r
        waves0.append((left_r * cos_c - left_i * sin_c, left_r * sin_c + left_i * cos_c))
    fields = column_pass(row_pass(waves0, into1_ref), band_ref, 0, FRAME1 // TILE, 0)
    waves1 = [(cos1 * real - sin1 * imag, cos1 * imag + sin1 * real) for real, imag in fields]
    fields = column_pass(row_pass(waves1, into2_ref), band_ref, 0, FRAME0 // TILE, -1)
    fields = [
        inside_grid(where_ref, real - measured_part(measured_ref, 0), imag - measured_part(measured_ref, 1))
        for (real, imag), measured_ref in zip(fields, measured_refs)
    ]
    fields = row_pass(column_pass(fields, band_ref, 1, FRAME1 // TILE, 0), out1_ref)
    total1 = sum(wave[0] * imag - wave[1] * real for wave, (real, imag) in zip(waves1, fields))
    fields = [(cos1 * real + sin1 * imag, cos1 * imag - sin1 * real) for real, imag in fields]
    fields = row_pass(column_pass(fields, band_ref, 1, BLOCK // TILE, 0), out2_ref)
    middle = slice(TILE, TILE + BLOCK)
    total0 = sum(
        wave[0][:, middle] * imag - wave[1][:, middle] * real for wave, (real, imag) in zip(waves0, fields)
    )
    return total0, total1


def first_angle(
    where_ref, across_ref, beside_ref, own_ref, measured_ref, into1_ref, into2_ref, out1_ref, out2_ref, band_ref,
    turn0_ref, turn1_ref, total0_ref, total1_ref, *, total_rows,
):
    turns(where_ref, across_ref, beside_ref, own_ref, turn0_ref, turn1_ref, total_rows)
    total0_ref[...], total1_ref[...] = sweep(
        where_ref, [measured_ref], turn0_ref, turn1_ref, into1_ref, into2_ref, out1_ref, out2_ref, band_ref
    )


def next_angles(where_ref, near_ref, far_ref, total0_ref, total1_ref, *refs):
    term0, term1 = sweep(where_ref, [near_ref, far_ref], *refs[:-2])
    refs[-2][...] = total0_ref[...] + term0
    refs[-1][...] = total1_ref[...] + term1


def last_angle(where_ref, measured_ref, total0_ref, total1_ref, *refs):
    own_ref, border_ref, core_ref = refs[-3:]
    term0, term1 = sweep(where_ref, [measured_ref], *refs[:-3])
    slice0, slice1 = total0_ref[...] + term0, total1_ref[...] + term1
    slice1 = slice1[:, TILE // 2 : TILE // 2 + BLOCK]
    for j in range(BLOCK // TILE):
        own_ref[j, :ROWS] = slice0[ROWS : 2 * ROWS, j * TILE : (j + 1) * TILE]
        own_ref[j, ROWS:] = slice1[REACH : REACH + ROWS, j * TILE : (j + 1) * TILE]
    even = where_ref[1] == 0
    low = jnp.concatenate([slice0[:ROWS], slice1[:REACH]], axis=0)
    high = jnp.concatenate([slice0[2 * ROWS :], slice1[REACH + ROWS :]], axis=0)
    border_ref[...] = jnp.where(even, low, high)
    core_ref[...] = jnp.where(even, high, low)


def add_strips(where_ref, own_ref, across_ref, beside_ref, out_ref):
    below, above = neighbours(where_ref[1] == 0, across_ref[...], beside_ref[...])
    for j in range(BLOCK // TILE):
        tile = slice(j * TILE, (j + 1) * TILE)
        out_ref[j, :ROWS] = own_ref[j, :ROWS] + (below[:ROWS, tile] + above[:ROWS, tile])
        out_ref[j, ROWS : ROWS + REACH] = own_ref[j, ROWS : ROWS + REACH] + below[ROWS:, tile]
        out_ref[j, ROWS + REACH :] = own_ref[j, ROWS + REACH :] + above[ROWS:, tile]


def call(kernel, shapes, scalars, arrays, flops, scratch=()):
    moved = sum(a.size * a.dtype.itemsize for a in arrays)
    moved += sum(int(s.size) * s.dtype.itemsize for s in shapes)
    return pl.pallas_call(
        kernel,
        out_shape=shapes,
        in_specs=[pl.BlockSpec(memory_space=pltpu.SMEM)] * len(scalars)
        + [pl.BlockSpec(memory_space=pltpu.VMEM)] * len(arrays),
        out_specs=[pl.BlockSpec(memory_space=pltpu.VMEM)] * len(shapes),
        scratch_shapes=list(scratch),
        compiler_params=pltpu.CompilerParams(vmem_limit_bytes=VMEM_LIMIT),
        cost_estimate=pl.CostEstimate(flops=flops, bytes_accessed=moved, transcendentals=0),
    )(*scalars, *arrays)


def swaps(pairs):
    return pairs + [(b, a) for a, b in pairs]


def body(total_rows, phase_delay, measured, tilts, fresnel_taps):
    columns = phase_delay.shape[2]
    strips = lax.axis_size("space")
    along = lax.axis_size("angle") // GROUP
    strip = lax.axis_index("space")
    block = lax.axis_index("angle") // along
    middle = strips // 2
    far = (strip == middle - 1) | (strip == middle)
    where = jnp.stack([strip * ROWS, strip & 1, block, jnp.where(far, GROUP - 1 - block, block)]).astype(jnp.int32)
    over_border = swaps([(i, i + 1) for i in range(1, strips - 1, 2)])
    in_chip = swaps([(i, i + 1) for i in range(0, strips, 2)])
    over_border_nearest = swaps(
        [
            ((i * GROUP + g) * along + j, ((i + 1) * GROUP + (GROUP - 1 - g if i + 1 == middle else g)) * along + j)
            for i in range(1, strips - 1, 2)
            for g in range(GROUP)
            for j in range(along)
        ]
    )

    def swapped(shift):
        return [(g * along + i, (g ^ shift) * along + i) for g in range(GROUP) for i in range(along)]

    struct = jax.ShapeDtypeStruct
    room = [pltpu.VMEM((2, ROWS, columns + 2 * TILE), F32), pltpu.SemaphoreType.DMA]
    to_border, to_core, own_phase = call(
        pack_phase,
        [struct((ROWS + REACH, FRAME1), F32)] * 2 + [struct((2, ROWS, FRAME1), F32)],
        [where],
        [phase_delay],
        0,
        room,
    )
    beside = lax.ppermute(to_core, "space", in_chip)
    across = lax.ppermute(to_border, ("space", "angle"), over_border_nearest)
    blocks = call(
        pack_measured, [struct((MESSAGE, TILE), F32)] * GROUP, [where, tilts], [measured, own_phase], 0, room
    )
    near, block1, block2, block3 = [blocks[0]] + [
        lax.ppermute(blocks[shift], "angle", swapped(shift)) for shift in range(1, GROUP)
    ]
    own, *matrices = call(
        prepare,
        [
            struct((2, 2, ROWS, FRAME1), F32),
            struct((4 * WIDE, 2 * WIDEST), BF16),
            struct((4 * ROWS, 4 * WIDE), BF16),
            struct((4 * WIDE, 4 * ROWS), BF16),
            struct((4 * WIDEST, 4 * WIDE), BF16),
            struct((2, 2, 512, 256), BF16),
        ],
        [where, fresnel_taps],
        [own_phase],
        10_000_000,
    )
    totals = [struct((WIDEST, BLOCK), F32), struct((WIDE, FRAME1), F32)]
    turn0, turn1, total0, total1 = call(
        functools.partial(first_angle, total_rows=total_rows),
        [struct((2, WIDEST, FRAME0), F32), struct((2, WIDE, FRAME1), F32)] + totals,
        [where],
        [across, beside, own, near, *matrices],
        800_000_000,
    )
    total0, total1 = call(
        next_angles, totals, [where], [block1, block2, total0, total1, turn0, turn1, *matrices], 4_000_000_000
    )
    tiles_struct = struct((BLOCK // TILE, 2 * ROWS, TILE), F32)
    tiles, to_border, to_core = call(
        last_angle,
        [tiles_struct] + [struct((ROWS + REACH, BLOCK), F32)] * 2,
        [where],
        [block3, total0, total1, turn0, turn1, *matrices],
        2_000_000_000,
    )
    beside = lax.ppermute(to_core, "space", in_chip)
    across = lax.ppermute(to_border, "space", over_border)
    (tiles,) = call(add_strips, [tiles_struct], [where], [tiles, across, beside], 0)
    beside_x = [[g * along + i for i in range(along)] for g in range(GROUP)]
    tiles = lax.all_to_all(tiles, "angle", 0, 0, axis_index_groups=beside_x)
    return jnp.sum(tiles, axis=0).reshape(2, ROWS, TILE)


def solution(mesh):
    def step(phase_delay, measured, tilts, fresnel_taps):
        return jax.shard_map(
            functools.partial(body, phase_delay.shape[1]),
            mesh=mesh,
            in_specs=(P(None, "space", None), P("angle", None, "space", None), P("angle", None), P()),
            out_specs=P(None, "space", "angle"),
            check_vma=False,
        )(phase_delay, measured, tilts, fresnel_taps)

    return step
```

```python
import functools

import jax
import jax.numpy as jnp
from jax import lax
from jax.experimental import pallas as pl
from jax.experimental.pallas import tpu as pltpu
from jax.sharding import PartitionSpec as P

TILE = 128
REACH = 16
TAPS = 2 * REACH + 1
ROWS = 32
WIDE = ROWS + 2 * REACH
WIDEST = ROWS + 4 * REACH
F32 = jnp.float32
BF16 = jnp.bfloat16
SIDE = 2 * REACH
GROUP = 4
BLOCK = 512
FRAME0 = BLOCK + 2 * TILE
FRAME1 = BLOCK + TILE
SIDES_AT = 2 * ROWS * BLOCK // TILE
TILTS_AT = SIDES_AT + ROWS
MESSAGE = TILTS_AT + 8
VMEM_LIMIT = 32 * 1024 * 1024


def split(x):
    high = x.astype(BF16)
    return high, (x - high.astype(F32)).astype(BF16)


def cos_sin(x):
    turns = jnp.round(x * 0.6366197723675814)
    rest = ((x - turns * 1.5703125) - turns * 4.837512969970703125e-4) - turns * 7.54978995489188216e-8
    square = rest * rest
    sine = rest + rest * square * (
        -1.6666654611e-1 + square * (8.3321608736e-3 + square * -1.9515295891e-4)
    )
    cosine = (1.0 - 0.5 * square) + square * square * (
        4.166664568298827e-2 + square * (-1.388731625493765e-3 + square * 2.443315711809948e-5)
    )
    quarter = turns.astype(jnp.int32)
    odd = (quarter & 1) == 1
    cos_part, sin_part = jnp.where(odd, sine, cosine), jnp.where(odd, cosine, sine)
    return (
        jnp.where(((quarter + 1) & 2) == 2, -cos_part, cos_part),
        jnp.where((quarter & 2) == 2, -sin_part, sin_part),
    )


def matmul(a, b):
    return jnp.dot(a, b, preferred_element_type=F32)


def tap_matrices(taps_ref, into1_ref, into2_ref, out1_ref, out2_ref, band_ref):
    lane = lax.broadcasted_iota(jnp.int32, (8, 256), 1)

    def laid(direction, part, start, step):
        out = jnp.zeros((8, 256), F32)
        for tap in range(TAPS):
            out = jnp.where(lane == (start + step * tap) % 256, taps_ref[direction, part, tap], out)
        return out

    def toeplitz(vector, rows):
        full = jnp.broadcast_to(vector[:1], (rows, 256))
        return pltpu.roll(full, 0, 1, stride=1, stride_axis=0)

    def put(ref, index, value):
        high, low = split(value)
        ref[index, 0] = high
        ref[index, 1] = low

    for ref, out_rows, in_rows, last, step, sign in (
        (into1_ref, WIDE, WIDEST, TAPS - 1, -1, 1.0),
        (into2_ref, ROWS, WIDE, TAPS - 1, -1, 1.0),
        (out1_ref, WIDE, ROWS, 1 - TAPS, 1, -1.0),
        (out2_ref, WIDEST, WIDE, 1 - TAPS, 1, -1.0),
    ):
        column = lax.broadcasted_iota(jnp.int32, (out_rows, 256), 1)
        real, imag = laid(0, 0, last, step), laid(0, 1, last, step) * sign
        real_2, imag_2 = laid(0, 0, in_rows + last, step), laid(0, 1, in_rows + last, step) * sign
        first = column < in_rows
        top = jnp.where(first, toeplitz(real, out_rows), -toeplitz(imag_2, out_rows))
        bottom = jnp.where(first, toeplitz(imag, out_rows), toeplitz(real_2, out_rows))
        high, low = split(jnp.concatenate([top, bottom], axis=0)[:, : 2 * in_rows])
        if ref.shape[1] == 2 * in_rows:
            ref[...] = jnp.concatenate([high, low], axis=0)
        else:
            high = high.astype(F32)
            low = low.astype(F32)
            both = jnp.concatenate([high, low], axis=0), jnp.concatenate([high, jnp.zeros_like(low)], axis=0)
            ref[...] = jnp.concatenate(both, axis=1).astype(BF16)
    for index, sign in ((0, 1.0), (1, -1.0)):
        first = 256 - TILE // 2 - REACH
        start, step = (first, 1) if index == 0 else (first + TAPS - 1, -1)
        real = toeplitz(laid(1, 0, start, step), 256)[:, :TILE]
        imag = toeplitz(laid(1, 1, start, step) * sign, 256)[:, :TILE]
        put(
            band_ref,
            index,
            jnp.concatenate(
                [
                    jnp.concatenate([real, imag], axis=1),
                    jnp.concatenate([-imag, real], axis=1),
                ],
                axis=0,
            ),
        )


def row_pass(fields, matrix_ref):
    columns = fields[0][0].shape[1]
    high, low = split(jnp.concatenate([jnp.concatenate(field, axis=0) for field in fields], axis=1))
    matrix = matrix_ref[...]
    count = matrix.shape[0] // 2
    if matrix.shape[1] == high.shape[0]:
        product = matmul(matrix, high)
        total = product[:count] + (product[count:] + matmul(matrix[:count], low))
    else:
        product = matmul(matrix, jnp.concatenate([high, low], axis=0))
        total = product[:count] + product[count:]
    pieces = [total[:, i * columns : (i + 1) * columns] for i in range(len(fields))]
    return [(piece[: count // 2], piece[count // 2 :]) for piece in pieces]


def column_pass(fields, band_ref, index, tiles, first):
    rows = fields[0][0].shape[0]
    have = fields[0][0].shape[1] // TILE
    blank = jnp.zeros((rows, TILE), BF16)

    def stacked(parts):
        def tile(part, j):
            return part[:, j * TILE : (j + 1) * TILE] if 0 <= j < have else blank

        return jnp.concatenate(
            [
                jnp.concatenate([tile(part, first + j + i) for part in field for i in range(2)], axis=1)
                for field in parts
                for j in range(tiles)
            ],
            axis=0,
        )

    levels = [[split(part) for part in field] for field in fields]
    high = stacked([[part[0] for part in field] for field in levels])
    low = stacked([[part[1] for part in field] for field in levels])
    band_high = band_ref[index, 0]
    out = matmul(high, band_high) + (matmul(low, band_high) + matmul(high, band_ref[index, 1]))
    results = []
    for i in range(len(fields)):
        pieces = [out[(i * tiles + j) * rows : (i * tiles + j + 1) * rows] for j in range(tiles)]
        results.append(
            (
                jnp.concatenate([p[:, :TILE] for p in pieces], axis=1),
                jnp.concatenate([p[:, TILE:] for p in pieces], axis=1),
            )
        )
    return results


def neighbours(even, across, beside):
    return jnp.where(even, across, beside), jnp.where(even, beside, across)


def half_tile(x):
    blank = jnp.zeros((x.shape[0], TILE // 2), x.dtype)
    return jnp.concatenate([blank, x, blank], axis=1)


def padded_columns(source_ref, room_ref, semaphore):
    columns = source_ref.shape[-1]
    copy = pltpu.make_async_copy(source_ref, room_ref.at[:, :, TILE : TILE + columns], semaphore)
    copy.start()
    blank = jnp.zeros(room_ref.shape[:2] + (TILE,), F32)
    room_ref[:, :, :TILE] = blank
    room_ref[:, :, TILE + columns :] = blank
    return copy


def block_of(room_ref, part, block):
    start = pl.multiple_of(block * BLOCK, TILE)
    return room_ref[part, :, pl.ds(start, FRAME0)][:, TILE // 2 : TILE // 2 + FRAME1]


def pack_phase(where_ref, phase_ref, border_ref, core_ref, own_ref, room_ref, semaphore):
    even = where_ref[1] == 0
    padded_columns(phase_ref, room_ref, semaphore).wait()
    low, high = slice(0, REACH), slice(ROWS - REACH, ROWS)
    border_ref[:ROWS] = block_of(room_ref, 0, where_ref[3])
    slice1 = block_of(room_ref, 1, where_ref[3])
    border_ref[ROWS:] = jnp.where(even, slice1[low], slice1[high])
    own_ref[0] = block_of(room_ref, 0, where_ref[2])
    own_ref[1] = block_of(room_ref, 1, where_ref[2])
    core_ref[:ROWS] = own_ref[0]
    core_ref[ROWS:] = jnp.where(even, own_ref[1, high], own_ref[1, low])


def pack_measured(where_ref, tilts_ref, measured_ref, after_ref, *refs):
    block_refs, room_ref, semaphore = refs[:GROUP], refs[GROUP], refs[GROUP + 1]
    padded_columns(measured_ref.at[0], room_ref, semaphore).wait()
    lane = lax.broadcasted_iota(jnp.int32, (ROWS, TILE), 1)
    tilts = jnp.where(lane[:8] == 0, tilts_ref[0, 0], tilts_ref[0, 1])
    for shift, ref in enumerate(block_refs):
        start = (where_ref[2] ^ shift) * BLOCK

        def tile(part, index):
            return room_ref[part, :, pl.ds(pl.multiple_of(start + index * TILE, TILE), TILE)]

        for part in range(2):
            for j in range(BLOCK // TILE):
                ref[pl.ds((part * (BLOCK // TILE) + j) * ROWS, ROWS)] = tile(part, 1 + j)
        sides = [
            pltpu.roll(tile(part, index), SIDE + 2 * SIDE * part, 1)
            for part in range(2)
            for index in (0, 1 + BLOCK // TILE)
        ]
        left, right = jnp.where(lane < SIDE, sides[0], sides[1]), jnp.where(lane < 3 * SIDE, sides[2], sides[3])
        ref[pl.ds(SIDES_AT, ROWS)] = jnp.where(lane < 2 * SIDE, left, right)
        ref[pl.ds(TILTS_AT, 8)] = tilts


def measured_part(ref, part):
    lane = lax.broadcasted_iota(jnp.int32, (ROWS, TILE), 1)
    sides = pltpu.roll(ref[pl.ds(SIDES_AT, ROWS)], 3 * SIDE - 2 * SIDE * part, 1)
    tiles = [ref[pl.ds((part * (BLOCK // TILE) + j) * ROWS, ROWS)] for j in range(BLOCK // TILE)]
    left, right = jnp.where(lane >= TILE - SIDE, sides, 0.0), jnp.where(lane < SIDE, sides, 0.0)
    return jnp.concatenate([left, *tiles, right], axis=1)


def prepare(where_ref, taps_ref, own_ref, turn_ref, into1_ref, into2_ref, out1_ref, out2_ref, band_ref):
    tap_matrices(taps_ref, into1_ref, into2_ref, out1_ref, out2_ref, band_ref)
    for layer in range(2):
        turn_ref[layer, 0], turn_ref[layer, 1] = inside_grid(where_ref, *cos_sin(own_ref[layer]))


def inside_grid(where_ref, *fields):
    count = fields[0].shape[1]
    margin = (count - BLOCK) // 2
    lane = lax.broadcasted_iota(jnp.int32, (1, count), 1)
    there = ((lane >= margin) | (where_ref[2] != 0)) & ((lane < margin + BLOCK) | (where_ref[2] != GROUP - 1))
    return [jnp.where(there, field, 0.0) for field in fields]


def turns(where_ref, across_ref, beside_ref, own_ref, turn0_ref, turn1_ref, total_rows):
    even = where_ref[1] == 0
    first_row = where_ref[0]
    below, above = neighbours(even, across_ref[...], beside_ref[...])
    below = [jnp.where(first_row > 0, x, 0.0) for x in inside_grid(where_ref, *cos_sin(below))]
    above = [jnp.where(first_row + ROWS < total_rows, x, 0.0) for x in inside_grid(where_ref, *cos_sin(above))]
    for part in range(2):
        turn0_ref[part] = half_tile(jnp.concatenate([below[part][:ROWS], own_ref[0, part], above[part][:ROWS]], axis=0))
        turn1_ref[part] = jnp.concatenate([below[part][ROWS:], own_ref[1, part], above[part][ROWS:]], axis=0)


def sweep(where_ref, measured_refs, turn0_ref, turn1_ref, into1_ref, into2_ref, out1_ref, out2_ref, band_ref):
    row = (where_ref[0] - 2 * REACH + lax.broadcasted_iota(jnp.int32, (WIDEST, TILE), 0)).astype(F32)
    column = where_ref[2] * BLOCK - TILE + lax.broadcasted_iota(jnp.int32, (8, FRAME0), 1)
    cos0, sin0, cos1, sin1 = turn0_ref[0], turn0_ref[1], turn1_ref[0], turn1_ref[1]
    waves0 = []
    for measured_ref in measured_refs:
        cos_r, sin_r = cos_sin(measured_ref[TILTS_AT : TILTS_AT + 1, :1] * row)
        cos_c, sin_c = cos_sin(measured_ref[TILTS_AT : TILTS_AT + 1, 1:2] * column.astype(F32))
        cos_r, sin_r, cos_c, sin_c = cos_r[:, :1], sin_r[:, :1], cos_c[:1], sin_c[:1]
        left_r, left_i = cos0 * cos_r - sin0 * sin_r, sin0 * cos_r + cos0 * sin_r
        waves0.append((left_r * cos_c - left_i * sin_c, left_r * sin_c + left_i * cos_c))
    fields = column_pass(row_pass(waves0, into1_ref), band_ref, 0, FRAME1 // TILE, 0)
    waves1 = [(cos1 * real - sin1 * imag, cos1 * imag + sin1 * real) for real, imag in fields]
    fields = column_pass(row_pass(waves1, into2_ref), band_ref, 0, FRAME0 // TILE, -1)
    fields = [
        inside_grid(where_ref, real - measured_part(measured_ref, 0), imag - measured_part(measured_ref, 1))
        for (real, imag), measured_ref in zip(fields, measured_refs)
    ]
    fields = row_pass(column_pass(fields, band_ref, 1, FRAME1 // TILE, 0), out1_ref)
    total1 = sum(wave[0] * imag - wave[1] * real for wave, (real, imag) in zip(waves1, fields))
    fields = [(cos1 * real + sin1 * imag, cos1 * imag - sin1 * real) for real, imag in fields]
    fields = row_pass(column_pass(fields, band_ref, 1, BLOCK // TILE, 0), out2_ref)
    middle = slice(TILE, TILE + BLOCK)
    total0 = sum(
        wave[0][:, middle] * imag - wave[1][:, middle] * real for wave, (real, imag) in zip(waves0, fields)
    )
    return total0, total1


def first_angles(
    where_ref, across_ref, beside_ref, own_ref, near_ref, far_ref, into1_ref, into2_ref, out1_ref, out2_ref, band_ref,
    turn0_ref, turn1_ref, total0_ref, total1_ref, *, total_rows,
):
    turns(where_ref, across_ref, beside_ref, own_ref, turn0_ref, turn1_ref, total_rows)
    total0_ref[...], total1_ref[...] = sweep(
        where_ref, [near_ref, far_ref], turn0_ref, turn1_ref, into1_ref, into2_ref, out1_ref, out2_ref, band_ref
    )


def last_angles(where_ref, near_ref, far_ref, total0_ref, total1_ref, *refs):
    own_ref, border_ref, core_ref = refs[-3:]
    term0, term1 = sweep(where_ref, [near_ref, far_ref], *refs[:-3])
    slice0, slice1 = total0_ref[...] + term0, total1_ref[...] + term1
    slice1 = slice1[:, TILE // 2 : TILE // 2 + BLOCK]
    for j in range(BLOCK // TILE):
        own_ref[j, :ROWS] = slice0[ROWS : 2 * ROWS, j * TILE : (j + 1) * TILE]
        own_ref[j, ROWS:] = slice1[REACH : REACH + ROWS, j * TILE : (j + 1) * TILE]
    even = where_ref[1] == 0
    low = jnp.concatenate([slice0[:ROWS], slice1[:REACH]], axis=0)
    high = jnp.concatenate([slice0[2 * ROWS :], slice1[REACH + ROWS :]], axis=0)
    border_ref[...] = jnp.where(even, low, high)
    core_ref[...] = jnp.where(even, high, low)


def add_strips(where_ref, own_ref, across_ref, beside_ref, out_ref):
    below, above = neighbours(where_ref[1] == 0, across_ref[...], beside_ref[...])
    for j in range(BLOCK // TILE):
        tile = slice(j * TILE, (j + 1) * TILE)
        out_ref[j, :ROWS] = own_ref[j, :ROWS] + (below[:ROWS, tile] + above[:ROWS, tile])
        out_ref[j, ROWS : ROWS + REACH] = own_ref[j, ROWS : ROWS + REACH] + below[ROWS:, tile]
        out_ref[j, ROWS + REACH :] = own_ref[j, ROWS + REACH :] + above[ROWS:, tile]


def call(kernel, shapes, scalars, arrays, flops, scratch=()):
    moved = sum(a.size * a.dtype.itemsize for a in arrays)
    moved += sum(int(s.size) * s.dtype.itemsize for s in shapes)
    return pl.pallas_call(
        kernel,
        out_shape=shapes,
        in_specs=[pl.BlockSpec(memory_space=pltpu.SMEM)] * len(scalars)
        + [pl.BlockSpec(memory_space=pltpu.VMEM)] * len(arrays),
        out_specs=[pl.BlockSpec(memory_space=pltpu.VMEM)] * len(shapes),
        scratch_shapes=list(scratch),
        compiler_params=pltpu.CompilerParams(vmem_limit_bytes=VMEM_LIMIT),
        cost_estimate=pl.CostEstimate(flops=flops, bytes_accessed=moved, transcendentals=0),
    )(*scalars, *arrays)


def swaps(pairs):
    return pairs + [(b, a) for a, b in pairs]


def body(total_rows, phase_delay, measured, tilts, fresnel_taps):
    columns = phase_delay.shape[2]
    strips = lax.axis_size("space")
    along = lax.axis_size("angle") // GROUP
    strip = lax.axis_index("space")
    block = lax.axis_index("angle") // along
    middle = strips // 2
    far = (strip == middle - 1) | (strip == middle)
    where = jnp.stack([strip * ROWS, strip & 1, block, jnp.where(far, GROUP - 1 - block, block)]).astype(jnp.int32)
    over_border = swaps([(i, i + 1) for i in range(1, strips - 1, 2)])
    in_chip = swaps([(i, i + 1) for i in range(0, strips, 2)])
    over_border_nearest = swaps(
        [
            ((i * GROUP + g) * along + j, ((i + 1) * GROUP + (GROUP - 1 - g if i + 1 == middle else g)) * along + j)
            for i in range(1, strips - 1, 2)
            for g in range(GROUP)
            for j in range(along)
        ]
    )

    def swapped(shift):
        return [(g * along + i, (g ^ shift) * along + i) for g in range(GROUP) for i in range(along)]

    struct = jax.ShapeDtypeStruct
    room = [pltpu.VMEM((2, ROWS, columns + 2 * TILE), F32), pltpu.SemaphoreType.DMA]
    to_border, to_core, own_phase = call(
        pack_phase,
        [struct((ROWS + REACH, FRAME1), F32)] * 2 + [struct((2, ROWS, FRAME1), F32)],
        [where],
        [phase_delay],
        0,
        room,
    )
    beside = lax.ppermute(to_core, "space", in_chip)
    across = lax.ppermute(to_border, ("space", "angle"), over_border_nearest)
    blocks = call(
        pack_measured, [struct((MESSAGE, TILE), F32)] * GROUP, [where, tilts], [measured, own_phase], 0, room
    )
    near, block1, block2, block3 = [blocks[0]] + [
        lax.ppermute(blocks[shift], "angle", swapped(shift)) for shift in range(1, GROUP)
    ]
    own, *matrices = call(
        prepare,
        [
            struct((2, 2, ROWS, FRAME1), F32),
            struct((4 * WIDE, 2 * WIDEST), BF16),
            struct((4 * ROWS, 4 * WIDE), BF16),
            struct((4 * WIDE, 4 * ROWS), BF16),
            struct((4 * WIDEST, 4 * WIDE), BF16),
            struct((2, 2, 512, 256), BF16),
        ],
        [where, fresnel_taps],
        [own_phase],
        10_000_000,
    )
    totals = [struct((WIDEST, BLOCK), F32), struct((WIDE, FRAME1), F32)]
    turn0, turn1, total0, total1 = call(
        functools.partial(first_angles, total_rows=total_rows),
        [struct((2, WIDEST, FRAME0), F32), struct((2, WIDE, FRAME1), F32)] + totals,
        [where],
        [across, beside, own, near, block2, *matrices],
        800_000_000,
    )
    tiles_struct = struct((BLOCK // TILE, 2 * ROWS, TILE), F32)
    tiles, to_border, to_core = call(
        last_angles,
        [tiles_struct] + [struct((ROWS + REACH, BLOCK), F32)] * 2,
        [where],
        [block3, block1, total0, total1, turn0, turn1, *matrices],
        4_000_000_000,
    )
    beside = lax.ppermute(to_core, "space", in_chip)
    across = lax.ppermute(to_border, "space", over_border)
    (tiles,) = call(add_strips, [tiles_struct], [where], [tiles, across, beside], 0)
    beside_x = [[g * along + i for i in range(along)] for g in range(GROUP)]
    tiles = lax.all_to_all(tiles, "angle", 0, 0, axis_index_groups=beside_x)
    return jnp.sum(tiles, axis=0).reshape(2, ROWS, TILE)


def solution(mesh):
    def step(phase_delay, measured, tilts, fresnel_taps):
        return jax.shard_map(
            functools.partial(body, phase_delay.shape[1]),
            mesh=mesh,
            in_specs=(P(None, "space", None), P("angle", None, "space", None), P("angle", None), P()),
            out_specs=P(None, "space", "angle"),
            check_vma=False,
        )(phase_delay, measured, tilts, fresnel_taps)

    return step
```

```python
import functools

import jax
import jax.numpy as jnp
from jax import lax
from jax.experimental import pallas as pl
from jax.experimental.pallas import tpu as pltpu
from jax.sharding import PartitionSpec as P

TILE = 128
REACH = 16
TAPS = 2 * REACH + 1
ROWS = 32
WIDE = ROWS + 2 * REACH
WIDEST = ROWS + 4 * REACH
F32 = jnp.float32
BF16 = jnp.bfloat16
SIDE = 2 * REACH
GROUP = 4
BLOCK = 512
FRAME0 = BLOCK + 2 * TILE
FRAME1 = BLOCK + TILE
SIDES_AT = 2 * ROWS * BLOCK // TILE
TILTS_AT = SIDES_AT + ROWS
MESSAGE = TILTS_AT + 8
VMEM_LIMIT = 32 * 1024 * 1024
PACK_LIMIT = 55259136


def split(x):
    high = x.astype(BF16)
    return high, (x - high.astype(F32)).astype(BF16)


def cos_sin(x):
    turns = jnp.round(x * 0.6366197723675814)
    rest = ((x - turns * 1.5703125) - turns * 4.837512969970703125e-4) - turns * 7.54978995489188216e-8
    square = rest * rest
    sine = rest + rest * square * (
        -1.6666654611e-1 + square * (8.3321608736e-3 + square * -1.9515295891e-4)
    )
    cosine = (1.0 - 0.5 * square) + square * square * (
        4.166664568298827e-2 + square * (-1.388731625493765e-3 + square * 2.443315711809948e-5)
    )
    quarter = turns.astype(jnp.int32)
    odd = (quarter & 1) == 1
    cos_part, sin_part = jnp.where(odd, sine, cosine), jnp.where(odd, cosine, sine)
    return (
        jnp.where(((quarter + 1) & 2) == 2, -cos_part, cos_part),
        jnp.where((quarter & 2) == 2, -sin_part, sin_part),
    )


def matmul(a, b):
    return jnp.dot(a, b, preferred_element_type=F32)


def tap_matrices(taps_ref, into1_ref, into2_ref, out1_ref, out2_ref, band_ref):
    lane = lax.broadcasted_iota(jnp.int32, (8, 256), 1)

    def laid(direction, part, start, step):
        out = jnp.zeros((8, 256), F32)
        for tap in range(TAPS):
            out = jnp.where(lane == (start + step * tap) % 256, taps_ref[direction, part, tap], out)
        return out

    def toeplitz(vector, rows):
        full = jnp.broadcast_to(vector[:1], (rows, 256))
        return pltpu.roll(full, 0, 1, stride=1, stride_axis=0)

    def put(ref, index, value):
        high, low = split(value)
        ref[index, 0] = high
        ref[index, 1] = low

    for ref, out_rows, in_rows, last, step, sign in (
        (into1_ref, WIDE, WIDEST, TAPS - 1, -1, 1.0),
        (into2_ref, ROWS, WIDE, TAPS - 1, -1, 1.0),
        (out1_ref, WIDE, ROWS, 1 - TAPS, 1, -1.0),
        (out2_ref, WIDEST, WIDE, 1 - TAPS, 1, -1.0),
    ):
        column = lax.broadcasted_iota(jnp.int32, (out_rows, 256), 1)
        real, imag = laid(0, 0, last, step), laid(0, 1, last, step) * sign
        real_2, imag_2 = laid(0, 0, in_rows + last, step), laid(0, 1, in_rows + last, step) * sign
        first = column < in_rows
        top = jnp.where(first, toeplitz(real, out_rows), -toeplitz(imag_2, out_rows))
        bottom = jnp.where(first, toeplitz(imag, out_rows), toeplitz(real_2, out_rows))
        high, low = split(jnp.concatenate([top, bottom], axis=0)[:, : 2 * in_rows])
        if ref.shape[1] == 2 * in_rows:
            ref[...] = jnp.concatenate([high, low], axis=0)
        else:
            high = high.astype(F32)
            low = low.astype(F32)
            both = jnp.concatenate([high, low], axis=0), jnp.concatenate([high, jnp.zeros_like(low)], axis=0)
            ref[...] = jnp.concatenate(both, axis=1).astype(BF16)
    for index, sign in ((0, 1.0), (1, -1.0)):
        first = 256 - TILE // 2 - REACH
        start, step = (first, 1) if index == 0 else (first + TAPS - 1, -1)
        real = toeplitz(laid(1, 0, start, step), 256)[:, :TILE]
        imag = toeplitz(laid(1, 1, start, step) * sign, 256)[:, :TILE]
        put(
            band_ref,
            index,
            jnp.concatenate(
                [
                    jnp.concatenate([real, imag], axis=1),
                    jnp.concatenate([-imag, real], axis=1),
                ],
                axis=0,
            ),
        )


def row_pass(fields, matrix_ref):
    columns = fields[0][0].shape[1]
    high, low = split(jnp.concatenate([jnp.concatenate(field, axis=0) for field in fields], axis=1))
    matrix = matrix_ref[...]
    count = matrix.shape[0] // 2
    if matrix.shape[1] == high.shape[0]:
        product = matmul(matrix, high)
        total = product[:count] + (product[count:] + matmul(matrix[:count], low))
    else:
        product = matmul(matrix, jnp.concatenate([high, low], axis=0))
        total = product[:count] + product[count:]
    pieces = [total[:, i * columns : (i + 1) * columns] for i in range(len(fields))]
    return [(piece[: count // 2], piece[count // 2 :]) for piece in pieces]


def column_pass(fields, band_ref, index, tiles, first):
    rows = fields[0][0].shape[0]
    have = fields[0][0].shape[1] // TILE
    blank = jnp.zeros((rows, TILE), BF16)

    def stacked(parts):
        def tile(part, j):
            return part[:, j * TILE : (j + 1) * TILE] if 0 <= j < have else blank

        return jnp.concatenate(
            [
                jnp.concatenate([tile(part, first + j + i) for part in field for i in range(2)], axis=1)
                for field in parts
                for j in range(tiles)
            ],
            axis=0,
        )

    levels = [[split(part) for part in field] for field in fields]
    high = stacked([[part[0] for part in field] for field in levels])
    low = stacked([[part[1] for part in field] for field in levels])
    band_high = band_ref[index, 0]
    out = matmul(high, band_high) + (matmul(low, band_high) + matmul(high, band_ref[index, 1]))
    results = []
    for i in range(len(fields)):
        pieces = [out[(i * tiles + j) * rows : (i * tiles + j + 1) * rows] for j in range(tiles)]
        results.append(
            (
                jnp.concatenate([p[:, :TILE] for p in pieces], axis=1),
                jnp.concatenate([p[:, TILE:] for p in pieces], axis=1),
            )
        )
    return results


def neighbours(even, across, beside):
    return jnp.where(even, across, beside), jnp.where(even, beside, across)


def half_tile(x):
    blank = jnp.zeros((x.shape[0], TILE // 2), x.dtype)
    return jnp.concatenate([blank, x, blank], axis=1)


def block_tile(ref, part, block, index):
    columns = ref.shape[-1]
    start = jnp.clip(block * BLOCK + index * TILE, 0, columns - TILE)
    tile = ref[part, :, pl.ds(pl.multiple_of(start, TILE), TILE)]
    if index < 0:
        return jnp.where(block == 0, 0.0, tile)
    if index * TILE >= BLOCK:
        return jnp.where(block == GROUP - 1, 0.0, tile)
    return tile


def phase_block(ref, part, block):
    tiles = [block_tile(ref, part, block, index) for index in range(-1, BLOCK // TILE + 1)]
    return jnp.concatenate(tiles, axis=1)[:, TILE // 2 : TILE // 2 + FRAME1]


def pack(where_ref, tilts_ref, phase_hbm, measured_hbm, border_ref, core_ref, own_ref, *refs):
    block_refs, (phase_ref, plane_ref, semaphores) = refs[:GROUP], refs[GROUP:]
    copies = []
    for source, room in ((phase_hbm, phase_ref), (measured_hbm.at[0], plane_ref)):
        for part in range(2):
            copies.append(pltpu.make_async_copy(source.at[part], room.at[part], semaphores.at[len(copies)]))
            copies[-1].start()
    copies[0].wait()
    copies[1].wait()
    even = where_ref[1] == 0
    low, high = slice(0, REACH), slice(ROWS - REACH, ROWS)
    border_ref[:ROWS] = phase_block(phase_ref, 0, where_ref[3])
    slice1 = phase_block(phase_ref, 1, where_ref[3])
    border_ref[ROWS:] = jnp.where(even, slice1[low], slice1[high])
    own_ref[0] = phase_block(phase_ref, 0, where_ref[2])
    own_ref[1] = phase_block(phase_ref, 1, where_ref[2])
    core_ref[:ROWS] = own_ref[0]
    core_ref[ROWS:] = jnp.where(even, own_ref[1, high], own_ref[1, low])
    lane = lax.broadcasted_iota(jnp.int32, (ROWS, TILE), 1)
    tilts = jnp.where(lane[:8] == 0, tilts_ref[0, 0], tilts_ref[0, 1])
    copies[2].wait()
    copies[3].wait()
    for shift, ref in enumerate(block_refs):
        block = where_ref[2] ^ shift
        for part in range(2):
            for j in range(BLOCK // TILE):
                ref[pl.ds((part * (BLOCK // TILE) + j) * ROWS, ROWS)] = block_tile(plane_ref, part, block, j)
        sides = [
            pltpu.roll(block_tile(plane_ref, part, block, index), SIDE + 2 * SIDE * part, 1)
            for part in range(2)
            for index in (-1, BLOCK // TILE)
        ]
        left, right = jnp.where(lane < SIDE, sides[0], sides[1]), jnp.where(lane < 3 * SIDE, sides[2], sides[3])
        ref[pl.ds(SIDES_AT, ROWS)] = jnp.where(lane < 2 * SIDE, left, right)
        ref[pl.ds(TILTS_AT, 8)] = tilts


def measured_part(ref, part):
    lane = lax.broadcasted_iota(jnp.int32, (ROWS, TILE), 1)
    sides = pltpu.roll(ref[pl.ds(SIDES_AT, ROWS)], 3 * SIDE - 2 * SIDE * part, 1)
    tiles = [ref[pl.ds((part * (BLOCK // TILE) + j) * ROWS, ROWS)] for j in range(BLOCK // TILE)]
    left, right = jnp.where(lane >= TILE - SIDE, sides, 0.0), jnp.where(lane < SIDE, sides, 0.0)
    return jnp.concatenate([left, *tiles, right], axis=1)


def prepare(where_ref, taps_ref, own_ref, turn_ref, into1_ref, into2_ref, out1_ref, out2_ref, band_ref):
    tap_matrices(taps_ref, into1_ref, into2_ref, out1_ref, out2_ref, band_ref)
    for layer in range(2):
        turn_ref[layer, 0], turn_ref[layer, 1] = inside_grid(where_ref, *cos_sin(own_ref[layer]))


def inside_grid(where_ref, *fields):
    count = fields[0].shape[1]
    margin = (count - BLOCK) // 2
    lane = lax.broadcasted_iota(jnp.int32, (1, count), 1)
    there = ((lane >= margin) | (where_ref[2] != 0)) & ((lane < margin + BLOCK) | (where_ref[2] != GROUP - 1))
    return [jnp.where(there, field, 0.0) for field in fields]


def turns(where_ref, across_ref, beside_ref, own_ref, turn0_ref, turn1_ref, total_rows):
    even = where_ref[1] == 0
    first_row = where_ref[0]
    below, above = neighbours(even, across_ref[...], beside_ref[...])
    below = [jnp.where(first_row > 0, x, 0.0) for x in inside_grid(where_ref, *cos_sin(below))]
    above = [jnp.where(first_row + ROWS < total_rows, x, 0.0) for x in inside_grid(where_ref, *cos_sin(above))]
    for part in range(2):
        turn0_ref[part] = half_tile(jnp.concatenate([below[part][:ROWS], own_ref[0, part], above[part][:ROWS]], axis=0))
        turn1_ref[part] = jnp.concatenate([below[part][ROWS:], own_ref[1, part], above[part][ROWS:]], axis=0)


def sweep(where_ref, measured_refs, turn0_ref, turn1_ref, into1_ref, into2_ref, out1_ref, out2_ref, band_ref):
    row = (where_ref[0] - 2 * REACH + lax.broadcasted_iota(jnp.int32, (WIDEST, TILE), 0)).astype(F32)
    column = where_ref[2] * BLOCK - TILE + lax.broadcasted_iota(jnp.int32, (8, FRAME0), 1)
    cos0, sin0, cos1, sin1 = turn0_ref[0], turn0_ref[1], turn1_ref[0], turn1_ref[1]
    waves0 = []
    for measured_ref in measured_refs:
        cos_r, sin_r = cos_sin(measured_ref[TILTS_AT : TILTS_AT + 1, :1] * row)
        cos_c, sin_c = cos_sin(measured_ref[TILTS_AT : TILTS_AT + 1, 1:2] * column.astype(F32))
        cos_r, sin_r, cos_c, sin_c = cos_r[:, :1], sin_r[:, :1], cos_c[:1], sin_c[:1]
        left_r, left_i = cos0 * cos_r - sin0 * sin_r, sin0 * cos_r + cos0 * sin_r
        waves0.append((left_r * cos_c - left_i * sin_c, left_r * sin_c + left_i * cos_c))
    fields = column_pass(row_pass(waves0, into1_ref), band_ref, 0, FRAME1 // TILE, 0)
    waves1 = [(cos1 * real - sin1 * imag, cos1 * imag + sin1 * real) for real, imag in fields]
    fields = column_pass(row_pass(waves1, into2_ref), band_ref, 0, FRAME0 // TILE, -1)
    fields = [
        inside_grid(where_ref, real - measured_part(measured_ref, 0), imag - measured_part(measured_ref, 1))
        for (real, imag), measured_ref in zip(fields, measured_refs)
    ]
    fields = row_pass(column_pass(fields, band_ref, 1, FRAME1 // TILE, 0), out1_ref)
    total1 = sum(wave[0] * imag - wave[1] * real for wave, (real, imag) in zip(waves1, fields))
    fields = [(cos1 * real + sin1 * imag, cos1 * imag - sin1 * real) for real, imag in fields]
    fields = row_pass(column_pass(fields, band_ref, 1, BLOCK // TILE, 0), out2_ref)
    middle = slice(TILE, TILE + BLOCK)
    total0 = sum(
        wave[0][:, middle] * imag - wave[1][:, middle] * real for wave, (real, imag) in zip(waves0, fields)
    )
    return total0, total1


def first_angles(
    where_ref, across_ref, beside_ref, own_ref, near_ref, far_ref, into1_ref, into2_ref, out1_ref, out2_ref, band_ref,
    turn0_ref, turn1_ref, total0_ref, total1_ref, *, total_rows,
):
    turns(where_ref, across_ref, beside_ref, own_ref, turn0_ref, turn1_ref, total_rows)
    total0_ref[...], total1_ref[...] = sweep(
        where_ref, [near_ref, far_ref], turn0_ref, turn1_ref, into1_ref, into2_ref, out1_ref, out2_ref, band_ref
    )


def last_angles(where_ref, near_ref, far_ref, total0_ref, total1_ref, *refs):
    own_ref, border_ref, core_ref = refs[-3:]
    term0, term1 = sweep(where_ref, [near_ref, far_ref], *refs[:-3])
    slice0, slice1 = total0_ref[...] + term0, total1_ref[...] + term1
    slice1 = slice1[:, TILE // 2 : TILE // 2 + BLOCK]
    for j in range(BLOCK // TILE):
        own_ref[j, :ROWS] = slice0[ROWS : 2 * ROWS, j * TILE : (j + 1) * TILE]
        own_ref[j, ROWS:] = slice1[REACH : REACH + ROWS, j * TILE : (j + 1) * TILE]
    even = where_ref[1] == 0
    low = jnp.concatenate([slice0[:ROWS], slice1[:REACH]], axis=0)
    high = jnp.concatenate([slice0[2 * ROWS :], slice1[REACH + ROWS :]], axis=0)
    border_ref[...] = jnp.where(even, low, high)
    core_ref[...] = jnp.where(even, high, low)


def add_strips(where_ref, own_ref, across_ref, beside_ref, out_ref):
    below, above = neighbours(where_ref[1] == 0, across_ref[...], beside_ref[...])
    for j in range(BLOCK // TILE):
        tile = slice(j * TILE, (j + 1) * TILE)
        out_ref[j, :ROWS] = own_ref[j, :ROWS] + (below[:ROWS, tile] + above[:ROWS, tile])
        out_ref[j, ROWS : ROWS + REACH] = own_ref[j, ROWS : ROWS + REACH] + below[ROWS:, tile]
        out_ref[j, ROWS + REACH :] = own_ref[j, ROWS + REACH :] + above[ROWS:, tile]


def call(kernel, shapes, scalars, arrays, flops, scratch=(), space=pltpu.VMEM, limit=VMEM_LIMIT):
    moved = sum(a.size * a.dtype.itemsize for a in arrays)
    moved += sum(int(s.size) * s.dtype.itemsize for s in shapes)
    return pl.pallas_call(
        kernel,
        out_shape=shapes,
        in_specs=[pl.BlockSpec(memory_space=pltpu.SMEM)] * len(scalars)
        + [pl.BlockSpec(memory_space=space)] * len(arrays),
        out_specs=[pl.BlockSpec(memory_space=pltpu.VMEM)] * len(shapes),
        scratch_shapes=list(scratch),
        compiler_params=pltpu.CompilerParams(vmem_limit_bytes=limit),
        cost_estimate=pl.CostEstimate(flops=flops, bytes_accessed=moved, transcendentals=0),
    )(*scalars, *arrays)


def swaps(pairs):
    return pairs + [(b, a) for a, b in pairs]


def body(total_rows, phase_delay, measured, tilts, fresnel_taps):
    columns = phase_delay.shape[2]
    strips = lax.axis_size("space")
    along = lax.axis_size("angle") // GROUP
    strip = lax.axis_index("space")
    block = lax.axis_index("angle") // along
    middle = strips // 2
    far = (strip == middle - 1) | (strip == middle)
    where = jnp.stack([strip * ROWS, strip & 1, block, jnp.where(far, GROUP - 1 - block, block)]).astype(jnp.int32)
    over_border = swaps([(i, i + 1) for i in range(1, strips - 1, 2)])
    in_chip = swaps([(i, i + 1) for i in range(0, strips, 2)])
    over_border_nearest = swaps(
        [
            ((i * GROUP + g) * along + j, ((i + 1) * GROUP + (GROUP - 1 - g if i + 1 == middle else g)) * along + j)
            for i in range(1, strips - 1, 2)
            for g in range(GROUP)
            for j in range(along)
        ]
    )

    def swapped(shift):
        return [(g * along + i, (g ^ shift) * along + i) for g in range(GROUP) for i in range(along)]

    struct = jax.ShapeDtypeStruct
    to_border, to_core, own_phase, *blocks = call(
        pack,
        [struct((ROWS + REACH, FRAME1), F32)] * 2
        + [struct((2, ROWS, FRAME1), F32)]
        + [struct((MESSAGE, TILE), F32)] * GROUP,
        [where, tilts],
        [phase_delay, measured],
        0,
        [pltpu.VMEM((2, ROWS, columns), F32)] * 2 + [pltpu.SemaphoreType.DMA((4,))],
        pltpu.HBM,
        PACK_LIMIT,
    )
    beside = lax.ppermute(to_core, "space", in_chip)
    across = lax.ppermute(to_border, ("space", "angle"), over_border_nearest)
    near, block1, block2, block3 = [blocks[0]] + [
        lax.ppermute(blocks[shift], "angle", swapped(shift)) for shift in range(1, GROUP)
    ]
    own, *matrices = call(
        prepare,
        [
            struct((2, 2, ROWS, FRAME1), F32),
            struct((4 * WIDE, 2 * WIDEST), BF16),
            struct((4 * ROWS, 4 * WIDE), BF16),
            struct((4 * WIDE, 4 * ROWS), BF16),
            struct((4 * WIDEST, 4 * WIDE), BF16),
            struct((2, 2, 512, 256), BF16),
        ],
        [where, fresnel_taps],
        [own_phase],
        10_000_000,
    )
    totals = [struct((WIDEST, BLOCK), F32), struct((WIDE, FRAME1), F32)]
    turn0, turn1, total0, total1 = call(
        functools.partial(first_angles, total_rows=total_rows),
        [struct((2, WIDEST, FRAME0), F32), struct((2, WIDE, FRAME1), F32)] + totals,
        [where],
        [across, beside, own, near, block2, *matrices],
        800_000_000,
    )
    tiles_struct = struct((BLOCK // TILE, 2 * ROWS, TILE), F32)
    tiles, to_border, to_core = call(
        last_angles,
        [tiles_struct] + [struct((ROWS + REACH, BLOCK), F32)] * 2,
        [where],
        [block3, block1, total0, total1, turn0, turn1, *matrices],
        4_000_000_000,
    )
    beside = lax.ppermute(to_core, "space", in_chip)
    across = lax.ppermute(to_border, "space", over_border)
    (tiles,) = call(add_strips, [tiles_struct], [where], [tiles, across, beside], 0)
    beside_x = [[g * along + i for i in range(along)] for g in range(GROUP)]
    tiles = lax.all_to_all(tiles, "angle", 0, 0, axis_index_groups=beside_x)
    return jnp.sum(tiles, axis=0).reshape(2, ROWS, TILE)


def solution(mesh):
    def step(phase_delay, measured, tilts, fresnel_taps):
        return jax.shard_map(
            functools.partial(body, phase_delay.shape[1]),
            mesh=mesh,
            in_specs=(P(None, "space", None), P("angle", None, "space", None), P("angle", None), P()),
            out_specs=P(None, "space", "angle"),
            check_vma=False,
        )(phase_delay, measured, tilts, fresnel_taps)

    return step
```

```python
import functools

import jax
import jax.numpy as jnp
from jax import lax
from jax.experimental import pallas as pl
from jax.experimental.pallas import tpu as pltpu
from jax.sharding import PartitionSpec as P

TILE = 128
REACH = 16
TAPS = 2 * REACH + 1
ROWS = 32
WIDE = ROWS + 2 * REACH
WIDEST = ROWS + 4 * REACH
F32 = jnp.float32
BF16 = jnp.bfloat16
SIDE = 2 * REACH
GROUP = 4
BLOCK = 512
FRAME0 = BLOCK + 2 * TILE
FRAME1 = BLOCK + TILE
SIDES_AT = 2 * ROWS * BLOCK // TILE
TILTS_AT = SIDES_AT + ROWS
MESSAGE = TILTS_AT + 8
VMEM_LIMIT = 32 * 1024 * 1024
PACK_LIMIT = 55259136


def split(x):
    high = x.astype(BF16)
    return high, (x - high.astype(F32)).astype(BF16)


def cos_sin(x):
    turns = jnp.round(x * 0.6366197723675814)
    rest = ((x - turns * 1.5703125) - turns * 4.837512969970703125e-4) - turns * 7.54978995489188216e-8
    square = rest * rest
    sine = rest + rest * square * (
        -1.6666654611e-1 + square * (8.3321608736e-3 + square * -1.9515295891e-4)
    )
    cosine = (1.0 - 0.5 * square) + square * square * (
        4.166664568298827e-2 + square * (-1.388731625493765e-3 + square * 2.443315711809948e-5)
    )
    quarter = turns.astype(jnp.int32)
    odd = (quarter & 1) == 1
    cos_part, sin_part = jnp.where(odd, sine, cosine), jnp.where(odd, cosine, sine)
    return (
        jnp.where(((quarter + 1) & 2) == 2, -cos_part, cos_part),
        jnp.where((quarter & 2) == 2, -sin_part, sin_part),
    )


def matmul(a, b):
    return jnp.dot(a, b, preferred_element_type=F32)


def tap_matrices(taps_ref, into1_ref, into2_ref, out1_ref, out2_ref, band_ref):
    lane = lax.broadcasted_iota(jnp.int32, (8, 256), 1)

    def laid(direction, part, start, step):
        out = jnp.zeros((8, 256), F32)
        for tap in range(TAPS):
            out = jnp.where(lane == (start + step * tap) % 256, taps_ref[direction, part, tap], out)
        return out

    def toeplitz(vector, rows):
        full = jnp.broadcast_to(vector[:1], (rows, 256))
        return pltpu.roll(full, 0, 1, stride=1, stride_axis=0)

    def put(ref, index, value):
        high, low = split(value)
        ref[index, 0] = high
        ref[index, 1] = low

    for ref, out_rows, in_rows, last, step, sign in (
        (into1_ref, WIDE, WIDEST, TAPS - 1, -1, 1.0),
        (into2_ref, ROWS, WIDE, TAPS - 1, -1, 1.0),
        (out1_ref, WIDE, ROWS, 1 - TAPS, 1, -1.0),
        (out2_ref, WIDEST, WIDE, 1 - TAPS, 1, -1.0),
    ):
        column = lax.broadcasted_iota(jnp.int32, (out_rows, 256), 1)
        real, imag = laid(0, 0, last, step), laid(0, 1, last, step) * sign
        real_2, imag_2 = laid(0, 0, in_rows + last, step), laid(0, 1, in_rows + last, step) * sign
        first = column < in_rows
        top = jnp.where(first, toeplitz(real, out_rows), -toeplitz(imag_2, out_rows))
        bottom = jnp.where(first, toeplitz(imag, out_rows), toeplitz(real_2, out_rows))
        high, low = split(jnp.concatenate([top, bottom], axis=0)[:, : 2 * in_rows])
        if ref.shape[1] == 2 * in_rows:
            ref[...] = jnp.concatenate([high, low], axis=0)
        else:
            high = high.astype(F32)
            low = low.astype(F32)
            both = jnp.concatenate([high, low], axis=0), jnp.concatenate([high, jnp.zeros_like(low)], axis=0)
            ref[...] = jnp.concatenate(both, axis=1).astype(BF16)
    for index, sign in ((0, 1.0), (1, -1.0)):
        first = 256 - TILE // 2 - REACH
        start, step = (first, 1) if index == 0 else (first + TAPS - 1, -1)
        real = toeplitz(laid(1, 0, start, step), 256)[:, :TILE]
        imag = toeplitz(laid(1, 1, start, step) * sign, 256)[:, :TILE]
        put(
            band_ref,
            index,
            jnp.concatenate(
                [
                    jnp.concatenate([real, imag], axis=1),
                    jnp.concatenate([-imag, real], axis=1),
                ],
                axis=0,
            ),
        )


def row_pass(fields, matrix_ref):
    columns = fields[0][0].shape[1]
    high, low = split(jnp.concatenate([jnp.concatenate(field, axis=0) for field in fields], axis=1))
    matrix = matrix_ref[...]
    count = matrix.shape[0] // 2
    if matrix.shape[1] == high.shape[0]:
        product = matmul(matrix, high)
        total = product[:count] + (product[count:] + matmul(matrix[:count], low))
    else:
        product = matmul(matrix, jnp.concatenate([high, low], axis=0))
        total = product[:count] + product[count:]
    pieces = [total[:, i * columns : (i + 1) * columns] for i in range(len(fields))]
    return [(piece[: count // 2], piece[count // 2 :]) for piece in pieces]


def column_pass(fields, band_ref, index, tiles, first):
    return [column_pass_of(field, band_ref, index, tiles, first) for field in fields]


def column_pass_of(field, band_ref, index, tiles, first):
    rows = field[0].shape[0]
    have = field[0].shape[1] // TILE
    blank = jnp.zeros((rows, TILE), BF16)

    def stacked(parts):
        def tile(part, j):
            return part[:, j * TILE : (j + 1) * TILE] if 0 <= j < have else blank

        return jnp.concatenate(
            [
                jnp.concatenate([tile(part, first + j + i) for part in parts for i in range(2)], axis=1)
                for j in range(tiles)
            ],
            axis=0,
        )

    levels = [split(part) for part in field]
    high = stacked([level[0] for level in levels])
    low = stacked([level[1] for level in levels])
    band_high = band_ref[index, 0]
    out = matmul(high, band_high) + (matmul(low, band_high) + matmul(high, band_ref[index, 1]))
    pieces = [out[j * rows : (j + 1) * rows] for j in range(tiles)]
    return (
        jnp.concatenate([piece[:, :TILE] for piece in pieces], axis=1),
        jnp.concatenate([piece[:, TILE:] for piece in pieces], axis=1),
    )


def neighbours(even, across, beside):
    return jnp.where(even, across, beside), jnp.where(even, beside, across)


def half_tile(x):
    blank = jnp.zeros((x.shape[0], TILE // 2), x.dtype)
    return jnp.concatenate([blank, x, blank], axis=1)


def block_tile(ref, part, block, index):
    columns = ref.shape[-1]
    start = jnp.clip(block * BLOCK + index * TILE, 0, columns - TILE)
    tile = ref[part, :, pl.ds(pl.multiple_of(start, TILE), TILE)]
    if index < 0:
        return jnp.where(block == 0, 0.0, tile)
    if index * TILE >= BLOCK:
        return jnp.where(block == GROUP - 1, 0.0, tile)
    return tile


def phase_block(ref, part, block):
    tiles = [block_tile(ref, part, block, index) for index in range(-1, BLOCK // TILE + 1)]
    return jnp.concatenate(tiles, axis=1)[:, TILE // 2 : TILE // 2 + FRAME1]


def pack(where_ref, tilts_ref, phase_hbm, measured_hbm, border_ref, core_ref, own_ref, *refs):
    block_refs, (phase_ref, plane_ref, semaphores) = refs[:GROUP], refs[GROUP:]
    copies = []
    for source, room in ((phase_hbm, phase_ref), (measured_hbm.at[0], plane_ref)):
        for part in range(2):
            copies.append(pltpu.make_async_copy(source.at[part], room.at[part], semaphores.at[len(copies)]))
            copies[-1].start()
    copies[0].wait()
    copies[1].wait()
    even = where_ref[1] == 0
    low, high = slice(0, REACH), slice(ROWS - REACH, ROWS)
    border_ref[:ROWS] = phase_block(phase_ref, 0, where_ref[3])
    slice1 = phase_block(phase_ref, 1, where_ref[3])
    border_ref[ROWS:] = jnp.where(even, slice1[low], slice1[high])
    own_ref[0] = phase_block(phase_ref, 0, where_ref[2])
    own_ref[1] = phase_block(phase_ref, 1, where_ref[2])
    core_ref[:ROWS] = own_ref[0]
    core_ref[ROWS:] = jnp.where(even, own_ref[1, high], own_ref[1, low])
    lane = lax.broadcasted_iota(jnp.int32, (ROWS, TILE), 1)
    tilts = jnp.where(lane[:8] == 0, tilts_ref[0, 0], tilts_ref[0, 1])
    copies[2].wait()
    copies[3].wait()
    for shift, ref in enumerate(block_refs):
        block = where_ref[2] ^ shift
        for part in range(2):
            for j in range(BLOCK // TILE):
                ref[pl.ds((part * (BLOCK // TILE) + j) * ROWS, ROWS)] = block_tile(plane_ref, part, block, j)
        sides = [
            pltpu.roll(block_tile(plane_ref, part, block, index), SIDE + 2 * SIDE * part, 1)
            for part in range(2)
            for index in (-1, BLOCK // TILE)
        ]
        left, right = jnp.where(lane < SIDE, sides[0], sides[1]), jnp.where(lane < 3 * SIDE, sides[2], sides[3])
        ref[pl.ds(SIDES_AT, ROWS)] = jnp.where(lane < 2 * SIDE, left, right)
        ref[pl.ds(TILTS_AT, 8)] = tilts


def measured_part(ref, part):
    lane = lax.broadcasted_iota(jnp.int32, (ROWS, TILE), 1)
    sides = pltpu.roll(ref[pl.ds(SIDES_AT, ROWS)], 3 * SIDE - 2 * SIDE * part, 1)
    tiles = [ref[pl.ds((part * (BLOCK // TILE) + j) * ROWS, ROWS)] for j in range(BLOCK // TILE)]
    left, right = jnp.where(lane >= TILE - SIDE, sides, 0.0), jnp.where(lane < SIDE, sides, 0.0)
    return jnp.concatenate([left, *tiles, right], axis=1)


def prepare(where_ref, taps_ref, own_ref, turn_ref, into1_ref, into2_ref, out1_ref, out2_ref, band_ref):
    tap_matrices(taps_ref, into1_ref, into2_ref, out1_ref, out2_ref, band_ref)
    for layer in range(2):
        turn_ref[layer, 0], turn_ref[layer, 1] = inside_grid(where_ref, *cos_sin(own_ref[layer]))


def inside_grid(where_ref, *fields):
    count = fields[0].shape[1]
    margin = (count - BLOCK) // 2
    lane = lax.broadcasted_iota(jnp.int32, (1, count), 1)
    there = ((lane >= margin) | (where_ref[2] != 0)) & ((lane < margin + BLOCK) | (where_ref[2] != GROUP - 1))
    return [jnp.where(there, field, 0.0) for field in fields]


def turns(where_ref, across_ref, beside_ref, own_ref, turn0_ref, turn1_ref, total_rows):
    even = where_ref[1] == 0
    first_row = where_ref[0]
    below, above = neighbours(even, across_ref[...], beside_ref[...])
    below = [jnp.where(first_row > 0, x, 0.0) for x in inside_grid(where_ref, *cos_sin(below))]
    above = [jnp.where(first_row + ROWS < total_rows, x, 0.0) for x in inside_grid(where_ref, *cos_sin(above))]
    for part in range(2):
        turn0_ref[part] = half_tile(jnp.concatenate([below[part][:ROWS], own_ref[0, part], above[part][:ROWS]], axis=0))
        turn1_ref[part] = jnp.concatenate([below[part][ROWS:], own_ref[1, part], above[part][ROWS:]], axis=0)


def sweep(where_ref, measured_refs, turn0_ref, turn1_ref, into1_ref, into2_ref, out1_ref, out2_ref, band_ref):
    row = (where_ref[0] - 2 * REACH + lax.broadcasted_iota(jnp.int32, (WIDEST, TILE), 0)).astype(F32)
    column = where_ref[2] * BLOCK - TILE + lax.broadcasted_iota(jnp.int32, (8, FRAME0), 1)
    cos0, sin0, cos1, sin1 = turn0_ref[0], turn0_ref[1], turn1_ref[0], turn1_ref[1]
    waves0 = []
    for measured_ref in measured_refs:
        cos_r, sin_r = cos_sin(measured_ref[TILTS_AT : TILTS_AT + 1, :1] * row)
        cos_c, sin_c = cos_sin(measured_ref[TILTS_AT : TILTS_AT + 1, 1:2] * column.astype(F32))
        cos_r, sin_r, cos_c, sin_c = cos_r[:, :1], sin_r[:, :1], cos_c[:1], sin_c[:1]
        left_r, left_i = cos0 * cos_r - sin0 * sin_r, sin0 * cos_r + cos0 * sin_r
        waves0.append((left_r * cos_c - left_i * sin_c, left_r * sin_c + left_i * cos_c))
    fields = column_pass(row_pass(waves0, into1_ref), band_ref, 0, FRAME1 // TILE, 0)
    waves1 = [(cos1 * real - sin1 * imag, cos1 * imag + sin1 * real) for real, imag in fields]
    fields = column_pass(row_pass(waves1, into2_ref), band_ref, 0, FRAME0 // TILE, -1)
    fields = [
        inside_grid(where_ref, real - measured_part(measured_ref, 0), imag - measured_part(measured_ref, 1))
        for (real, imag), measured_ref in zip(fields, measured_refs)
    ]
    fields = row_pass(column_pass(fields, band_ref, 1, FRAME1 // TILE, 0), out1_ref)
    total1 = sum(wave[0] * imag - wave[1] * real for wave, (real, imag) in zip(waves1, fields))
    fields = [(cos1 * real + sin1 * imag, cos1 * imag - sin1 * real) for real, imag in fields]
    fields = row_pass(column_pass(fields, band_ref, 1, BLOCK // TILE, 0), out2_ref)
    middle = slice(TILE, TILE + BLOCK)
    total0 = sum(
        wave[0][:, middle] * imag - wave[1][:, middle] * real for wave, (real, imag) in zip(waves0, fields)
    )
    return total0, total1


def first_angles(
    where_ref, across_ref, beside_ref, own_ref, near_ref, far_ref, into1_ref, into2_ref, out1_ref, out2_ref, band_ref,
    turn0_ref, turn1_ref, total0_ref, total1_ref, *, total_rows,
):
    turns(where_ref, across_ref, beside_ref, own_ref, turn0_ref, turn1_ref, total_rows)
    total0_ref[...], total1_ref[...] = sweep(
        where_ref, [near_ref, far_ref], turn0_ref, turn1_ref, into1_ref, into2_ref, out1_ref, out2_ref, band_ref
    )


def last_angles(where_ref, near_ref, far_ref, total0_ref, total1_ref, *refs):
    own_ref, border_ref, core_ref = refs[-3:]
    term0, term1 = sweep(where_ref, [near_ref, far_ref], *refs[:-3])
    slice0, slice1 = total0_ref[...] + term0, total1_ref[...] + term1
    slice1 = slice1[:, TILE // 2 : TILE // 2 + BLOCK]
    for j in range(BLOCK // TILE):
        own_ref[j, :ROWS] = slice0[ROWS : 2 * ROWS, j * TILE : (j + 1) * TILE]
        own_ref[j, ROWS:] = slice1[REACH : REACH + ROWS, j * TILE : (j + 1) * TILE]
    even = where_ref[1] == 0
    low = jnp.concatenate([slice0[:ROWS], slice1[:REACH]], axis=0)
    high = jnp.concatenate([slice0[2 * ROWS :], slice1[REACH + ROWS :]], axis=0)
    border_ref[...] = jnp.where(even, low, high)
    core_ref[...] = jnp.where(even, high, low)


def add_strips(where_ref, own_ref, across_ref, beside_ref, out_ref):
    below, above = neighbours(where_ref[1] == 0, across_ref[...], beside_ref[...])
    for j in range(BLOCK // TILE):
        tile = slice(j * TILE, (j + 1) * TILE)
        out_ref[j, :ROWS] = own_ref[j, :ROWS] + (below[:ROWS, tile] + above[:ROWS, tile])
        out_ref[j, ROWS : ROWS + REACH] = own_ref[j, ROWS : ROWS + REACH] + below[ROWS:, tile]
        out_ref[j, ROWS + REACH :] = own_ref[j, ROWS + REACH :] + above[ROWS:, tile]


def call(kernel, shapes, scalars, arrays, flops, scratch=(), space=pltpu.VMEM, limit=VMEM_LIMIT):
    moved = sum(a.size * a.dtype.itemsize for a in arrays)
    moved += sum(int(s.size) * s.dtype.itemsize for s in shapes)
    return pl.pallas_call(
        kernel,
        out_shape=shapes,
        in_specs=[pl.BlockSpec(memory_space=pltpu.SMEM)] * len(scalars)
        + [pl.BlockSpec(memory_space=space)] * len(arrays),
        out_specs=[pl.BlockSpec(memory_space=pltpu.VMEM)] * len(shapes),
        scratch_shapes=list(scratch),
        compiler_params=pltpu.CompilerParams(vmem_limit_bytes=limit),
        cost_estimate=pl.CostEstimate(flops=flops, bytes_accessed=moved, transcendentals=0),
    )(*scalars, *arrays)


def swaps(pairs):
    return pairs + [(b, a) for a, b in pairs]


def body(total_rows, phase_delay, measured, tilts, fresnel_taps):
    columns = phase_delay.shape[2]
    strips = lax.axis_size("space")
    along = lax.axis_size("angle") // GROUP
    strip = lax.axis_index("space")
    block = lax.axis_index("angle") // along
    middle = strips // 2
    far = (strip == middle - 1) | (strip == middle)
    where = jnp.stack([strip * ROWS, strip & 1, block, jnp.where(far, GROUP - 1 - block, block)]).astype(jnp.int32)
    over_border = swaps([(i, i + 1) for i in range(1, strips - 1, 2)])
    in_chip = swaps([(i, i + 1) for i in range(0, strips, 2)])
    over_border_nearest = swaps(
        [
            ((i * GROUP + g) * along + j, ((i + 1) * GROUP + (GROUP - 1 - g if i + 1 == middle else g)) * along + j)
            for i in range(1, strips - 1, 2)
            for g in range(GROUP)
            for j in range(along)
        ]
    )

    def swapped(shift):
        return [(g * along + i, (g ^ shift) * along + i) for g in range(GROUP) for i in range(along)]

    struct = jax.ShapeDtypeStruct
    to_border, to_core, own_phase, *blocks = call(
        pack,
        [struct((ROWS + REACH, FRAME1), F32)] * 2
        + [struct((2, ROWS, FRAME1), F32)]
        + [struct((MESSAGE, TILE), F32)] * GROUP,
        [where, tilts],
        [phase_delay, measured],
        0,
        [pltpu.VMEM((2, ROWS, columns), F32)] * 2 + [pltpu.SemaphoreType.DMA((4,))],
        pltpu.HBM,
        PACK_LIMIT,
    )
    beside = lax.ppermute(to_core, "space", in_chip)
    across = lax.ppermute(to_border, ("space", "angle"), over_border_nearest)
    near, block1, block2, block3 = [blocks[0]] + [
        lax.ppermute(blocks[shift], "angle", swapped(shift)) for shift in range(1, GROUP)
    ]
    own, *matrices = call(
        prepare,
        [
            struct((2, 2, ROWS, FRAME1), F32),
            struct((4 * WIDE, 2 * WIDEST), BF16),
            struct((4 * ROWS, 4 * WIDE), BF16),
            struct((4 * WIDE, 4 * ROWS), BF16),
            struct((4 * WIDEST, 4 * WIDE), BF16),
            struct((2, 2, 512, 256), BF16),
        ],
        [where, fresnel_taps],
        [own_phase],
        10_000_000,
    )
    totals = [struct((WIDEST, BLOCK), F32), struct((WIDE, FRAME1), F32)]
    turn0, turn1, total0, total1 = call(
        functools.partial(first_angles, total_rows=total_rows),
        [struct((2, WIDEST, FRAME0), F32), struct((2, WIDE, FRAME1), F32)] + totals,
        [where],
        [across, beside, own, near, block2, *matrices],
        800_000_000,
    )
    tiles_struct = struct((BLOCK // TILE, 2 * ROWS, TILE), F32)
    tiles, to_border, to_core = call(
        last_angles,
        [tiles_struct] + [struct((ROWS + REACH, BLOCK), F32)] * 2,
        [where],
        [block3, block1, total0, total1, turn0, turn1, *matrices],
        4_000_000_000,
    )
    beside = lax.ppermute(to_core, "space", in_chip)
    across = lax.ppermute(to_border, "space", over_border)
    (tiles,) = call(add_strips, [tiles_struct], [where], [tiles, across, beside], 0)
    beside_x = [[g * along + i for i in range(along)] for g in range(GROUP)]
    tiles = lax.all_to_all(tiles, "angle", 0, 0, axis_index_groups=beside_x)
    return jnp.sum(tiles, axis=0).reshape(2, ROWS, TILE)


def solution(mesh):
    def step(phase_delay, measured, tilts, fresnel_taps):
        return jax.shard_map(
            functools.partial(body, phase_delay.shape[1]),
            mesh=mesh,
            in_specs=(P(None, "space", None), P("angle", None, "space", None), P("angle", None), P()),
            out_specs=P(None, "space", "angle"),
            check_vma=False,
        )(phase_delay, measured, tilts, fresnel_taps)

    return step
```

```python
import functools

import jax
import jax.numpy as jnp
from jax import lax
from jax.experimental import pallas as pl
from jax.experimental.pallas import tpu as pltpu
from jax.sharding import PartitionSpec as P

TILE = 128
REACH = 16
TAPS = 2 * REACH + 1
ROWS = 32
WIDE = ROWS + 2 * REACH
WIDEST = ROWS + 4 * REACH
F32 = jnp.float32
BF16 = jnp.bfloat16
SIDE = 2 * REACH
GROUP = 4
BLOCK = 512
FRAME0 = BLOCK + 2 * TILE
FRAME1 = BLOCK + TILE
SIDES_AT = 2 * ROWS * BLOCK // TILE
TILTS_AT = SIDES_AT + ROWS
MESSAGE = TILTS_AT + 8
VMEM_LIMIT = 32 * 1024 * 1024
PACK_LIMIT = 55259136


def split(x):
    high = x.astype(BF16)
    return high, (x - high.astype(F32)).astype(BF16)


def cos_sin(x):
    turns = jnp.round(x * 0.6366197723675814)
    rest = ((x - turns * 1.5703125) - turns * 4.837512969970703125e-4) - turns * 7.54978995489188216e-8
    square = rest * rest
    sine = rest + rest * square * (
        -1.6666654611e-1 + square * (8.3321608736e-3 + square * -1.9515295891e-4)
    )
    cosine = (1.0 - 0.5 * square) + square * square * (
        4.166664568298827e-2 + square * (-1.388731625493765e-3 + square * 2.443315711809948e-5)
    )
    quarter = turns.astype(jnp.int32)
    odd = (quarter & 1) == 1
    cos_part, sin_part = jnp.where(odd, sine, cosine), jnp.where(odd, cosine, sine)
    return (
        jnp.where(((quarter + 1) & 2) == 2, -cos_part, cos_part),
        jnp.where((quarter & 2) == 2, -sin_part, sin_part),
    )


def matmul(a, b):
    return jnp.dot(a, b, preferred_element_type=F32)


def tap_matrices(taps_ref, into1_ref, into2_ref, out1_ref, out2_ref, band_ref):
    lane = lax.broadcasted_iota(jnp.int32, (8, 256), 1)

    def laid(direction, part, start, step):
        out = jnp.zeros((8, 256), F32)
        for tap in range(TAPS):
            out = jnp.where(lane == (start + step * tap) % 256, taps_ref[direction, part, tap], out)
        return out

    def toeplitz(vector, rows):
        full = jnp.broadcast_to(vector[:1], (rows, 256))
        return pltpu.roll(full, 0, 1, stride=1, stride_axis=0)

    def put(ref, index, value):
        high, low = split(value)
        ref[index, 0] = high
        ref[index, 1] = low

    for ref, out_rows, in_rows, last, step, sign in (
        (into1_ref, WIDE, WIDEST, TAPS - 1, -1, 1.0),
        (into2_ref, ROWS, WIDE, TAPS - 1, -1, 1.0),
        (out1_ref, WIDE, ROWS, 1 - TAPS, 1, -1.0),
        (out2_ref, WIDEST, WIDE, 1 - TAPS, 1, -1.0),
    ):
        column = lax.broadcasted_iota(jnp.int32, (out_rows, 256), 1)
        real, imag = laid(0, 0, last, step), laid(0, 1, last, step) * sign
        real_2, imag_2 = laid(0, 0, in_rows + last, step), laid(0, 1, in_rows + last, step) * sign
        first = column < in_rows
        top = jnp.where(first, toeplitz(real, out_rows), -toeplitz(imag_2, out_rows))
        bottom = jnp.where(first, toeplitz(imag, out_rows), toeplitz(real_2, out_rows))
        high, low = split(jnp.concatenate([top, bottom], axis=0)[:, : 2 * in_rows])
        if ref.shape[1] == 2 * in_rows:
            ref[...] = jnp.concatenate([high, low], axis=0)
        else:
            high = high.astype(F32)
            low = low.astype(F32)
            both = jnp.concatenate([high, low], axis=0), jnp.concatenate([high, jnp.zeros_like(low)], axis=0)
            ref[...] = jnp.concatenate(both, axis=1).astype(BF16)
    for index, sign in ((0, 1.0), (1, -1.0)):
        first = 256 - TILE // 2 - REACH
        start, step = (first, 1) if index == 0 else (first + TAPS - 1, -1)
        real = toeplitz(laid(1, 0, start, step), 256)[:, :TILE]
        imag = toeplitz(laid(1, 1, start, step) * sign, 256)[:, :TILE]
        put(
            band_ref,
            index,
            jnp.concatenate(
                [
                    jnp.concatenate([real, imag], axis=1),
                    jnp.concatenate([-imag, real], axis=1),
                ],
                axis=0,
            ),
        )


def row_pass(fields, matrix_ref):
    columns = fields[0][0].shape[1]
    high, low = split(jnp.concatenate([jnp.concatenate(field, axis=0) for field in fields], axis=1))
    matrix = matrix_ref[...]
    count = matrix.shape[0] // 2
    if matrix.shape[1] == high.shape[0]:
        product = matmul(matrix, high)
        total = product[:count] + (product[count:] + matmul(matrix[:count], low))
    else:
        product = matmul(matrix, jnp.concatenate([high, low], axis=0))
        total = product[:count] + product[count:]
    pieces = [total[:, i * columns : (i + 1) * columns] for i in range(len(fields))]
    return [(piece[: count // 2], piece[count // 2 :]) for piece in pieces]


def column_pass(fields, band_ref, index, tiles, first):
    return [column_pass_of(field, band_ref, index, tiles, first) for field in fields]


def column_pass_of(field, band_ref, index, tiles, first):
    rows = field[0].shape[0]
    have = field[0].shape[1] // TILE
    blank = jnp.zeros((rows, TILE), BF16)

    def stacked(parts):
        def tile(part, j):
            return part[:, j * TILE : (j + 1) * TILE] if 0 <= j < have else blank

        return jnp.concatenate(
            [
                jnp.concatenate([tile(part, first + j + i) for part in parts for i in range(2)], axis=1)
                for j in range(tiles)
            ],
            axis=0,
        )

    levels = [split(part) for part in field]
    high = stacked([level[0] for level in levels])
    low = stacked([level[1] for level in levels])
    band_high = band_ref[index, 0]
    out = matmul(high, band_high) + (matmul(low, band_high) + matmul(high, band_ref[index, 1]))
    pieces = [out[j * rows : (j + 1) * rows] for j in range(tiles)]
    return (
        jnp.concatenate([piece[:, :TILE] for piece in pieces], axis=1),
        jnp.concatenate([piece[:, TILE:] for piece in pieces], axis=1),
    )


def neighbours(even, across, beside):
    return jnp.where(even, across, beside), jnp.where(even, beside, across)


def half_tile(x):
    blank = jnp.zeros((x.shape[0], TILE // 2), x.dtype)
    return jnp.concatenate([blank, x, blank], axis=1)


def block_tile(ref, part, block, index):
    columns = ref.shape[-1]
    start = jnp.clip(block * BLOCK + index * TILE, 0, columns - TILE)
    tile = ref[part, :, pl.ds(pl.multiple_of(start, TILE), TILE)]
    if index < 0:
        return jnp.where(block == 0, 0.0, tile)
    if index * TILE >= BLOCK:
        return jnp.where(block == GROUP - 1, 0.0, tile)
    return tile


def phase_block(ref, part, block):
    tiles = [block_tile(ref, part, block, index) for index in range(-1, BLOCK // TILE + 1)]
    return jnp.concatenate(tiles, axis=1)[:, TILE // 2 : TILE // 2 + FRAME1]


def pack(where_ref, tilts_ref, phase_hbm, measured_hbm, border_ref, core_ref, own_ref, *refs):
    block_refs, (phase_ref, plane_ref, semaphores) = refs[:GROUP], refs[GROUP:]
    copies = []
    for source, room in ((phase_hbm, phase_ref), (measured_hbm.at[0], plane_ref)):
        for part in range(2):
            copies.append(pltpu.make_async_copy(source.at[part], room.at[part], semaphores.at[len(copies)]))
            copies[-1].start()
    copies[0].wait()
    copies[1].wait()
    even = where_ref[1] == 0
    low, high = slice(0, REACH), slice(ROWS - REACH, ROWS)
    border_ref[:ROWS] = phase_block(phase_ref, 0, where_ref[3])
    slice1 = phase_block(phase_ref, 1, where_ref[3])
    border_ref[ROWS:] = jnp.where(even, slice1[low], slice1[high])
    own_ref[0] = phase_block(phase_ref, 0, where_ref[2])
    own_ref[1] = phase_block(phase_ref, 1, where_ref[2])
    core_ref[:ROWS] = own_ref[0]
    core_ref[ROWS:] = jnp.where(even, own_ref[1, high], own_ref[1, low])
    lane = lax.broadcasted_iota(jnp.int32, (ROWS, TILE), 1)
    tilts = jnp.where(lane[:8] == 0, tilts_ref[0, 0], tilts_ref[0, 1])
    copies[2].wait()
    copies[3].wait()
    for shift, ref in enumerate(block_refs):
        block = where_ref[2] ^ shift
        for part in range(2):
            for j in range(BLOCK // TILE):
                ref[pl.ds((part * (BLOCK // TILE) + j) * ROWS, ROWS)] = block_tile(plane_ref, part, block, j)
        sides = [
            pltpu.roll(block_tile(plane_ref, part, block, index), SIDE + 2 * SIDE * part, 1)
            for part in range(2)
            for index in (-1, BLOCK // TILE)
        ]
        left, right = jnp.where(lane < SIDE, sides[0], sides[1]), jnp.where(lane < 3 * SIDE, sides[2], sides[3])
        ref[pl.ds(SIDES_AT, ROWS)] = jnp.where(lane < 2 * SIDE, left, right)
        ref[pl.ds(TILTS_AT, 8)] = tilts


def measured_part(ref, part):
    lane = lax.broadcasted_iota(jnp.int32, (ROWS, TILE), 1)
    sides = pltpu.roll(ref[pl.ds(SIDES_AT, ROWS)], 3 * SIDE - 2 * SIDE * part, 1)
    tiles = [ref[pl.ds((part * (BLOCK // TILE) + j) * ROWS, ROWS)] for j in range(BLOCK // TILE)]
    left, right = jnp.where(lane >= TILE - SIDE, sides, 0.0), jnp.where(lane < SIDE, sides, 0.0)
    return jnp.concatenate([left, *tiles, right], axis=1)


def prepare(where_ref, taps_ref, own_ref, turn_ref, into1_ref, into2_ref, out1_ref, out2_ref, band_ref):
    tap_matrices(taps_ref, into1_ref, into2_ref, out1_ref, out2_ref, band_ref)
    for layer in range(2):
        turn_ref[layer, 0], turn_ref[layer, 1] = inside_grid(where_ref, *cos_sin(own_ref[layer]))


def inside_grid(where_ref, *fields):
    count = fields[0].shape[1]
    margin = (count - BLOCK) // 2
    lane = lax.broadcasted_iota(jnp.int32, (1, count), 1)
    there = ((lane >= margin) | (where_ref[2] != 0)) & ((lane < margin + BLOCK) | (where_ref[2] != GROUP - 1))
    return [jnp.where(there, field, 0.0) for field in fields]


def turns(where_ref, across_ref, beside_ref, own_ref, turn0_ref, turn1_ref, total_rows):
    even = where_ref[1] == 0
    first_row = where_ref[0]
    below, above = neighbours(even, across_ref[...], beside_ref[...])
    below = [jnp.where(first_row > 0, x, 0.0) for x in inside_grid(where_ref, *cos_sin(below))]
    above = [jnp.where(first_row + ROWS < total_rows, x, 0.0) for x in inside_grid(where_ref, *cos_sin(above))]
    for part in range(2):
        turn0_ref[part] = half_tile(jnp.concatenate([below[part][:ROWS], own_ref[0, part], above[part][:ROWS]], axis=0))
        turn1_ref[part] = jnp.concatenate([below[part][ROWS:], own_ref[1, part], above[part][ROWS:]], axis=0)


def sweep(where_ref, measured_refs, turn0_ref, turn1_ref, into1_ref, into2_ref, out1_ref, out2_ref, band_ref):
    row = (where_ref[0] - 2 * REACH + lax.broadcasted_iota(jnp.int32, (WIDEST, TILE), 0)).astype(F32)
    column = where_ref[2] * BLOCK - TILE + lax.broadcasted_iota(jnp.int32, (8, FRAME0), 1)
    cos0, sin0, cos1, sin1 = turn0_ref[0], turn0_ref[1], turn1_ref[0], turn1_ref[1]
    waves0 = []
    for measured_ref in measured_refs:
        cos_r, sin_r = cos_sin(measured_ref[TILTS_AT : TILTS_AT + 1, :1] * row)
        cos_c, sin_c = cos_sin(measured_ref[TILTS_AT : TILTS_AT + 1, 1:2] * column.astype(F32))
        cos_r, sin_r, cos_c, sin_c = cos_r[:, :1], sin_r[:, :1], cos_c[:1], sin_c[:1]
        left_r, left_i = cos0 * cos_r - sin0 * sin_r, sin0 * cos_r + cos0 * sin_r
        waves0.append((left_r * cos_c - left_i * sin_c, left_r * sin_c + left_i * cos_c))
    fields = column_pass(row_pass(waves0, into1_ref), band_ref, 0, FRAME1 // TILE, 0)
    waves1 = [(cos1 * real - sin1 * imag, cos1 * imag + sin1 * real) for real, imag in fields]
    fields = column_pass(row_pass(waves1, into2_ref), band_ref, 0, FRAME0 // TILE, -1)
    fields = [
        inside_grid(where_ref, real - measured_part(measured_ref, 0), imag - measured_part(measured_ref, 1))
        for (real, imag), measured_ref in zip(fields, measured_refs)
    ]
    fields = row_pass(column_pass(fields, band_ref, 1, FRAME1 // TILE, 0), out1_ref)
    total1 = sum(wave[0] * imag - wave[1] * real for wave, (real, imag) in zip(waves1, fields))
    fields = [(cos1 * real + sin1 * imag, cos1 * imag - sin1 * real) for real, imag in fields]
    fields = row_pass(column_pass(fields, band_ref, 1, BLOCK // TILE, 0), out2_ref)
    middle = slice(TILE, TILE + BLOCK)
    total0 = sum(
        wave[0][:, middle] * imag - wave[1][:, middle] * real for wave, (real, imag) in zip(waves0, fields)
    )
    return total0, total1


def first_angles(
    where_ref, across_ref, beside_ref, own_ref, near_ref, far_ref, into1_ref, into2_ref, out1_ref, out2_ref, band_ref,
    turn0_ref, turn1_ref, total0_ref, total1_ref, *, total_rows,
):
    turns(where_ref, across_ref, beside_ref, own_ref, turn0_ref, turn1_ref, total_rows)
    total0_ref[...], total1_ref[...] = sweep(
        where_ref, [near_ref, far_ref], turn0_ref, turn1_ref, into1_ref, into2_ref, out1_ref, out2_ref, band_ref
    )


def last_angles(where_ref, near_ref, far_ref, total0_ref, total1_ref, *refs):
    own_ref, border_ref, core_ref = refs[-3:]
    term0, term1 = sweep(where_ref, [near_ref, far_ref], *refs[:-3])
    slice0, slice1 = total0_ref[...] + term0, total1_ref[...] + term1
    slice1 = slice1[:, TILE // 2 : TILE // 2 + BLOCK]
    for j in range(BLOCK // TILE):
        own_ref[j, :ROWS] = slice0[ROWS : 2 * ROWS, j * TILE : (j + 1) * TILE]
        own_ref[j, ROWS:] = slice1[REACH : REACH + ROWS, j * TILE : (j + 1) * TILE]
    even = where_ref[1] == 0
    low = jnp.concatenate([slice0[:ROWS], slice1[:REACH]], axis=0)
    high = jnp.concatenate([slice0[2 * ROWS :], slice1[REACH + ROWS :]], axis=0)
    border_ref[...] = jnp.where(even, low, high)
    core_ref[...] = jnp.where(even, high, low)


def add_strips(where_ref, own_ref, across_ref, beside_ref, out_ref):
    below, above = neighbours(where_ref[1] == 0, across_ref[...], beside_ref[...])
    for j in range(BLOCK // TILE):
        tile = slice(j * TILE, (j + 1) * TILE)
        out_ref[j, :ROWS] = own_ref[j, :ROWS] + (below[:ROWS, tile] + above[:ROWS, tile])
        out_ref[j, ROWS : ROWS + REACH] = own_ref[j, ROWS : ROWS + REACH] + below[ROWS:, tile]
        out_ref[j, ROWS + REACH :] = own_ref[j, ROWS + REACH :] + above[ROWS:, tile]


def call(kernel, shapes, scalars, arrays, flops, scratch=(), space=pltpu.VMEM, limit=VMEM_LIMIT):
    moved = sum(a.size * a.dtype.itemsize for a in arrays)
    moved += sum(int(s.size) * s.dtype.itemsize for s in shapes)
    return pl.pallas_call(
        kernel,
        out_shape=shapes,
        in_specs=[pl.BlockSpec(memory_space=pltpu.SMEM)] * len(scalars)
        + [pl.BlockSpec(memory_space=space)] * len(arrays),
        out_specs=[pl.BlockSpec(memory_space=pltpu.VMEM)] * len(shapes),
        scratch_shapes=list(scratch),
        compiler_params=pltpu.CompilerParams(vmem_limit_bytes=limit),
        cost_estimate=pl.CostEstimate(flops=flops, bytes_accessed=moved, transcendentals=0),
    )(*scalars, *arrays)


def swaps(pairs):
    return pairs + [(b, a) for a, b in pairs]


def body(total_rows, phase_delay, measured, tilts, fresnel_taps):
    columns = phase_delay.shape[2]
    strips = lax.axis_size("space")
    along = lax.axis_size("angle") // GROUP
    strip = lax.axis_index("space")
    block = lax.axis_index("angle") // along
    middle = strips // 2
    far = (strip == middle - 1) | (strip == middle)
    where = jnp.stack([strip * ROWS, strip & 1, block, jnp.where(far, GROUP - 1 - block, block)]).astype(jnp.int32)
    over_border = swaps([(i, i + 1) for i in range(1, strips - 1, 2)])
    in_chip = swaps([(i, i + 1) for i in range(0, strips, 2)])
    over_border_nearest = swaps(
        [
            ((i * GROUP + g) * along + j, ((i + 1) * GROUP + (GROUP - 1 - g if i + 1 == middle else g)) * along + j)
            for i in range(1, strips - 1, 2)
            for g in range(GROUP)
            for j in range(along)
        ]
    )

    def swapped(shift):
        return [(g * along + i, (g ^ shift) * along + i) for g in range(GROUP) for i in range(along)]

    struct = jax.ShapeDtypeStruct
    to_border, to_core, own_phase, *blocks = call(
        pack,
        [struct((ROWS + REACH, FRAME1), F32)] * 2
        + [struct((2, ROWS, FRAME1), F32)]
        + [struct((MESSAGE, TILE), F32)] * GROUP,
        [where, tilts],
        [phase_delay, measured],
        0,
        [pltpu.VMEM((2, ROWS, columns), F32)] * 2 + [pltpu.SemaphoreType.DMA((4,))],
        pltpu.HBM,
        PACK_LIMIT,
    )
    beside = lax.ppermute(to_core, "space", in_chip)
    across = lax.ppermute(to_border, ("space", "angle"), over_border_nearest)
    near, block1, block2, block3 = [blocks[0]] + [
        lax.ppermute(blocks[shift], "angle", swapped(shift)) for shift in range(1, GROUP)
    ]
    own, *matrices = call(
        prepare,
        [
            struct((2, 2, ROWS, FRAME1), F32),
            struct((4 * WIDE, 2 * WIDEST), BF16),
            struct((4 * ROWS, 4 * WIDE), BF16),
            struct((4 * WIDE, 4 * ROWS), BF16),
            struct((4 * WIDEST, 4 * WIDE), BF16),
            struct((2, 2, 512, 256), BF16),
        ],
        [where, fresnel_taps],
        [own_phase],
        10_000_000,
    )
    totals = [struct((WIDEST, BLOCK), F32), struct((WIDE, FRAME1), F32)]
    turn0, turn1, total0, total1 = call(
        functools.partial(first_angles, total_rows=total_rows),
        [struct((2, WIDEST, FRAME0), F32), struct((2, WIDE, FRAME1), F32)] + totals,
        [where],
        [across, beside, own, near, block3, *matrices],
        800_000_000,
    )
    tiles_struct = struct((BLOCK // TILE, 2 * ROWS, TILE), F32)
    tiles, to_border, to_core = call(
        last_angles,
        [tiles_struct] + [struct((ROWS + REACH, BLOCK), F32)] * 2,
        [where],
        [block2, block1, total0, total1, turn0, turn1, *matrices],
        4_000_000_000,
    )
    beside = lax.ppermute(to_core, "space", in_chip)
    across = lax.ppermute(to_border, "space", over_border)
    (tiles,) = call(add_strips, [tiles_struct], [where], [tiles, across, beside], 0)
    beside_x = [[g * along + i for i in range(along)] for g in range(GROUP)]
    tiles = lax.all_to_all(tiles, "angle", 0, 0, axis_index_groups=beside_x)
    return jnp.sum(tiles, axis=0).reshape(2, ROWS, TILE)


def solution(mesh):
    def step(phase_delay, measured, tilts, fresnel_taps):
        return jax.shard_map(
            functools.partial(body, phase_delay.shape[1]),
            mesh=mesh,
            in_specs=(P(None, "space", None), P("angle", None, "space", None), P("angle", None), P()),
            out_specs=P(None, "space", "angle"),
            check_vma=False,
        )(phase_delay, measured, tilts, fresnel_taps)

    return step
```
